32 devices in a mesh: prompt: 4 (over y, x), vocab: 8 (over z, core).
Axes of the slice: x: 2, y: 2, z: 4, core: 2. Of those that a mesh axis runs over, the one named last changes fastest.
Arguments:
- hidden: bfloat16 [512, 8192], P('prompt')
- head: bfloat16 [8192, 65536], P('prompt', 'vocab')
- gain: float32 [8192], replicated, may hold values from 0.25 to 1.75
- refusal_ids: int32 [512, 16], P('prompt'), may hold values from 0 to 65535, as said below
- refusal_count: int32 [512], P('prompt'), may hold values from 1 to 16
- loss_scale: float32 [512], P('prompt'), may hold values from 8 to 32
Outputs:
- grad_hidden: float32 [512, 8192], P('prompt', 'vocab')
- log_refusal: float32 [512], P('prompt')
The draws below stay inside these ranges and needn't reach their ends.
Inputs may be any that keep to these rules, and one draw needn't show every extreme that they name: `refusal_ids`: the first refusal_count entries of a prompt's list are distinct ids below 65536; later entries are ignored.
All inputs are finite; a program needn't handle non-finite values.
Results may differ from the reference program's by a relative error of at most 0.0027.
The reference program's roundings to bfloat16 on the way (of `normed` and `grad_logits`) count: a program that leaves them out, or rounds other values in their place, can miss the bound.
Values may be sent and summed in bfloat16 or wider, within the bound.
No kernel may reach another device: no remote copies, remote signals or barrier semaphores. Data moves between devices by JAX's collectives and lax.ppermute only.
A program may use at most 256 MiB of HBM per device.

```python
import math
import jax
import jax.numpy as jnp
from jax import lax

D = 8192
VOCAB = 65536
K = 16
PROMPTS = 512


def special_parts(key):
    base = jax.random.fold_in(key, 5)
    rows_pick = jax.random.permutation(jax.random.fold_in(base, 1), PROMPTS)[:4]
    quarter = VOCAB // 4
    first_cols = jnp.arange(4) * quarter + jax.random.randint(jax.random.fold_in(base, 2), (4,), 0, quarter - 1)
    strength = jnp.array([1.5, 2.2, 3.0, 4.0], jnp.float32)
    leading = jax.random.normal(jax.random.fold_in(base, 3), (D, 4), jnp.float32) * strength * (60.0 / D)
    nearby = leading * (1.0 - 2.0 / (60.0 * strength)) + 0.3 / math.sqrt(D) * jax.random.normal(jax.random.fold_in(base, 4), (D, 4), jnp.float32)
    return (rows_pick, first_cols, strength, leading, nearby)


def draw_hidden(key, part):
    drawn = jax.random.normal(jax.random.fold_in(key, 11), (PROMPTS, D), jnp.float32)
    rows_pick, first_cols, strength, leading, nearby = special_parts(key)
    aligned = leading.T * (D / (60.0 * strength[:, None]))
    aligned = aligned + 0.05 * jax.random.normal(jax.random.fold_in(key, 14), (4, D), jnp.float32)
    drawn = drawn.at[rows_pick].set(aligned)
    return drawn.astype(jnp.bfloat16)


def draw_head(key, part):
    col_scale = jnp.exp(jax.random.uniform(jax.random.fold_in(key, 21), (1, VOCAB), jnp.float32, math.log(0.25), math.log(2.5)))
    shared = jax.random.normal(jax.random.fold_in(key, 23), (D, 1), jnp.float32)
    drawn = jax.random.normal(jax.random.fold_in(key, 22), (D, VOCAB), jnp.float32)
    drawn = (drawn + 0.6 * shared) * col_scale / math.sqrt(D)
    rows_pick, first_cols, strength, leading, nearby = special_parts(key)
    drawn = drawn.at[:, first_cols].set(leading)
    drawn = drawn.at[:, first_cols + 1].set(nearby)
    return drawn.astype(jnp.bfloat16)


def draw_refusal_ids(key, part):
    span_size = VOCAB // K
    offsets = jax.random.randint(jax.random.fold_in(key, 31), (PROMPTS, K), 0, span_size)
    offsets = offsets.at[0, K - 1].set(span_size - 1)
    offsets = offsets.at[1, 0].set(0)
    return (jnp.arange(K)[None, :] * span_size + offsets).astype(jnp.int32)


def draw_refusal_count(key, part):
    counts = jax.random.randint(jax.random.fold_in(key, 32), (PROMPTS,), 1, K + 1)
    position = jnp.arange(PROMPTS)
    counts = jnp.where(position % 7 == 0, K, counts)
    counts = jnp.where(position % 7 == 3, 1, counts)
    return counts.astype(jnp.int32)


def level_of(own_key, dims, split, low, top_value):
    level, own = 1.0, jax.random.fold_in(own_key, 6)
    for dim, parts in split:
        draws = jnp.exp(jax.random.uniform(jax.random.fold_in(own, dim), (parts,), jnp.float32, low / len(split), top_value / len(split)))
        level = level * jnp.repeat(draws, dims[dim] // parts).reshape([-1 if axis == dim else 1 for axis in range(len(dims))])
    return level


def setup_inputs(seed: int = 0) -> dict:
    streams_of = jax.random.split(jax.random.key(seed), 7)
    hidden = draw_hidden(jax.random.fold_in(streams_of[6], 71), 0)
    head = draw_head(jax.random.fold_in(streams_of[6], 71), 0)
    gain = jnp.clip(1.0 + 0.15 * jax.random.normal(streams_of[2], (D,), jnp.float32), 0.25, 1.75)
    refusal_ids = draw_refusal_ids(jax.random.fold_in(streams_of[6], 71), 0)
    refusal_count = draw_refusal_count(jax.random.fold_in(streams_of[6], 71), 0)
    loss_scale = jnp.clip(8.0 + 24.0 * jax.random.uniform(streams_of[5], (PROMPTS,), jnp.float32) ** level_of(streams_of[5], (PROMPTS,), ((0, 4),), -0.2, 0.2), 8.0, 32.0)
    return dict(hidden=hidden, head=head, gain=gain, refusal_ids=refusal_ids, refusal_count=refusal_count, loss_scale=loss_scale)


epsilon = 1e-05
lowest = -1e+30

def reference(hidden, head, gain, refusal_ids, refusal_count, loss_scale):
    hidden_f = hidden.astype(jnp.float32)
    inverse_rms = lax.rsqrt(lax.optimization_barrier(jnp.mean(hidden_f * hidden_f, axis=1, keepdims=True)) + epsilon)
    normed = (hidden_f * inverse_rms * gain).astype(jnp.bfloat16)
    logits = jnp.dot(normed, head, preferred_element_type=jnp.float32)
    in_list = jnp.arange(K)[None, :] < refusal_count[:, None]
    picked = jnp.take_along_axis(logits, refusal_ids, axis=1)
    peak_all = lax.optimization_barrier(jnp.max(logits, axis=1))
    peak_ref = lax.optimization_barrier(jnp.max(jnp.where(in_list, picked, lowest), axis=1))
    sum_all = lax.optimization_barrier(jnp.sum(jnp.exp(logits - peak_all[:, None]), axis=1))
    sum_ref = lax.optimization_barrier(jnp.sum(jnp.exp(jnp.where(in_list, picked - peak_ref[:, None], lowest)), axis=1))
    lse_all = peak_all + jnp.log(sum_all)
    lse_ref = peak_ref + jnp.log(sum_ref)
    log_refusal = lse_ref - lse_all
    row_index = jnp.arange(PROMPTS).astype(jnp.int32)[:, None]
    member = jnp.zeros(logits.shape, jnp.int32).at[row_index, refusal_ids].max(in_list.astype(jnp.int32)) > 0
    grad_logits = loss_scale[:, None] * (jnp.exp(jnp.where(member, logits - lse_ref[:, None], lowest)) - jnp.exp(logits - lse_all[:, None]))
    grad_b = grad_logits.astype(jnp.bfloat16)
    grad_normed = jnp.dot(grad_b, head.T, preferred_element_type=jnp.float32)
    row_term = lax.optimization_barrier(jnp.sum(grad_normed * normed.astype(jnp.float32), axis=1))
    grad_hidden = inverse_rms * gain * grad_normed - hidden_f * (inverse_rms * inverse_rms / D) * row_term[:, None]
    return (grad_hidden, log_refusal)
```

```python
import jax
import jax.numpy as jnp
from jax import lax
from jax.experimental import pallas as pl
from jax.experimental.pallas import tpu as pltpu
from jax.sharding import PartitionSpec as P

epsilon = 1e-05
lowest = -1e30


def members(ids, start, width):
    rows = ids.shape[0]
    column = lax.broadcasted_iota(jnp.int32, (rows, width), 1) + start
    found = column == ids[:, 0:1]
    for k in range(1, ids.shape[1]):
        found = found | (column == ids[:, k : k + 1])
    return found


def stats_kernel(chunk, logits_ref, ids_ref, out_ref):
    rows, width = logits_ref.shape
    ids = ids_ref[...]
    peak_all = jnp.full((rows, 1), lowest, jnp.float32)
    peak_ref = jnp.full((rows, 1), lowest, jnp.float32)
    for start in range(0, width, chunk):
        piece = logits_ref[:, start : start + chunk]
        found = members(ids, start, chunk)
        peak_all = jnp.maximum(peak_all, jnp.max(piece, axis=1, keepdims=True))
        peak_ref = jnp.maximum(
            peak_ref, jnp.max(jnp.where(found, piece, lowest), axis=1, keepdims=True)
        )
    sum_all = jnp.zeros((rows, 1), jnp.float32)
    sum_ref = jnp.zeros((rows, 1), jnp.float32)
    for start in range(0, width, chunk):
        piece = logits_ref[:, start : start + chunk]
        found = members(ids, start, chunk)
        sum_all = sum_all + jnp.sum(jnp.exp(piece - peak_all), axis=1, keepdims=True)
        sum_ref = sum_ref + jnp.sum(
            jnp.exp(jnp.where(found, piece - peak_ref, lowest)), axis=1, keepdims=True
        )
    lane = lax.broadcasted_iota(jnp.int32, out_ref.shape, 1)
    out_ref[...] = jnp.where(
        lane == 0, peak_all, jnp.where(lane == 1, peak_ref, jnp.where(lane == 2, sum_all, sum_ref))
    )


def row_stats(logits, ids):
    rows, width = logits.shape
    block = min(rows, 16)
    return pl.pallas_call(
        lambda *refs: stats_kernel(min(width, 1024), *refs),
        grid=(rows // block,),
        in_specs=[
            pl.BlockSpec((block, width), lambda i: (i, 0)),
            pl.BlockSpec((block, ids.shape[1]), lambda i: (i, 0)),
        ],
        out_specs=pl.BlockSpec((block, 128), lambda i: (i, 0)),
        out_shape=jax.ShapeDtypeStruct((rows, 128), jnp.float32),
        name="row_stats",
    )(logits, ids)


def grad_kernel(chunk, logits_ref, ids_ref, scalars_ref, out_ref, term_ref):
    rows, width = logits_ref.shape
    ids = ids_ref[...]
    lse_ref = scalars_ref[:, 0:1]
    lse_all = scalars_ref[:, 1:2]
    scale = scalars_ref[:, 2:3]
    term = jnp.zeros((rows, 1), jnp.float32)
    for start in range(0, width, chunk):
        piece = logits_ref[:, start : start + chunk]
        found = members(ids, start, chunk)
        grad = scale * (
            jnp.exp(jnp.where(found, piece - lse_ref, lowest)) - jnp.exp(piece - lse_all)
        )
        grad = grad.astype(jnp.bfloat16)
        out_ref[:, start : start + chunk] = grad
        term = term + jnp.sum(grad.astype(jnp.float32) * piece, axis=1, keepdims=True)
    term_ref[...] = jnp.broadcast_to(term, term_ref.shape)


def logit_grads(logits, ids, scalars):
    rows, width = logits.shape
    block = min(rows, 16)
    return pl.pallas_call(
        lambda *refs: grad_kernel(min(width, 1024), *refs),
        grid=(rows // block,),
        in_specs=[
            pl.BlockSpec((block, width), lambda i: (i, 0)),
            pl.BlockSpec((block, ids.shape[1]), lambda i: (i, 0)),
            pl.BlockSpec((block, scalars.shape[1]), lambda i: (i, 0)),
        ],
        out_specs=[
            pl.BlockSpec((block, width), lambda i: (i, 0)),
            pl.BlockSpec((block, 128), lambda i: (i, 0)),
        ],
        out_shape=[
            jax.ShapeDtypeStruct((rows, width), jnp.bfloat16),
            jax.ShapeDtypeStruct((rows, 128), jnp.float32),
        ],
        name="logit_grads",
    )(logits, ids, scalars)


def shards(hidden, head, gain, refusal_ids, refusal_count, loss_scale):
    row_count, model_width = hidden.shape
    vocab_local = head.shape[1]
    list_length = refusal_ids.shape[1]
    prompt_size = lax.axis_size("prompt")
    vocab_size = lax.axis_size("vocab")
    group = vocab_size // prompt_size

    hidden_f = hidden.astype(jnp.float32)
    inverse_rms = lax.rsqrt(jnp.mean(hidden_f * hidden_f, axis=1, keepdims=True) + epsilon)
    normed = (hidden_f * inverse_rms * gain).astype(jnp.bfloat16)
    normed_all = lax.all_to_all(normed, "prompt", split_axis=1, concat_axis=0, tiled=True)
    partial = jnp.dot(normed_all, head, preferred_element_type=jnp.float32)
    logits = lax.psum_scatter(partial, "prompt", scatter_dimension=0, tiled=True)

    vocab_start = lax.axis_index("vocab") * vocab_local
    in_list = jnp.arange(list_length)[None, :] < refusal_count[:, None]
    ids = jnp.where(in_list, refusal_ids - vocab_start, -1)

    stats = row_stats(logits, ids)[:, :4].T
    stats = lax.all_gather(stats, "vocab", axis=0)
    peaks = jnp.max(stats[:, :2], axis=0)
    sums = jnp.sum(stats[:, 2:] * jnp.exp(stats[:, :2] - peaks[None]), axis=0)
    lse_all, lse_ref = peaks + jnp.log(sums)
    log_refusal = lse_ref - lse_all

    scalars = jnp.stack([lse_ref, lse_all, loss_scale, loss_scale], axis=1)
    grad_b, term = logit_grads(logits, ids, scalars)
    row_term = lax.psum(term[:, 0], "vocab")

    grad_all = lax.all_gather(grad_b, "prompt", axis=0, tiled=True)
    grad_part = lax.dot_general(
        grad_all, head, (((1,), (1,)), ((), ())), preferred_element_type=jnp.float32
    )
    grad_rows = lax.psum_scatter(grad_part, "vocab", scatter_dimension=0, tiled=True)
    moves = []
    for p in range(prompt_size):
        for r in range(prompt_size):
            for i in range(group):
                moves.append((p * vocab_size + r * group + i, r * vocab_size + p * group + i))
    grad_rows = lax.ppermute(grad_rows, ("prompt", "vocab"), moves)
    groups = [[p * group + i for i in range(group)] for p in range(prompt_size)]
    grad_cols = lax.all_to_all(
        grad_rows, "vocab", split_axis=1, concat_axis=0, axis_index_groups=groups, tiled=True
    )

    slice_width = model_width // vocab_size
    col_start = lax.axis_index("vocab") * slice_width
    hidden_cols = lax.dynamic_slice_in_dim(hidden, col_start, slice_width, 1).astype(jnp.float32)
    gain_cols = lax.dynamic_slice_in_dim(gain, col_start, slice_width, 0)
    grad_hidden = (
        inverse_rms * gain_cols * grad_cols
        - hidden_cols * (inverse_rms * inverse_rms / model_width) * row_term[:, None]
    )
    return (grad_hidden, log_refusal)


def solution(mesh):
    return jax.shard_map(
        shards,
        mesh=mesh,
        in_specs=(
            P("prompt", None),
            P("prompt", "vocab"),
            P(),
            P("prompt", None),
            P("prompt"),
            P("prompt"),
        ),
        out_specs=(P("prompt", "vocab"), P("prompt")),
        check_vma=False,
    )
```

```python
import functools
import math

import jax
import jax.numpy as jnp
from jax import lax
from jax.experimental import pallas as pl
from jax.experimental.pallas import tpu as pltpu
from jax.sharding import PartitionSpec as P

epsilon = 1e-05
lowest = -1e30
tail = 128
steps = 64
code_top = 32000.0
per_step = math.log(2.0) / steps
megabyte = 1024 * 1024


def encode(value):
    top = jnp.max(jnp.abs(value), axis=1, keepdims=True)
    power = jnp.ceil(jnp.log(jnp.maximum(top, 1e-30) * (1.0 / code_top)) * (1.0 / per_step))
    code = jnp.round(value * jnp.exp(power * -per_step))
    return code.astype(jnp.int32).astype(jnp.int16), power


def decode(codes_ref, tile, width, vocab_local, rows=slice(None)):
    powers = codes_ref[rows, vocab_local : vocab_local + tail].astype(jnp.int32).astype(jnp.float32)
    lane = lax.broadcasted_iota(jnp.int32, powers.shape, 1)
    power = jnp.sum(jnp.where(lane == tile, powers, 0.0), axis=1, keepdims=True)
    start = tile * width
    if not isinstance(start, int):
        start = pl.multiple_of(start, width)
    codes = codes_ref[rows, pl.ds(start, width)].astype(jnp.int32).astype(jnp.float32)
    return codes * jnp.exp(power * per_step)


def put(out_ref, powers_ref, rows, tile, width, vocab_local, value):
    code, power = encode(value)
    out_ref[:, pl.ds(pl.multiple_of(tile * width, width), width)] = code
    lane = lax.broadcasted_iota(jnp.int32, (value.shape[0], tail), 1)
    powers = jnp.where(lane >= tile, power, powers_ref[rows, :])
    powers_ref[rows, :] = powers
    out_ref[:, vocab_local:] = powers.astype(jnp.int32).astype(jnp.int16)


def dot(a, b):
    return jnp.dot(a, b, preferred_element_type=jnp.float32)


def far_kernel(width, vocab_local, x_ref, head_ref, first_ref, second_ref, powers_ref):
    tile = pl.program_id(0)
    value = dot(x_ref[...], head_ref[...])
    half = value.shape[0] // 2
    put(first_ref, powers_ref, slice(0, half), tile, width, vocab_local, value[:half])
    put(second_ref, powers_ref, slice(half, 2 * half), tile, width, vocab_local, value[half:])


def far_codes(rows_in, head, width):
    rows, depth = rows_in.shape
    vocab_local = head.shape[1]
    return pl.pallas_call(
        functools.partial(far_kernel, width, vocab_local),
        grid=(vocab_local // width,),
        in_specs=[
            pl.BlockSpec((rows, depth), lambda j: (0, 0)),
            pl.BlockSpec((depth, width), lambda j: (0, j)),
        ],
        out_specs=[pl.BlockSpec((rows // 2, vocab_local + tail), lambda j: (0, 0))] * 2,
        out_shape=[jax.ShapeDtypeStruct((rows // 2, vocab_local + tail), jnp.int16)] * 2,
        scratch_shapes=[pltpu.VMEM((rows, tail), jnp.float32)],
        compiler_params=pltpu.CompilerParams(vmem_limit_bytes=40 * megabyte),
        cost_estimate=pl.CostEstimate(
            flops=2 * rows * depth * vocab_local,
            bytes_accessed=2 * depth * vocab_local,
            transcendentals=0,
        ),
        name="far_codes",
    )(rows_in, head)


def near_kernel(
    width, vocab_local, x_ref, y_ref, head_ref, by_x_ref, by_y_ref, to_x_ref, to_y_ref, powers_ref
):
    tile = pl.program_id(0)
    rows = x_ref.shape[0]
    half = rows // 2
    value = dot(jnp.concatenate([x_ref[...], y_ref[...]], axis=0), head_ref[...])
    for_x, for_y = value[:rows], value[rows:]
    more_x = decode(by_y_ref, tile, width, vocab_local)
    more_y = decode(by_x_ref, tile, width, vocab_local)
    for_x = jnp.concatenate([for_x[:half], for_x[half:] + more_x], axis=0)
    for_y = jnp.concatenate([for_y[:half] + more_y, for_y[half:]], axis=0)
    put(to_x_ref, powers_ref, slice(0, rows), tile, width, vocab_local, for_x)
    put(to_y_ref, powers_ref, slice(rows, 2 * rows), tile, width, vocab_local, for_y)


def near_codes(part, rows_x, rows_y, head, by_x, by_y, width):
    depth = rows_x.shape[1]
    rows = rows_x.shape[0] // 2
    vocab_local = head.shape[1]
    whole = lambda r: pl.BlockSpec((r, vocab_local + tail), lambda j: (0, 0))
    return pl.pallas_call(
        functools.partial(near_kernel, width, vocab_local),
        grid=(vocab_local // width,),
        in_specs=[
            pl.BlockSpec((rows, depth), lambda j: (part, 0)),
            pl.BlockSpec((rows, depth), lambda j: (part, 0)),
            pl.BlockSpec((depth, width), lambda j: (0, j)),
            whole(rows // 2),
            whole(rows // 2),
        ],
        out_specs=[whole(rows)] * 2,
        out_shape=[jax.ShapeDtypeStruct((rows, vocab_local + tail), jnp.int16)] * 2,
        scratch_shapes=[pltpu.VMEM((2 * rows, tail), jnp.float32)],
        compiler_params=pltpu.CompilerParams(vmem_limit_bytes=40 * megabyte),
        cost_estimate=pl.CostEstimate(
            flops=4 * rows * depth * vocab_local,
            bytes_accessed=2 * depth * vocab_local,
            transcendentals=0,
        ),
        name="near_codes",
    )(rows_x, rows_y, head, by_x, by_y)


def own_kernel(x_ref, head_ref, out_ref):
    out_ref[...] = dot(x_ref[...], head_ref[...])


def own_logits(rows_in, head, width):
    rows, depth = rows_in.shape
    vocab_local = head.shape[1]
    return pl.pallas_call(
        own_kernel,
        grid=(vocab_local // width,),
        in_specs=[
            pl.BlockSpec((rows, depth), lambda j: (0, 0)),
            pl.BlockSpec((depth, width), lambda j: (0, j)),
        ],
        out_specs=pl.BlockSpec((rows, width), lambda j: (0, j)),
        out_shape=jax.ShapeDtypeStruct((rows, vocab_local), jnp.float32),
        compiler_params=pltpu.CompilerParams(vmem_limit_bytes=40 * megabyte),
        cost_estimate=pl.CostEstimate(
            flops=2 * rows * depth * vocab_local,
            bytes_accessed=2 * depth * vocab_local,
            transcendentals=0,
        ),
        name="own_logits",
    )(rows_in, head)


def members(ids, start, width):
    rows = ids.shape[0]
    column = lax.broadcasted_iota(jnp.int32, (rows, width), 1) + start
    found = column == ids[:, 0:1]
    for k in range(1, ids.shape[1]):
        found = found | (column == ids[:, k : k + 1])
    return found


def stats_kernel(width, vocab_local, own_ref, by_x_ref, by_y_ref, ids_ref, logits_ref, listed_ref, out_ref):
    rows = own_ref.shape[0]
    ids = ids_ref[...]
    top_all = jnp.full((rows, width), lowest, jnp.float32)
    top_ref = jnp.full((rows, width), lowest, jnp.float32)
    for tile in range(vocab_local // width):
        at = slice(tile * width, (tile + 1) * width)
        piece = (
            own_ref[:, at]
            + decode(by_x_ref, tile, width, vocab_local)
            + decode(by_y_ref, tile, width, vocab_local)
        )
        listed = jnp.where(members(ids, tile * width, width), piece, lowest)
        logits_ref[:, at] = piece
        listed_ref[:, at] = listed
        top_all = jnp.maximum(top_all, piece)
        top_ref = jnp.maximum(top_ref, listed)
    peak_all = jnp.max(top_all, axis=1, keepdims=True)
    peak_ref = jnp.max(top_ref, axis=1, keepdims=True)
    sum_all = jnp.zeros((rows, width), jnp.float32)
    sum_ref = jnp.zeros((rows, width), jnp.float32)
    for tile in range(vocab_local // width):
        at = slice(tile * width, (tile + 1) * width)
        sum_all = sum_all + jnp.exp(logits_ref[:, at] - peak_all)
        sum_ref = sum_ref + jnp.exp(listed_ref[:, at] - peak_ref)
    sum_all = jnp.sum(sum_all, axis=1, keepdims=True)
    sum_ref = jnp.sum(sum_ref, axis=1, keepdims=True)
    lane = lax.broadcasted_iota(jnp.int32, out_ref.shape, 1)
    out_ref[...] = jnp.where(
        lane == 0, peak_all, jnp.where(lane == 1, peak_ref, jnp.where(lane == 2, sum_all, sum_ref))
    )


def row_stats(part, own, by_x, by_y, ids, width):
    rows = by_x.shape[0]
    vocab_local = own.shape[1]
    block = 16
    skip = part * (rows // block)
    return pl.pallas_call(
        functools.partial(stats_kernel, width, vocab_local),
        grid=(rows // block,),
        in_specs=[
            pl.BlockSpec((block, vocab_local), lambda i: (i + skip, 0)),
            pl.BlockSpec((block, vocab_local + tail), lambda i: (i, 0)),
            pl.BlockSpec((block, vocab_local + tail), lambda i: (i, 0)),
            pl.BlockSpec((block, ids.shape[1]), lambda i: (i + skip, 0)),
        ],
        out_specs=[
            pl.BlockSpec((block, vocab_local), lambda i: (i, 0)),
            pl.BlockSpec((block, vocab_local), lambda i: (i, 0)),
            pl.BlockSpec((block, 128), lambda i: (i, 0)),
        ],
        out_shape=[
            jax.ShapeDtypeStruct((rows, vocab_local), jnp.float32),
            jax.ShapeDtypeStruct((rows, vocab_local), jnp.float32),
            jax.ShapeDtypeStruct((rows, 128), jnp.float32),
        ],
        compiler_params=pltpu.CompilerParams(vmem_limit_bytes=40 * megabyte),
        cost_estimate=pl.CostEstimate(
            flops=64 * rows * vocab_local,
            bytes_accessed=16 * rows * vocab_local,
            transcendentals=2 * rows * vocab_local,
        ),
        name="row_stats",
    )(own, by_x, by_y, ids)


def grad_kernel(width, logits_ref, listed_ref, scalars_ref, out_ref, term_ref):
    rows, vocab_local = logits_ref.shape
    lse_ref = scalars_ref[:, 0:1]
    lse_all = scalars_ref[:, 1:2]
    scale = scalars_ref[:, 2:3]
    term = jnp.zeros((rows, width), jnp.float32)
    for start in range(0, vocab_local, width):
        at = slice(start, start + width)
        piece = logits_ref[:, at]
        grad = scale * (jnp.exp(listed_ref[:, at] - lse_ref) - jnp.exp(piece - lse_all))
        grad = grad.astype(jnp.bfloat16)
        out_ref[:, at] = grad
        term = term + grad.astype(jnp.float32) * piece
    term_ref[...] = jnp.broadcast_to(jnp.sum(term, axis=1, keepdims=True), term_ref.shape)


def logit_grads(logits, listed, scalars, width):
    rows, vocab_local = logits.shape
    block = 16
    return pl.pallas_call(
        functools.partial(grad_kernel, width),
        grid=(rows // block,),
        in_specs=[
            pl.BlockSpec((block, vocab_local), lambda i: (i, 0)),
            pl.BlockSpec((block, vocab_local), lambda i: (i, 0)),
            pl.BlockSpec((block, scalars.shape[1]), lambda i: (i, 0)),
        ],
        out_specs=[
            pl.BlockSpec((block, vocab_local), lambda i: (i, 0)),
            pl.BlockSpec((block, 128), lambda i: (i, 0)),
        ],
        out_shape=[
            jax.ShapeDtypeStruct((rows, vocab_local), jnp.bfloat16),
            jax.ShapeDtypeStruct((rows, 128), jnp.float32),
        ],
        compiler_params=pltpu.CompilerParams(vmem_limit_bytes=40 * megabyte),
        cost_estimate=pl.CostEstimate(
            flops=8 * rows * vocab_local,
            bytes_accessed=10 * rows * vocab_local,
            transcendentals=2 * rows * vocab_local,
        ),
        name="logit_grads",
    )(logits, listed, scalars)


def after(value, *others):
    return lax.optimization_barrier((value, *others))[0]


def shards(hidden, head, gain, refusal_ids, refusal_count, loss_scale):
    row_count, model_width = hidden.shape
    depth, vocab_local = head.shape
    list_length = refusal_ids.shape[1]
    prompt_size = lax.axis_size("prompt")
    vocab_size = lax.axis_size("vocab")
    group = vocab_size // prompt_size
    width = min(1024, vocab_local)
    half = row_count // 2
    me = lax.axis_index("prompt")
    to_x, to_y, to_far = ([(p, p ^ k) for p in range(prompt_size)] for k in (1, 2, 3))
    send = lambda value, pairs: lax.ppermute(value, "prompt", pairs)

    hidden_f = hidden.astype(jnp.float32)
    inverse_rms = lax.rsqrt(jnp.mean(hidden_f * hidden_f, axis=1, keepdims=True) + epsilon)
    normed = (hidden_f * inverse_rms * gain).astype(jnp.bfloat16)
    columns = lambda p: lax.dynamic_slice_in_dim(normed, p * depth, depth, 1)
    for_far = columns(me ^ 3)
    far = [send(for_far[:half], to_far), send(for_far[half:], to_far)]
    rows_x = send(columns(me ^ 1), to_x)
    rows_y = send(columns(me ^ 2), to_y)

    far_a = far_codes(far[0], head, width)
    by_x_a, by_y_a = send(far_a[0], to_x), send(far_a[1], to_y)
    far_b = far_codes(after(far[1], *far_a), head, width)
    by_x_b, by_y_b = send(far_b[0], to_x), send(far_b[1], to_y)
    near_a = near_codes(0, rows_x, rows_y, head, by_x_a, by_y_a, width)
    sums_a = send(near_a[0], to_x), send(near_a[1], to_y)
    near_b = near_codes(1, rows_x, rows_y, head, by_x_b, by_y_b, width)
    own = own_logits(after(columns(me), *near_b), head, width)
    sums_b = send(near_b[0], to_x), send(near_b[1], to_y)

    vocab_start = lax.axis_index("vocab") * vocab_local
    in_list = jnp.arange(list_length)[None, :] < refusal_count[:, None]
    ids = jnp.where(in_list, refusal_ids - vocab_start, -1)

    moves = []
    for p in range(prompt_size):
        for r in range(prompt_size):
            for i in range(group):
                moves.append((p * vocab_size + r * group + i, r * vocab_size + p * group + i))
    groups = [[p * group + i for i in range(group)] for p in range(prompt_size)]

    grads, terms, logs = [], [], []
    for part, sums in enumerate((sums_a, sums_b)):
        logits, listed, stats = row_stats(part, own, *sums, ids, width)
        stats = lax.all_gather(stats[:, :4].T, "vocab", axis=0)
        peaks = jnp.max(stats[:, :2], axis=0)
        sums = jnp.sum(stats[:, 2:] * jnp.exp(stats[:, :2] - peaks[None]), axis=0)
        lse_all, lse_ref = peaks + jnp.log(sums)
        logs.append(lse_ref - lse_all)
        scale = loss_scale[part * half : (part + 1) * half]
        scalars = jnp.stack([lse_ref, lse_all, scale, scale], axis=1)
        grad_b, term = logit_grads(logits, listed, scalars, width)
        terms.append(term[:, 0])
        grad_all = lax.all_gather(grad_b, "prompt", axis=0, tiled=True)
        grad_part = lax.dot_general(
            grad_all, head, (((1,), (1,)), ((), ())), preferred_element_type=jnp.float32
        )
        grads.append(lax.psum_scatter(grad_part, "vocab", scatter_dimension=0, tiled=True))
    row_term = lax.psum(jnp.concatenate(terms), "vocab")
    log_refusal = jnp.concatenate(logs)

    grad_cols = []
    for grad_rows in grads:
        grad_rows = lax.ppermute(grad_rows, ("prompt", "vocab"), moves)
        grad_cols.append(
            lax.all_to_all(
                grad_rows, "vocab", split_axis=1, concat_axis=0, axis_index_groups=groups, tiled=True
            )
        )
    grad_cols = jnp.concatenate(grad_cols)

    slice_width = model_width // vocab_size
    col_start = lax.axis_index("vocab") * slice_width
    hidden_cols = lax.dynamic_slice_in_dim(hidden, col_start, slice_width, 1).astype(jnp.float32)
    gain_cols = lax.dynamic_slice_in_dim(gain, col_start, slice_width, 0)
    grad_hidden = (
        inverse_rms * gain_cols * grad_cols
        - hidden_cols * (inverse_rms * inverse_rms / model_width) * row_term[:, None]
    )
    return (grad_hidden, log_refusal)


def solution(mesh):
    return jax.shard_map(
        shards,
        mesh=mesh,
        in_specs=(
            P("prompt", None),
            P("prompt", "vocab"),
            P(),
            P("prompt", None),
            P("prompt"),
            P("prompt"),
        ),
        out_specs=(P("prompt", "vocab"), P("prompt")),
        check_vma=False,
    )
```

```python
import functools
import math

import jax
import jax.numpy as jnp
from jax import lax
from jax.experimental import pallas as pl
from jax.experimental.pallas import tpu as pltpu
from jax.sharding import PartitionSpec as P

epsilon = 1e-05
lowest = -1e30
tail = 128
steps = 64
code_top = 32000.0
per_step = math.log(2.0) / steps
megabyte = 1024 * 1024


def encode(value):
    top = jnp.max(jnp.abs(value), axis=1, keepdims=True)
    power = jnp.ceil(jnp.log(jnp.maximum(top, 1e-30) * (1.0 / code_top)) * (1.0 / per_step))
    code = jnp.round(value * jnp.exp(power * -per_step))
    return code.astype(jnp.int32).astype(jnp.int16), power


def decode(codes_ref, tile, width, vocab_local, rows=slice(None)):
    powers = codes_ref[rows, vocab_local : vocab_local + tail].astype(jnp.int32).astype(jnp.float32)
    lane = lax.broadcasted_iota(jnp.int32, powers.shape, 1)
    power = jnp.sum(jnp.where(lane == tile, powers, 0.0), axis=1, keepdims=True)
    start = tile * width
    if not isinstance(start, int):
        start = pl.multiple_of(start, width)
    codes = codes_ref[rows, pl.ds(start, width)].astype(jnp.int32).astype(jnp.float32)
    return codes * jnp.exp(power * per_step)


def put(out_ref, powers_ref, rows, tile, width, vocab_local, value):
    code, power = encode(value)
    out_ref[:, pl.ds(pl.multiple_of(tile * width, width), width)] = code
    lane = lax.broadcasted_iota(jnp.int32, (value.shape[0], tail), 1)
    powers = jnp.where(lane >= tile, power, powers_ref[rows, :])
    powers_ref[rows, :] = powers
    out_ref[:, vocab_local:] = powers.astype(jnp.int32).astype(jnp.int16)


def dot(a, b):
    return jnp.dot(a, b, preferred_element_type=jnp.float32)


def compiler_params():
    return pltpu.CompilerParams(vmem_limit_bytes=40 * megabyte)


def small_cost():
    return pl.CostEstimate(flops=1024, bytes_accessed=1024, transcendentals=0)


def constant(*shape):
    return pl.BlockSpec(shape, lambda *_: (0,) * len(shape))


def far_kernel(width, x_ref, head_ref, first_ref, second_ref, powers_ref):
    tile = pl.program_id(0)
    columns = first_ref.shape[1] - tail
    value = dot(x_ref[...], head_ref[...])
    q = value.shape[0] // 4
    first = jnp.concatenate([value[:q], value[2 * q : 3 * q]], axis=0)
    second = jnp.concatenate([value[q : 2 * q], value[3 * q :]], axis=0)
    put(first_ref, powers_ref, slice(0, 2 * q), tile, width, columns, first)
    put(second_ref, powers_ref, slice(2 * q, 4 * q), tile, width, columns, second)


def far_codes(rows_in, head, width, skip, tiles):
    rows, depth = rows_in.shape
    columns = tiles * width
    return pl.pallas_call(
        functools.partial(far_kernel, width),
        grid=(tiles,),
        in_specs=[
            constant(rows, depth),
            pl.BlockSpec((depth, width), lambda j: (0, j + skip)),
        ],
        out_specs=[constant(rows // 2, columns + tail)] * 2,
        out_shape=[jax.ShapeDtypeStruct((rows // 2, columns + tail), jnp.int16)] * 2,
        scratch_shapes=[pltpu.VMEM((rows, tail), jnp.float32)],
        compiler_params=compiler_params(),
        cost_estimate=small_cost(),
        name="far_codes",
    )(rows_in, head)


def decode_any(refs, tile, width):
    columns = refs[0].shape[1] - tail
    if len(refs) == 1:
        return decode(refs[0], tile, width, columns)
    each = columns // width
    if isinstance(tile, int):
        return decode(refs[tile // each], tile % each, width, columns)
    low = decode(refs[0], jnp.minimum(tile, each - 1), width, columns)
    high = decode(refs[1], jnp.maximum(tile - each, 0), width, columns)
    return jnp.where(tile < each, low, high)


def near_kernel(width, parts, x_ref, y_ref, own_ref, head_ref, *refs):
    by_x_refs, by_y_refs = refs[:parts], refs[parts : 2 * parts]
    to_x_ref, to_y_ref, out_ref, powers_ref = refs[2 * parts :]
    tile = pl.program_id(0)
    rows = x_ref.shape[0]
    half = rows // 2
    columns = to_x_ref.shape[1] - tail
    value = dot(jnp.concatenate([x_ref[...], y_ref[...], own_ref[...]], axis=0), head_ref[...])
    out_ref[...] = value[2 * rows :]
    more_x = decode_any(by_y_refs, tile, width)
    more_y = decode_any(by_x_refs, tile, width)
    for_x = jnp.concatenate([value[:half], value[half:rows] + more_x], axis=0)
    for_y = jnp.concatenate([value[rows : rows + half] + more_y, value[rows + half : 2 * rows]], axis=0)
    put(to_x_ref, powers_ref, slice(0, rows), tile, width, columns, for_x)
    put(to_y_ref, powers_ref, slice(rows, 2 * rows), tile, width, columns, for_y)


def near_codes(part, rows_x, rows_y, rows_own, head, by_x, by_y, width, skip, tiles):
    depth = rows_x.shape[1]
    rows = rows_x.shape[0] // 2
    columns = tiles * width
    received = pl.BlockSpec((rows // 2, by_x[0].shape[1]), lambda j: (part, 0))
    return pl.pallas_call(
        functools.partial(near_kernel, width, len(by_x)),
        grid=(tiles,),
        in_specs=[pl.BlockSpec((rows, depth), lambda j: (part, 0))] * 3
        + [pl.BlockSpec((depth, width), lambda j: (0, j + skip))]
        + [received] * (2 * len(by_x)),
        out_specs=[constant(rows, columns + tail)] * 2 + [pl.BlockSpec((rows, width), lambda j: (0, j))],
        out_shape=[jax.ShapeDtypeStruct((rows, columns + tail), jnp.int16)] * 2
        + [jax.ShapeDtypeStruct((rows, columns), jnp.float32)],
        scratch_shapes=[pltpu.VMEM((2 * rows, tail), jnp.float32)],
        compiler_params=compiler_params(),
        cost_estimate=small_cost(),
        name="near_codes",
    )(rows_x, rows_y, rows_own, head, *by_x, *by_y)


def members(ids, start, width):
    rows = ids.shape[0]
    column = lax.broadcasted_iota(jnp.int32, (rows, width), 1) + start
    found = column == ids[:, 0:1]
    for k in range(1, ids.shape[1]):
        found = found | (column == ids[:, k : k + 1])
    return found


def stats_kernel(width, parts, *refs):
    own_refs, by_x_refs, by_y_refs = refs[:parts], refs[parts : 2 * parts], refs[2 * parts : 3 * parts]
    ids_ref, logits_ref, listed_ref, out_ref = refs[3 * parts :]
    rows, columns = logits_ref.shape
    each = columns // parts
    ids = ids_ref[...]
    top_all = jnp.full((rows, width), lowest, jnp.float32)
    top_ref = jnp.full((rows, width), lowest, jnp.float32)
    for start in range(0, columns, width):
        at = slice(start, start + width)
        inner = start % each
        piece = own_refs[start // each][:, inner : inner + width]
        piece = piece + decode_any(by_x_refs, start // width, width)
        piece = piece + decode_any(by_y_refs, start // width, width)
        listed = jnp.where(members(ids, start, width), piece, lowest)
        logits_ref[:, at] = piece
        listed_ref[:, at] = listed
        top_all = jnp.maximum(top_all, piece)
        top_ref = jnp.maximum(top_ref, listed)
    peak_all = jnp.max(top_all, axis=1, keepdims=True)
    peak_ref = jnp.max(top_ref, axis=1, keepdims=True)
    sum_all = jnp.zeros((rows, width), jnp.float32)
    sum_ref = jnp.zeros((rows, width), jnp.float32)
    for start in range(0, columns, width):
        at = slice(start, start + width)
        sum_all = sum_all + jnp.exp(logits_ref[:, at] - peak_all)
        sum_ref = sum_ref + jnp.exp(listed_ref[:, at] - peak_ref)
    sum_all = jnp.sum(sum_all, axis=1, keepdims=True)
    sum_ref = jnp.sum(sum_ref, axis=1, keepdims=True)
    lane = lax.broadcasted_iota(jnp.int32, out_ref.shape, 1)
    out_ref[...] = jnp.where(
        lane == 0, peak_all, jnp.where(lane == 1, peak_ref, jnp.where(lane == 2, sum_all, sum_ref))
    )


def row_stats(part, own, by_x, by_y, ids, width):
    rows = own[0].shape[0]
    parts = len(own)
    columns = own[0].shape[1] * parts
    block = min(rows, 16)
    skip = part * (rows // block)
    across = lambda array: pl.BlockSpec((block, array.shape[1]), lambda i: (i, 0))
    return pl.pallas_call(
        functools.partial(stats_kernel, width, parts),
        grid=(rows // block,),
        in_specs=[across(a) for a in (*own, *by_x, *by_y)]
        + [pl.BlockSpec((block, ids.shape[1]), lambda i: (i + skip, 0))],
        out_specs=[
            pl.BlockSpec((block, columns), lambda i: (i, 0)),
            pl.BlockSpec((block, columns), lambda i: (i, 0)),
            pl.BlockSpec((block, 128), lambda i: (i, 0)),
        ],
        out_shape=[
            jax.ShapeDtypeStruct((rows, columns), jnp.float32),
            jax.ShapeDtypeStruct((rows, columns), jnp.float32),
            jax.ShapeDtypeStruct((rows, 128), jnp.float32),
        ],
        compiler_params=compiler_params(),
        cost_estimate=small_cost(),
        name="row_stats",
    )(*own, *by_x, *by_y, ids)


def grad_kernel(width, logits_ref, listed_ref, stats_ref, scale_ref, out_ref, info_ref):
    rows, columns = logits_ref.shape
    stats = [stats_ref[v] for v in range(stats_ref.shape[0])]
    peaks = functools.reduce(jnp.maximum, [s[:, :2] for s in stats])
    sums = functools.reduce(jnp.add, [s[:, 2:4] * jnp.exp(s[:, :2] - peaks) for s in stats])
    lse = peaks + jnp.log(sums)
    lse_all, lse_ref = lse[:, 0:1], lse[:, 1:2]
    scale = scale_ref[...]
    term = jnp.zeros((rows, width), jnp.float32)
    for start in range(0, columns, width):
        at = slice(start, start + width)
        piece = logits_ref[:, at]
        grad = scale * (jnp.exp(listed_ref[:, at] - lse_ref) - jnp.exp(piece - lse_all))
        grad = grad.astype(jnp.bfloat16)
        out_ref[:, at] = grad
        term = term + grad.astype(jnp.float32) * piece
    lane = lax.broadcasted_iota(jnp.int32, info_ref.shape, 1)
    info_ref[...] = jnp.where(lane == 0, jnp.sum(term, axis=1, keepdims=True), lse_ref - lse_all)


def logit_grads(part, logits, listed, stats, scale, width):
    rows, columns = logits.shape
    block = min(rows, 16)
    skip = part * (rows // block)
    return pl.pallas_call(
        functools.partial(grad_kernel, width),
        grid=(rows // block,),
        in_specs=[
            pl.BlockSpec((block, columns), lambda i: (i, 0)),
            pl.BlockSpec((block, columns), lambda i: (i, 0)),
            pl.BlockSpec((stats.shape[0], block, 128), lambda i: (0, i, 0)),
            pl.BlockSpec((block, 1), lambda i: (i + skip, 0)),
        ],
        out_specs=[
            pl.BlockSpec((block, columns), lambda i: (i, 0)),
            pl.BlockSpec((block, 128), lambda i: (i, 0)),
        ],
        out_shape=[
            jax.ShapeDtypeStruct((rows, columns), jnp.bfloat16),
            jax.ShapeDtypeStruct((rows, 128), jnp.float32),
        ],
        compiler_params=compiler_params(),
        cost_estimate=small_cost(),
        name="logit_grads",
    )(logits, listed, stats, scale)


def put_row(out_ref, value):
    code, power = encode(value)
    width = value.shape[1]
    out_ref[:, :width] = code
    out_ref[:, width:] = jnp.broadcast_to(power, (value.shape[0], tail)).astype(jnp.int32).astype(jnp.int16)


def take_row(codes_ref):
    width = codes_ref.shape[1] - tail
    power = codes_ref[:, width:].astype(jnp.int32).astype(jnp.float32)[:, 0:1]
    return codes_ref[:, :width].astype(jnp.int32).astype(jnp.float32) * jnp.exp(power * per_step)


def back_kernel(tiles, started, ends, place_ref, *refs):
    grads, head_ref, refs = refs[:5], refs[5], refs[6:]
    so_far_ref, refs = (refs[0], refs[1:]) if started else (None, refs)
    total_ref, refs = refs[-1], refs[:-1]
    tile = pl.program_id(0)

    @pl.when(tile == 0)
    def _():
        total_ref[...] = so_far_ref[...] if started else jnp.zeros_like(total_ref)

    grad = jnp.concatenate([g[...] for g in grads], axis=0)
    total_ref[...] += lax.dot_general(
        grad, head_ref[...], (((1,), (1,)), ((), ())), preferred_element_type=jnp.float32
    )

    @pl.when(tile == tiles - 1)
    def _():
        if not ends:
            refs[0][...] = total_ref[...]
            return
        keep_ref, sends = refs[0], refs[1:]
        width = keep_ref.shape[1]
        block = lambda b: total_ref[:, pl.ds(pl.multiple_of(b * width, width), width)]
        mine = place_ref[0]
        keep_ref[...] = block(mine)
        for k, send_ref in enumerate(sends, 1):
            put_row(send_ref, block(mine ^ k))


def back(grads, head, so_far, place, width, skip, tiles, group):
    depth = head.shape[0]
    rows = sum(g.shape[0] for g in grads)
    across = lambda g: pl.BlockSpec(
        (g.shape[0], width), (lambda j: (0, j + skip)) if g.shape[1] > tiles * width else (lambda j: (0, j))
    )
    started = [] if so_far is None else [so_far]
    if group:
        part = depth // group
        shapes = [((rows, part), jnp.float32)] + [((rows, part + tail), jnp.int16)] * (group - 1)
    else:
        shapes = [((rows, depth), jnp.float32)]
    return pl.pallas_call(
        functools.partial(back_kernel, tiles, bool(started), bool(group)),
        grid=(tiles,),
        in_specs=[pl.BlockSpec(memory_space=pltpu.SMEM)]
        + [across(g) for g in grads]
        + [pl.BlockSpec((depth, width), lambda j: (0, j + skip))]
        + [constant(rows, depth)] * len(started),
        out_specs=[constant(*shape) for shape, _ in shapes],
        out_shape=[jax.ShapeDtypeStruct(*s) for s in shapes],
        scratch_shapes=[pltpu.VMEM((rows, depth), jnp.float32)],
        compiler_params=compiler_params(),
        cost_estimate=small_cost(),
        name="grad_rows",
    )(place, *grads, head, *started)


def group_kernel(place_ref, keep_ref, *refs):
    total_ref = refs[-1]
    count = place_ref.shape[0] - 1
    out_ref, sends, received = refs[-2 - count], refs[-1 - count : -1], refs[: -2 - count]
    total = keep_ref[...]
    for codes_ref in received:
        total = total + take_row(codes_ref)
    total_ref[...] = total
    rows = out_ref.shape[0]
    block = lambda b: total_ref[pl.ds(pl.multiple_of(b * rows, rows), rows), :]
    out_ref[...] = block(place_ref[0])
    for k, send_ref in enumerate(sends, 1):
        put_row(send_ref, block(place_ref[k]))


def group_sum(place, keep, received):
    blocks = place.shape[0]
    rows, width = keep.shape
    own = (rows // blocks, width)
    coded = (rows // blocks, width + tail)
    return pl.pallas_call(
        group_kernel,
        in_specs=[pl.BlockSpec(memory_space=pltpu.SMEM)]
        + [pl.BlockSpec(memory_space=pltpu.VMEM)] * (1 + len(received)),
        out_specs=[pl.BlockSpec(memory_space=pltpu.VMEM)] * blocks,
        out_shape=[jax.ShapeDtypeStruct(own, jnp.float32)]
        + [jax.ShapeDtypeStruct(coded, jnp.int16)] * (blocks - 1),
        scratch_shapes=[pltpu.VMEM((rows, width), jnp.float32)],
        compiler_params=compiler_params(),
        cost_estimate=small_cost(),
        name="group_sum",
    )(place, keep, *received)


def after(value, *others):
    return lax.optimization_barrier((value, *others))[0]


def last_kernel(keep_ref, *refs):
    total = keep_ref[...]
    for codes_ref in refs[:-1]:
        total = total + take_row(codes_ref)
    put_row(refs[-1], total)


def last_sum(keep, received):
    rows, width = keep.shape
    return pl.pallas_call(
        last_kernel,
        in_specs=[pl.BlockSpec(memory_space=pltpu.VMEM)] * (1 + len(received)),
        out_specs=pl.BlockSpec(memory_space=pltpu.VMEM),
        out_shape=jax.ShapeDtypeStruct((rows, width + tail), jnp.int16),
        compiler_params=compiler_params(),
        cost_estimate=small_cost(),
        name="last_sum",
    )(keep, *received)


def shards(hidden, head, gain, refusal_ids, refusal_count, loss_scale):
    row_count, model_width = hidden.shape
    depth, vocab_local = head.shape
    list_length = refusal_ids.shape[1]
    prompt_size = lax.axis_size("prompt")
    vocab_size = lax.axis_size("vocab")
    group = vocab_size // prompt_size
    width = min(1024, vocab_local // 2)
    tiles = vocab_local // width
    half = row_count // 2
    me = lax.axis_index("prompt")
    shard = lax.axis_index("vocab")
    to_x, to_y, to_far = ([(p, p ^ k) for p in range(prompt_size)] for k in (1, 2, 3))
    send = lambda value, pairs: lax.ppermute(value, "prompt", pairs)

    hidden_f = hidden.astype(jnp.float32)
    inverse_rms = lax.rsqrt(jnp.mean(hidden_f * hidden_f, axis=1, keepdims=True) + epsilon)
    normed = (hidden_f * inverse_rms * gain).astype(jnp.bfloat16)
    columns = lambda p: lax.dynamic_slice_in_dim(normed, p * depth, depth, 1)
    rows_far = send(columns(me ^ 3), to_far)
    rows_x = send(columns(me ^ 1), to_x)
    rows_y = send(columns(me ^ 2), to_y)
    rows_own = columns(me)

    by_x, by_y = [], []
    for skip in (0, tiles // 2):
        first, second = far_codes(rows_far, head, width, skip, tiles // 2)
        by_x.append(send(first, to_x))
        by_y.append(send(second, to_y))
    own_a, sums_x_a, sums_y_a = [], [], []
    for c, skip in enumerate((0, tiles // 2)):
        codes_x, codes_y, own = near_codes(
            0, rows_x, rows_y, rows_own, head, [by_x[c]], [by_y[c]], width, skip, tiles // 2
        )
        own_a.append(own)
        sums_x_a.append(send(codes_x, to_x))
        sums_y_a.append(send(codes_y, to_y))
    codes_x, codes_y, own = near_codes(
        1, rows_x, rows_y, after(rows_own, *own_a), head, by_x, by_y, width, 0, tiles
    )
    halves = (
        (own_a, sums_x_a, sums_y_a),
        ([own], [send(codes_x, to_x)], [send(codes_y, to_y)]),
    )

    in_list = jnp.arange(list_length)[None, :] < refusal_count[:, None]
    ids = jnp.where(in_list, refusal_ids - shard * vocab_local, -1)

    block, member = shard // group, shard % group
    place_group = jnp.stack([member]).astype(jnp.int32)
    place_block = jnp.stack([block ^ k ^ me for k in range(prompt_size)]).astype(jnp.int32)
    to_member = [[(v, v ^ k) for v in range(vocab_size)] for k in range(1, group)]
    to_block = [
        [(v, ((v // group) ^ k) * group + v % group) for v in range(vocab_size)]
        for k in range(1, prompt_size)
    ]
    moves = []
    for p in range(prompt_size):
        for r in range(prompt_size):
            for i in range(group):
                moves.append((p * vocab_size + r * group + i, r * vocab_size + p * group + i))

    infos, grad_cols, grads, turns, before_back = [], [], [], [], []
    for part, (own, sums_x, sums_y) in enumerate(halves):
        logits, listed, stats = row_stats(part, own, sums_x, sums_y, after(ids, *infos), width)
        stats = lax.all_gather(stats, "vocab", axis=0)
        grad, info = logit_grads(part, logits, listed, stats, loss_scale[:, None], width)
        infos.append(info)
        grads.append((grad, send(grad, to_x), send(grad, to_y)))
    info = jnp.concatenate(infos)
    terms = lax.all_gather(info, "vocab", axis=0)

    for part, (grad, grad_x, grad_y) in enumerate(grads):
        quarter = half // 2
        pieces = 1 + part
        so_far = None
        grad_x, grad_y = after(grad_x, *turns), after(grad_y, *turns)
        for c in range(pieces):
            at = slice(c * vocab_local // pieces, (c + 1) * vocab_local // pieces)
            far_0 = send(grad_y[:quarter, at], to_x)
            far_1 = send(grad_x[quarter:, at], to_y)
            so_far = back(
                (grad, grad_x, grad_y, far_0, far_1),
                head,
                so_far,
                after(place_group, *before_back),
                width,
                c * tiles // pieces,
                tiles // pieces,
                group if c == pieces - 1 else 0,
            )
            if c < pieces - 1:
                so_far = so_far[0]
        keep, *codes = so_far
        turns = [keep]
        keep, *codes = group_sum(
            place_block, keep, [lax.ppermute(c, "vocab", to) for c, to in zip(codes, to_member)]
        )
        before_back = [keep, terms]
        codes = last_sum(keep, [lax.ppermute(c, "vocab", to) for c, to in zip(codes, to_block)])
        grad_cols.append(lax.ppermute(codes, ("prompt", "vocab"), moves))
    row_term = jnp.sum(terms[:, :, 0], axis=0)
    log_refusal = info[:, 1]

    slice_width = model_width // vocab_size
    col_start = shard * slice_width
    codes = jnp.concatenate(grad_cols)
    power = codes[:, slice_width : slice_width + 1].astype(jnp.float32)
    grad_cols = codes[:, :slice_width].astype(jnp.float32) * jnp.exp(power * per_step)
    hidden_cols = lax.dynamic_slice_in_dim(hidden, col_start, slice_width, 1).astype(jnp.float32)
    gain_cols = lax.dynamic_slice_in_dim(gain, col_start, slice_width, 0)
    grad_hidden = (
        inverse_rms * gain_cols * grad_cols
        - hidden_cols * (inverse_rms * inverse_rms / model_width) * row_term[:, None]
    )
    return (grad_hidden, log_refusal)


def solution(mesh):
    return jax.shard_map(
        shards,
        mesh=mesh,
        in_specs=(
            P("prompt", None),
            P("prompt", "vocab"),
            P(),
            P("prompt", None),
            P("prompt"),
            P("prompt"),
        ),
        out_specs=(P("prompt", "vocab"), P("prompt")),
        check_vma=False,
    )
```

```python
import functools
import math

import jax
import jax.numpy as jnp
from jax import lax
from jax.experimental import pallas as pl
from jax.experimental.pallas import tpu as pltpu
from jax.sharding import PartitionSpec as P

epsilon = 1e-05
lowest = -1e30
tail = 128
steps = 64
code_top = 32000.0
per_step = math.log(2.0) / steps
megabyte = 1024 * 1024


def encode(value):
    top = jnp.max(jnp.abs(value), axis=1, keepdims=True)
    power = jnp.ceil(jnp.log(jnp.maximum(top, 1e-30) * (1.0 / code_top)) * (1.0 / per_step))
    code = jnp.round(value * jnp.exp(power * -per_step))
    return code.astype(jnp.int32).astype(jnp.int16), power


def decode(codes_ref, tile, width, vocab_local, rows=slice(None)):
    powers = codes_ref[rows, vocab_local : vocab_local + tail].astype(jnp.int32).astype(jnp.float32)
    lane = lax.broadcasted_iota(jnp.int32, powers.shape, 1)
    power = jnp.sum(jnp.where(lane == tile, powers, 0.0), axis=1, keepdims=True)
    start = tile * width
    if not isinstance(start, int):
        start = pl.multiple_of(start, width)
    codes = codes_ref[rows, pl.ds(start, width)].astype(jnp.int32).astype(jnp.float32)
    return codes * jnp.exp(power * per_step)


def put(out_ref, powers_ref, rows, tile, width, vocab_local, value):
    code, power = encode(value)
    out_ref[:, pl.ds(pl.multiple_of(tile * width, width), width)] = code
    lane = lax.broadcasted_iota(jnp.int32, (value.shape[0], tail), 1)
    powers = jnp.where(lane >= tile, power, powers_ref[rows, :])
    powers_ref[rows, :] = powers
    out_ref[:, vocab_local:] = powers.astype(jnp.int32).astype(jnp.int16)


def dot(a, b):
    return jnp.dot(a, b, preferred_element_type=jnp.float32)


def compiler_params():
    return pltpu.CompilerParams(vmem_limit_bytes=20 * megabyte)


def small_cost():
    return pl.CostEstimate(flops=1024, bytes_accessed=1024, transcendentals=0)


def constant(*shape):
    return pl.BlockSpec(shape, lambda *_: (0,) * len(shape))


def far_kernel(width, x_ref, head_ref, first_ref, second_ref, powers_ref):
    tile = pl.program_id(0)
    columns = first_ref.shape[1] - tail
    value = dot(x_ref[...], head_ref[...])
    q = value.shape[0] // 4
    first = jnp.concatenate([value[:q], value[2 * q : 3 * q]], axis=0)
    second = jnp.concatenate([value[q : 2 * q], value[3 * q :]], axis=0)
    put(first_ref, powers_ref, slice(0, 2 * q), tile, width, columns, first)
    put(second_ref, powers_ref, slice(2 * q, 4 * q), tile, width, columns, second)


def far_codes(rows_in, head, width, skip, tiles):
    rows, depth = rows_in.shape
    columns = tiles * width
    return pl.pallas_call(
        functools.partial(far_kernel, width),
        grid=(tiles,),
        in_specs=[
            constant(rows, depth),
            pl.BlockSpec((depth, width), lambda j: (0, j + skip)),
        ],
        out_specs=[constant(rows // 2, columns + tail)] * 2,
        out_shape=[jax.ShapeDtypeStruct((rows // 2, columns + tail), jnp.int16)] * 2,
        scratch_shapes=[pltpu.VMEM((rows, tail), jnp.float32)],
        compiler_params=compiler_params(),
        cost_estimate=small_cost(),
        name="far_codes",
    )(rows_in, head)


def decode_any(refs, tile, width):
    columns = refs[0].shape[1] - tail
    if len(refs) == 1:
        return decode(refs[0], tile, width, columns)
    each = columns // width
    if isinstance(tile, int):
        return decode(refs[tile // each], tile % each, width, columns)
    low = decode(refs[0], jnp.minimum(tile, each - 1), width, columns)
    high = decode(refs[1], jnp.maximum(tile - each, 0), width, columns)
    return jnp.where(tile < each, low, high)


def near_kernel(width, parts, x_ref, y_ref, head_ref, *refs):
    by_x_refs, by_y_refs = refs[:parts], refs[parts : 2 * parts]
    to_x_ref, to_y_ref, powers_ref = refs[2 * parts :]
    tile = pl.program_id(0)
    rows = x_ref.shape[0]
    half = rows // 2
    columns = to_x_ref.shape[1] - tail
    value = dot(jnp.concatenate([x_ref[...], y_ref[...]], axis=0), head_ref[...])
    more_x = decode_any(by_y_refs, tile, width)
    more_y = decode_any(by_x_refs, tile, width)
    for_x = jnp.concatenate([value[:half], value[half:rows] + more_x], axis=0)
    for_y = jnp.concatenate([value[rows : rows + half] + more_y, value[rows + half :]], axis=0)
    put(to_x_ref, powers_ref, slice(0, rows), tile, width, columns, for_x)
    put(to_y_ref, powers_ref, slice(rows, 2 * rows), tile, width, columns, for_y)


def near_codes(part, rows_x, rows_y, head, by_x, by_y, width, skip, tiles):
    depth = rows_x.shape[1]
    rows = rows_x.shape[0] // 2
    columns = tiles * width
    received = pl.BlockSpec((rows // 2, by_x[0].shape[1]), lambda j: (part, 0))
    return pl.pallas_call(
        functools.partial(near_kernel, width, len(by_x)),
        grid=(tiles,),
        in_specs=[pl.BlockSpec((rows, depth), lambda j: (part, 0))] * 2
        + [pl.BlockSpec((depth, width), lambda j: (0, j + skip))]
        + [received] * (2 * len(by_x)),
        out_specs=[constant(rows, columns + tail)] * 2,
        out_shape=[jax.ShapeDtypeStruct((rows, columns + tail), jnp.int16)] * 2,
        scratch_shapes=[pltpu.VMEM((2 * rows, tail), jnp.float32)],
        compiler_params=compiler_params(),
        cost_estimate=small_cost(),
        name="near_codes",
    )(rows_x, rows_y, head, *by_x, *by_y)


def own_kernel(x_ref, head_ref, out_ref):
    out_ref[...] = dot(x_ref[...], head_ref[...])


def own_logits(rows_in, head, width):
    rows, depth = rows_in.shape
    columns = head.shape[1]
    return pl.pallas_call(
        own_kernel,
        grid=(columns // width,),
        in_specs=[
            constant(rows, depth),
            pl.BlockSpec((depth, width), lambda j: (0, j)),
        ],
        out_specs=pl.BlockSpec((rows, width), lambda j: (0, j)),
        out_shape=jax.ShapeDtypeStruct((rows, columns), jnp.float32),
        compiler_params=compiler_params(),
        cost_estimate=small_cost(),
        name="own_logits",
    )(rows_in, head)


def members(ids, start, width):
    rows = ids.shape[0]
    column = lax.broadcasted_iota(jnp.int32, (rows, width), 1) + start
    found = column == ids[:, 0:1]
    for k in range(1, ids.shape[1]):
        found = found | (column == ids[:, k : k + 1])
    return found


def stats_kernel(width, parts, *refs):
    own_ref, by_x_refs, by_y_refs = refs[0], refs[1 : 1 + parts], refs[1 + parts : 1 + 2 * parts]
    ids_ref, logits_ref, listed_ref, out_ref = refs[1 + 2 * parts :]
    rows, columns = logits_ref.shape
    ids = ids_ref[...]
    top_all = jnp.full((rows, width), lowest, jnp.float32)
    top_ref = jnp.full((rows, width), lowest, jnp.float32)
    for start in range(0, columns, width):
        at = slice(start, start + width)
        piece = own_ref[:, at] + decode_any(by_x_refs, start // width, width)
        piece = piece + decode_any(by_y_refs, start // width, width)
        listed = jnp.where(members(ids, start, width), piece, lowest)
        logits_ref[:, at] = piece
        listed_ref[:, at] = listed
        top_all = jnp.maximum(top_all, piece)
        top_ref = jnp.maximum(top_ref, listed)
    peak_all = jnp.max(top_all, axis=1, keepdims=True)
    peak_ref = jnp.max(top_ref, axis=1, keepdims=True)
    sum_all = jnp.zeros((rows, width), jnp.float32)
    sum_ref = jnp.zeros((rows, width), jnp.float32)
    for start in range(0, columns, width):
        at = slice(start, start + width)
        sum_all = sum_all + jnp.exp(logits_ref[:, at] - peak_all)
        sum_ref = sum_ref + jnp.exp(listed_ref[:, at] - peak_ref)
    sum_all = jnp.sum(sum_all, axis=1, keepdims=True)
    sum_ref = jnp.sum(sum_ref, axis=1, keepdims=True)
    lane = lax.broadcasted_iota(jnp.int32, out_ref.shape, 1)
    out_ref[...] = jnp.where(
        lane == 0, peak_all, jnp.where(lane == 1, peak_ref, jnp.where(lane == 2, sum_all, sum_ref))
    )


def row_stats(part, own, by_x, by_y, ids, width):
    rows = by_x[0].shape[0]
    parts = len(by_x)
    columns = own.shape[1]
    block = min(rows, 16)
    skip = part * (rows // block)
    across = lambda array: pl.BlockSpec((block, array.shape[1]), lambda i: (i, 0))
    return pl.pallas_call(
        functools.partial(stats_kernel, width, parts),
        grid=(rows // block,),
        in_specs=[pl.BlockSpec((block, columns), lambda i: (i + skip, 0))]
        + [across(a) for a in (*by_x, *by_y)]
        + [pl.BlockSpec((block, ids.shape[1]), lambda i: (i + skip, 0))],
        out_specs=[
            pl.BlockSpec((block, columns), lambda i: (i, 0)),
            pl.BlockSpec((block, columns), lambda i: (i, 0)),
            pl.BlockSpec((block, 128), lambda i: (i, 0)),
        ],
        out_shape=[
            jax.ShapeDtypeStruct((rows, columns), jnp.float32),
            jax.ShapeDtypeStruct((rows, columns), jnp.float32),
            jax.ShapeDtypeStruct((rows, 128), jnp.float32),
        ],
        compiler_params=compiler_params(),
        cost_estimate=small_cost(),
        name="row_stats",
    )(own, *by_x, *by_y, ids)


def grad_kernel(width, logits_ref, listed_ref, stats_ref, scale_ref, out_ref, info_ref):
    rows, columns = logits_ref.shape
    stats = [stats_ref[v] for v in range(stats_ref.shape[0])]
    peaks = functools.reduce(jnp.maximum, [s[:, :2] for s in stats])
    sums = functools.reduce(jnp.add, [s[:, 2:4] * jnp.exp(s[:, :2] - peaks) for s in stats])
    lse = peaks + jnp.log(sums)
    lse_all, lse_ref = lse[:, 0:1], lse[:, 1:2]
    scale = scale_ref[...]
    term = jnp.zeros((rows, width), jnp.float32)
    for start in range(0, columns, width):
        at = slice(start, start + width)
        piece = logits_ref[:, at]
        grad = scale * (jnp.exp(listed_ref[:, at] - lse_ref) - jnp.exp(piece - lse_all))
        grad = grad.astype(jnp.bfloat16)
        out_ref[:, at] = grad
        term = term + grad.astype(jnp.float32) * piece
    lane = lax.broadcasted_iota(jnp.int32, info_ref.shape, 1)
    info_ref[...] = jnp.broadcast_to(lse_ref - lse_all, info_ref.shape)
    term = jnp.sum(term, axis=1, keepdims=True)
    high = term.astype(jnp.bfloat16).astype(jnp.float32)
    middle = (term - high).astype(jnp.bfloat16).astype(jnp.float32)
    low = term - high - middle
    term = jnp.where(lane == 0, high, jnp.where(lane == 1, middle, jnp.where(lane == 2, low, 0.0)))
    out_ref[:, columns:] = term.astype(jnp.bfloat16)


def logit_grads(part, logits, listed, stats, scale, width):
    rows, columns = logits.shape
    block = min(rows, 16)
    skip = part * (rows // block)
    return pl.pallas_call(
        functools.partial(grad_kernel, width),
        grid=(rows // block,),
        in_specs=[
            pl.BlockSpec((block, columns), lambda i: (i, 0)),
            pl.BlockSpec((block, columns), lambda i: (i, 0)),
            pl.BlockSpec((stats.shape[0], block, 128), lambda i: (0, i, 0)),
            pl.BlockSpec((block, 1), lambda i: (i + skip, 0)),
        ],
        out_specs=[
            pl.BlockSpec((block, columns + tail), lambda i: (i, 0)),
            pl.BlockSpec((block, 128), lambda i: (i, 0)),
        ],
        out_shape=[
            jax.ShapeDtypeStruct((rows, columns + tail), jnp.bfloat16),
            jax.ShapeDtypeStruct((rows, 128), jnp.float32),
        ],
        compiler_params=compiler_params(),
        cost_estimate=small_cost(),
        name="logit_grads",
    )(logits, listed, stats, scale)


def put_row(out_ref, value):
    width = value.shape[1] - tail
    code, power = encode(value[:, :width])
    term, term_power = encode(value[:, width : width + 1])
    lane = lax.broadcasted_iota(jnp.int32, (value.shape[0], tail), 1)
    beside = jnp.where(lane == 0, power, jnp.where(lane == 1, term.astype(jnp.int32).astype(jnp.float32), term_power))
    out_ref[:, :width] = code
    out_ref[:, width:] = beside.astype(jnp.int32).astype(jnp.int16)


def take_row(codes_ref):
    width = codes_ref.shape[1] - tail
    beside = codes_ref[:, width:].astype(jnp.int32).astype(jnp.float32)
    value = codes_ref[:, :width].astype(jnp.int32).astype(jnp.float32) * jnp.exp(beside[:, 0:1] * per_step)
    term = beside[:, 1:2] * jnp.exp(beside[:, 2:3] * per_step)
    return value, jnp.broadcast_to(term, beside.shape)


def back_kernel(tiles, keeps, place_ref, *refs):
    grads, terms, head_ref, outs, total_ref = refs[:5], refs[5:10], refs[10], refs[11:-1], refs[-1]
    tile = pl.program_id(0)

    @pl.when(tile == 0)
    def _():
        total_ref[...] = jnp.zeros_like(total_ref)

    grad = jnp.concatenate([g[...] for g in grads], axis=0)
    total_ref[...] += lax.dot_general(
        grad, head_ref[...], (((1,), (1,)), ((), ())), preferred_element_type=jnp.float32
    )

    @pl.when(tile == tiles - 1)
    def _():
        term = jnp.concatenate([t[...].astype(jnp.float32) for t in terms], axis=0)
        term = jnp.broadcast_to(term[:, 0:1] + term[:, 1:2] + term[:, 2:3], (term.shape[0], tail))
        width = outs[0].shape[1] - tail
        for k, out_ref in enumerate(outs):
            start = pl.multiple_of((place_ref[1] ^ k) * width, width)
            if k == 0 and keeps:
                out_ref[:, :width] = total_ref[:, pl.ds(start, width)]
                out_ref[:, width:] = term
            else:
                put_row(out_ref, jnp.concatenate([total_ref[:, pl.ds(start, width)], term], axis=1))


def back(grads, head, place, width, group, keeps):
    depth, columns = head.shape
    rows = sum(g.shape[0] for g in grads)
    blocks = max(group // 2, 1)
    part = depth // group
    types = [jnp.float32 if keeps and k == 0 else jnp.int16 for k in range(blocks)]
    across = lambda g: pl.BlockSpec((g.shape[0], width), lambda j, place: (0, j))
    beside = lambda g: pl.BlockSpec((g.shape[0], tail), lambda j, place: (0, columns // tail))
    return pl.pallas_call(
        functools.partial(back_kernel, columns // width, keeps),
        grid_spec=pltpu.PrefetchScalarGridSpec(
            num_scalar_prefetch=1,
            grid=(columns // width,),
            in_specs=[across(g) for g in grads]
            + [beside(g) for g in grads]
            + [pl.BlockSpec((blocks * part, width), lambda j, place: (place[0], j))],
            out_specs=[constant(rows, part + tail)] * blocks,
            scratch_shapes=[pltpu.VMEM((rows, blocks * part), jnp.float32)],
        ),
        out_shape=[jax.ShapeDtypeStruct((rows, part + tail), t) for t in types],
        compiler_params=compiler_params(),
        cost_estimate=small_cost(),
        name="grad_rows",
    )(place, *grads, *grads, head)


def group_kernel(place_ref, keep_ref, *refs):
    total_ref = refs[-1]
    count = place_ref.shape[0] - 1
    out_ref, sends, received = refs[-2 - count], refs[-1 - count : -1], refs[: -2 - count]
    width = keep_ref.shape[1] - tail
    total, term = keep_ref[:, :width], keep_ref[:, width:]
    for codes_ref in received:
        more, more_term = take_row(codes_ref)
        total, term = total + more, term + more_term
    total_ref[:, :width] = total
    total_ref[:, width:] = term
    rows = out_ref.shape[0]
    block = lambda b: total_ref[pl.ds(pl.multiple_of(b * rows, rows), rows), :]
    out_ref[...] = block(place_ref[0])
    for k, send_ref in enumerate(sends, 1):
        put_row(send_ref, block(place_ref[k]))


def group_sum(place, keep, received):
    blocks = place.shape[0]
    rows, width = keep.shape
    each = (rows // blocks, width)
    return pl.pallas_call(
        group_kernel,
        in_specs=[pl.BlockSpec(memory_space=pltpu.SMEM)]
        + [pl.BlockSpec(memory_space=pltpu.VMEM)] * (1 + len(received)),
        out_specs=[pl.BlockSpec(memory_space=pltpu.VMEM)] * blocks,
        out_shape=[jax.ShapeDtypeStruct(each, jnp.float32)]
        + [jax.ShapeDtypeStruct(each, jnp.int16)] * (blocks - 1),
        scratch_shapes=[pltpu.VMEM((rows, width), jnp.float32)],
        compiler_params=compiler_params(),
        cost_estimate=small_cost(),
        name="group_sum",
    )(place, keep, *received)


def last_kernel(keep_ref, *refs):
    width = keep_ref.shape[1] - tail
    total, term = keep_ref[:, :width], keep_ref[:, width:]
    for codes_ref in refs[:-1]:
        more, more_term = take_row(codes_ref)
        total, term = total + more, term + more_term
    put_row(refs[-1], jnp.concatenate([total, term], axis=1))


def last_sum(keep, received):
    return pl.pallas_call(
        last_kernel,
        in_specs=[pl.BlockSpec(memory_space=pltpu.VMEM)] * (1 + len(received)),
        out_specs=pl.BlockSpec(memory_space=pltpu.VMEM),
        out_shape=jax.ShapeDtypeStruct(keep.shape, jnp.int16),
        compiler_params=compiler_params(),
        cost_estimate=small_cost(),
        name="last_sum",
    )(keep, *received)


def after(value, *others):
    return lax.optimization_barrier((value, *others))[0]


def shards(hidden, head, gain, refusal_ids, refusal_count, loss_scale):
    row_count, model_width = hidden.shape
    depth, vocab_local = head.shape
    list_length = refusal_ids.shape[1]
    prompt_size = lax.axis_size("prompt")
    vocab_size = lax.axis_size("vocab")
    group = vocab_size // prompt_size
    width = min(1024, vocab_local // 2)
    tiles = vocab_local // width
    half = row_count // 2
    me = lax.axis_index("prompt")
    shard = lax.axis_index("vocab")
    to_x, to_y, to_far = ([(p, p ^ k) for p in range(prompt_size)] for k in (1, 2, 3))
    send = lambda value, pairs: lax.ppermute(value, "prompt", pairs)

    hidden_f = hidden.astype(jnp.float32)
    inverse_rms = lax.rsqrt(jnp.mean(hidden_f * hidden_f, axis=1, keepdims=True) + epsilon)
    normed = (hidden_f * inverse_rms * gain).astype(jnp.bfloat16)
    columns = lambda p: lax.dynamic_slice_in_dim(normed, p * depth, depth, 1)
    rows_far = send(columns(me ^ 3), to_far)
    rows_x = send(columns(me ^ 1), to_x)
    rows_y = send(columns(me ^ 2), to_y)
    own = own_logits(columns(me), head, width)
    rows_far = after(rows_far, rows_x, rows_y, own)

    by_x, by_y = [], []
    for skip in (0, tiles // 2):
        first, second = far_codes(rows_far, head, width, skip, tiles // 2)
        by_x.append(send(first, to_x))
        by_y.append(send(second, to_y))
    sums_x_a, sums_y_a = [], []
    for c, skip in enumerate((0, tiles // 2)):
        codes_x, codes_y = near_codes(
            0, rows_x, rows_y, head, [by_x[c]], [by_y[c]], width, skip, tiles // 2
        )
        sums_x_a.append(send(codes_x, to_x))
        sums_y_a.append(send(codes_y, to_y))
    rows_x = after(rows_x, codes_x, sums_x_a[0], sums_y_a[0])
    codes_x, codes_y = near_codes(1, rows_x, rows_y, head, by_x, by_y, width, 0, tiles)
    halves = ((sums_x_a, sums_y_a), ([send(codes_x, to_x)], [send(codes_y, to_y)]))

    in_list = jnp.arange(list_length)[None, :] < refusal_count[:, None]
    ids = jnp.where(in_list, refusal_ids - shard * vocab_local, -1)

    block, member = shard // group, shard % group
    spread = max(group // 2, 1)
    place_other = jnp.stack([(member // spread) ^ 1, member % spread]).astype(jnp.int32)
    place_mine = jnp.stack([member // spread, member % spread]).astype(jnp.int32)
    place_block = jnp.stack([block ^ k ^ me for k in range(prompt_size)]).astype(jnp.int32)
    to_member = [[(v, v ^ k) for v in range(vocab_size)] for k in range(1, group)]
    to_block = [
        [(v, ((v // group) ^ k) * group + v % group) for v in range(vocab_size)]
        for k in range(1, prompt_size)
    ]
    moves = []
    for p in range(prompt_size):
        for r in range(prompt_size):
            for i in range(group):
                moves.append((p * vocab_size + r * group + i, r * vocab_size + p * group + i))

    infos, grads = [], []
    for part, (sums_x, sums_y) in enumerate(halves):
        logits, listed, stats = row_stats(part, own, sums_x, sums_y, after(ids, *infos), width)
        stats = lax.all_gather(stats, "vocab", axis=0)
        grad, info = logit_grads(part, logits, listed, stats, loss_scale[:, None], width)
        infos.append(info)
        grads.append((grad, send(grad, to_x), send(grad, to_y)))
    log_refusal = jnp.concatenate([info[:, 0] for info in infos])

    quarter = half // 2
    gathered = []
    for grad, grad_x, grad_y in grads:
        far_0 = send(grad_y[:quarter], to_x)
        far_1 = send(grad_x[quarter:], to_y)
        gathered.append((grad, grad_x, grad_y, far_0, far_1))
    (_, grad_x, grad_y, far_0, far_1) = gathered[1]
    waits_other, waits_mine = [grad_x, grad_y], [far_0, far_1]
    grad_cols = []
    for parts in gathered:
        others = back(parts, head, after(place_other, *waits_other), width, group, False)
        received = [lax.ppermute(c, "vocab", to) for c, to in zip(others, to_member[spread - 1 :])]
        keep, *codes = back(parts, head, after(place_mine, *others, *waits_mine), width, group, True)
        received += [lax.ppermute(c, "vocab", to) for c, to in zip(codes, to_member)]
        keep, *codes = group_sum(place_block, keep, received)
        received = [lax.ppermute(c, "vocab", to) for c, to in zip(codes, to_block)]
        waits_other, waits_mine = [keep], received
        codes = last_sum(keep, received)
        grad_cols.append(lax.ppermute(codes, ("prompt", "vocab"), moves))

    slice_width = model_width // vocab_size
    col_start = shard * slice_width
    codes = jnp.concatenate(grad_cols)
    power = codes[:, slice_width : slice_width + 1].astype(jnp.float32)
    grad_cols = codes[:, :slice_width].astype(jnp.float32) * jnp.exp(power * per_step)
    term = codes[:, slice_width + 1 : slice_width + 3].astype(jnp.float32)
    row_term = term[:, 0] * jnp.exp(term[:, 1] * per_step)
    hidden_cols = lax.dynamic_slice_in_dim(hidden, col_start, slice_width, 1).astype(jnp.float32)
    gain_cols = lax.dynamic_slice_in_dim(gain, col_start, slice_width, 0)
    grad_hidden = (
        inverse_rms * gain_cols * grad_cols
        - hidden_cols * (inverse_rms * inverse_rms / model_width) * row_term[:, None]
    )
    return (grad_hidden, log_refusal)


def solution(mesh):
    return jax.shard_map(
        shards,
        mesh=mesh,
        in_specs=(
            P("prompt", None),
            P("prompt", "vocab"),
            P(),
            P("prompt", None),
            P("prompt"),
            P("prompt"),
        ),
        out_specs=(P("prompt", "vocab"), P("prompt")),
        check_vma=False,
    )
```

```python
import functools
import math

import jax
import jax.numpy as jnp
from jax import lax
from jax.experimental import pallas as pl
from jax.experimental.pallas import tpu as pltpu
from jax.sharding import PartitionSpec as P

epsilon = 1e-05
lowest = -1e30
tail = 128
steps = 64
code_top = 32000.0
per_step = math.log(2.0) / steps
megabyte = 1024 * 1024


def encode(value):
    top = jnp.max(jnp.abs(value), axis=1, keepdims=True)
    power = jnp.ceil(jnp.log(jnp.maximum(top, 1e-30) * (1.0 / code_top)) * (1.0 / per_step))
    code = jnp.round(value * jnp.exp(power * -per_step))
    return code.astype(jnp.int32).astype(jnp.int16), power


def decode(codes_ref, tile, width, vocab_local, rows=slice(None)):
    powers = codes_ref[rows, vocab_local : vocab_local + tail].astype(jnp.int32).astype(jnp.float32)
    lane = lax.broadcasted_iota(jnp.int32, powers.shape, 1)
    power = jnp.sum(jnp.where(lane == tile, powers, 0.0), axis=1, keepdims=True)
    start = tile * width
    if not isinstance(start, int):
        start = pl.multiple_of(start, width)
    codes = codes_ref[rows, pl.ds(start, width)].astype(jnp.int32).astype(jnp.float32)
    return codes * jnp.exp(power * per_step)


def put(out_ref, powers_ref, rows, tile, width, vocab_local, value):
    code, power = encode(value)
    out_ref[:, pl.ds(pl.multiple_of(tile * width, width), width)] = code
    lane = lax.broadcasted_iota(jnp.int32, (value.shape[0], tail), 1)
    powers = jnp.where(lane >= tile, power, powers_ref[rows, :])
    powers_ref[rows, :] = powers
    out_ref[:, vocab_local:] = powers.astype(jnp.int32).astype(jnp.int16)


def dot(a, b):
    return jnp.dot(a, b, preferred_element_type=jnp.float32)


def compiler_params():
    return pltpu.CompilerParams(vmem_limit_bytes=28 * megabyte)


def small_cost():
    return pl.CostEstimate(flops=1024, bytes_accessed=1024, transcendentals=0)


streams = 4


def head_specs(depth, width, skip=0):
    block = (depth // streams, width)
    return [pl.BlockSpec(block, lambda j, q=q: (q, j + skip)) for q in range(streams)]


def dot_head(x, head_refs):
    each = x.shape[1] // len(head_refs)
    return functools.reduce(
        jnp.add, [dot(x[:, q * each : (q + 1) * each], ref[...]) for q, ref in enumerate(head_refs)]
    )


def constant(*shape):
    return pl.BlockSpec(shape, lambda *_: (0,) * len(shape))


def far_kernel(width, x_ref, *refs):
    head_refs, (first_ref, second_ref, powers_ref) = refs[:streams], refs[streams:]
    tile = pl.program_id(0)
    columns = first_ref.shape[1] - tail
    value = dot_head(x_ref, head_refs)
    q = value.shape[0] // 4
    first = jnp.concatenate([value[:q], value[2 * q : 3 * q]], axis=0)
    second = jnp.concatenate([value[q : 2 * q], value[3 * q :]], axis=0)
    put(first_ref, powers_ref, slice(0, 2 * q), tile, width, columns, first)
    put(second_ref, powers_ref, slice(2 * q, 4 * q), tile, width, columns, second)


def far_codes(rows_in, head, width, skip, tiles):
    rows, depth = rows_in.shape
    columns = tiles * width
    return pl.pallas_call(
        functools.partial(far_kernel, width),
        grid=(tiles,),
        in_specs=[constant(rows, depth)] + head_specs(depth, width, skip),
        out_specs=[constant(rows // 2, columns + tail)] * 2,
        out_shape=[jax.ShapeDtypeStruct((rows // 2, columns + tail), jnp.int16)] * 2,
        scratch_shapes=[pltpu.VMEM((rows, tail), jnp.float32)],
        compiler_params=compiler_params(),
        cost_estimate=small_cost(),
        name="far_codes",
    )(rows_in, *[head] * streams)


def decode_any(refs, tile, width):
    columns = refs[0].shape[1] - tail
    if len(refs) == 1:
        return decode(refs[0], tile, width, columns)
    each = columns // width
    if isinstance(tile, int):
        return decode(refs[tile // each], tile % each, width, columns)
    low = decode(refs[0], jnp.minimum(tile, each - 1), width, columns)
    high = decode(refs[1], jnp.maximum(tile - each, 0), width, columns)
    return jnp.where(tile < each, low, high)


def near_kernel(width, parts, x_ref, y_ref, *refs):
    head_refs, refs = refs[:streams], refs[streams:]
    by_x_refs, by_y_refs = refs[:parts], refs[parts : 2 * parts]
    to_x_ref, to_y_ref, powers_ref = refs[2 * parts :]
    tile = pl.program_id(0)
    rows = x_ref.shape[0]
    half = rows // 2
    columns = to_x_ref.shape[1] - tail
    value = dot_head(jnp.concatenate([x_ref[...], y_ref[...]], axis=0), head_refs)
    more_x = decode_any(by_y_refs, tile, width)
    more_y = decode_any(by_x_refs, tile, width)
    for_x = jnp.concatenate([value[:half], value[half:rows] + more_x], axis=0)
    for_y = jnp.concatenate([value[rows : rows + half] + more_y, value[rows + half :]], axis=0)
    put(to_x_ref, powers_ref, slice(0, rows), tile, width, columns, for_x)
    put(to_y_ref, powers_ref, slice(rows, 2 * rows), tile, width, columns, for_y)


def near_codes(part, rows_x, rows_y, head, by_x, by_y, width, skip, tiles):
    depth = rows_x.shape[1]
    rows = rows_x.shape[0] // 2
    columns = tiles * width
    received = pl.BlockSpec((rows // 2, by_x[0].shape[1]), lambda j: (part, 0))
    return pl.pallas_call(
        functools.partial(near_kernel, width, len(by_x)),
        grid=(tiles,),
        in_specs=[pl.BlockSpec((rows, depth), lambda j: (part, 0))] * 2
        + head_specs(depth, width, skip)
        + [received] * (2 * len(by_x)),
        out_specs=[constant(rows, columns + tail)] * 2,
        out_shape=[jax.ShapeDtypeStruct((rows, columns + tail), jnp.int16)] * 2,
        scratch_shapes=[pltpu.VMEM((2 * rows, tail), jnp.float32)],
        compiler_params=compiler_params(),
        cost_estimate=small_cost(),
        name="near_codes",
    )(rows_x, rows_y, *[head] * streams, *by_x, *by_y)


def own_kernel(x_ref, *refs):
    refs[-1][...] = dot_head(x_ref, refs[:-1])


def own_logits(rows_in, head, width):
    rows, depth = rows_in.shape
    columns = head.shape[1]
    return pl.pallas_call(
        own_kernel,
        grid=(columns // width,),
        in_specs=[constant(rows, depth)] + head_specs(depth, width),
        out_specs=pl.BlockSpec((rows, width), lambda j: (0, j)),
        out_shape=jax.ShapeDtypeStruct((rows, columns), jnp.float32),
        compiler_params=compiler_params(),
        cost_estimate=small_cost(),
        name="own_logits",
    )(rows_in, *[head] * streams)


def members(ids, start, width):
    rows = ids.shape[0]
    column = lax.broadcasted_iota(jnp.int32, (rows, width), 1) + start
    found = column == ids[:, 0:1]
    for k in range(1, ids.shape[1]):
        found = found | (column == ids[:, k : k + 1])
    return found


def stats_kernel(width, parts, *refs):
    own_ref, by_x_refs, by_y_refs = refs[0], refs[1 : 1 + parts], refs[1 + parts : 1 + 2 * parts]
    ids_ref, logits_ref, listed_ref, out_ref = refs[1 + 2 * parts :]
    rows, columns = logits_ref.shape
    ids = ids_ref[...]
    top_all = jnp.full((rows, width), lowest, jnp.float32)
    top_ref = jnp.full((rows, width), lowest, jnp.float32)
    for start in range(0, columns, width):
        at = slice(start, start + width)
        piece = own_ref[:, at] + decode_any(by_x_refs, start // width, width)
        piece = piece + decode_any(by_y_refs, start // width, width)
        listed = jnp.where(members(ids, start, width), piece, lowest)
        logits_ref[:, at] = piece
        listed_ref[:, at] = listed
        top_all = jnp.maximum(top_all, piece)
        top_ref = jnp.maximum(top_ref, listed)
    peak_all = jnp.max(top_all, axis=1, keepdims=True)
    peak_ref = jnp.max(top_ref, axis=1, keepdims=True)
    sum_all = jnp.zeros((rows, width), jnp.float32)
    sum_ref = jnp.zeros((rows, width), jnp.float32)
    for start in range(0, columns, width):
        at = slice(start, start + width)
        sum_all = sum_all + jnp.exp(logits_ref[:, at] - peak_all)
        sum_ref = sum_ref + jnp.exp(listed_ref[:, at] - peak_ref)
    sum_all = jnp.sum(sum_all, axis=1, keepdims=True)
    sum_ref = jnp.sum(sum_ref, axis=1, keepdims=True)
    lane = lax.broadcasted_iota(jnp.int32, out_ref.shape, 1)
    out_ref[...] = jnp.where(
        lane == 0, peak_all, jnp.where(lane == 1, peak_ref, jnp.where(lane == 2, sum_all, sum_ref))
    )


def row_stats(part, own, by_x, by_y, ids, width):
    rows = by_x[0].shape[0]
    parts = len(by_x)
    columns = own.shape[1]
    block = min(rows, 16)
    skip = part * (rows // block)
    across = lambda array: pl.BlockSpec((block, array.shape[1]), lambda i: (i, 0))
    return pl.pallas_call(
        functools.partial(stats_kernel, width, parts),
        grid=(rows // block,),
        in_specs=[pl.BlockSpec((block, columns), lambda i: (i + skip, 0))]
        + [across(a) for a in (*by_x, *by_y)]
        + [pl.BlockSpec((block, ids.shape[1]), lambda i: (i + skip, 0))],
        out_specs=[
            pl.BlockSpec((block, columns), lambda i: (i, 0)),
            pl.BlockSpec((block, columns), lambda i: (i, 0)),
            pl.BlockSpec((block, 128), lambda i: (i, 0)),
        ],
        out_shape=[
            jax.ShapeDtypeStruct((rows, columns), jnp.float32),
            jax.ShapeDtypeStruct((rows, columns), jnp.float32),
            jax.ShapeDtypeStruct((rows, 128), jnp.float32),
        ],
        compiler_params=compiler_params(),
        cost_estimate=small_cost(),
        name="row_stats",
    )(own, *by_x, *by_y, ids)


def grad_kernel(width, logits_ref, listed_ref, stats_ref, scale_ref, out_ref, info_ref):
    rows, columns = logits_ref.shape
    stats = [stats_ref[v] for v in range(stats_ref.shape[0])]
    peaks = functools.reduce(jnp.maximum, [s[:, :2] for s in stats])
    sums = functools.reduce(jnp.add, [s[:, 2:4] * jnp.exp(s[:, :2] - peaks) for s in stats])
    lse = peaks + jnp.log(sums)
    lse_all, lse_ref = lse[:, 0:1], lse[:, 1:2]
    scale = scale_ref[...]
    term = jnp.zeros((rows, width), jnp.float32)
    for start in range(0, columns, width):
        at = slice(start, start + width)
        piece = logits_ref[:, at]
        grad = scale * (jnp.exp(listed_ref[:, at] - lse_ref) - jnp.exp(piece - lse_all))
        grad = grad.astype(jnp.bfloat16)
        out_ref[:, at] = grad
        term = term + grad.astype(jnp.float32) * piece
    lane = lax.broadcasted_iota(jnp.int32, info_ref.shape, 1)
    info_ref[...] = jnp.broadcast_to(lse_ref - lse_all, info_ref.shape)
    term = jnp.sum(term, axis=1, keepdims=True)
    high = term.astype(jnp.bfloat16).astype(jnp.float32)
    middle = (term - high).astype(jnp.bfloat16).astype(jnp.float32)
    low = term - high - middle
    term = jnp.where(lane == 0, high, jnp.where(lane == 1, middle, jnp.where(lane == 2, low, 0.0)))
    out_ref[:, columns:] = term.astype(jnp.bfloat16)


def logit_grads(part, logits, listed, stats, scale, width):
    rows, columns = logits.shape
    block = min(rows, 16)
    skip = part * (rows // block)
    return pl.pallas_call(
        functools.partial(grad_kernel, width),
        grid=(rows // block,),
        in_specs=[
            pl.BlockSpec((block, columns), lambda i: (i, 0)),
            pl.BlockSpec((block, columns), lambda i: (i, 0)),
            pl.BlockSpec((stats.shape[0], block, 128), lambda i: (0, i, 0)),
            pl.BlockSpec((block, 1), lambda i: (i + skip, 0)),
        ],
        out_specs=[
            pl.BlockSpec((block, columns + tail), lambda i: (i, 0)),
            pl.BlockSpec((block, 128), lambda i: (i, 0)),
        ],
        out_shape=[
            jax.ShapeDtypeStruct((rows, columns + tail), jnp.bfloat16),
            jax.ShapeDtypeStruct((rows, 128), jnp.float32),
        ],
        compiler_params=compiler_params(),
        cost_estimate=small_cost(),
        name="logit_grads",
    )(logits, listed, stats, scale)


def put_row(out_ref, value):
    width = value.shape[1] - tail
    code, power = encode(value[:, :width])
    term, term_power = encode(value[:, width : width + 1])
    lane = lax.broadcasted_iota(jnp.int32, (value.shape[0], tail), 1)
    beside = jnp.where(lane == 0, power, jnp.where(lane == 1, term.astype(jnp.int32).astype(jnp.float32), term_power))
    out_ref[:, :width] = code
    out_ref[:, width:] = beside.astype(jnp.int32).astype(jnp.int16)


def take_row(codes_ref):
    width = codes_ref.shape[1] - tail
    beside = codes_ref[:, width:].astype(jnp.int32).astype(jnp.float32)
    value = codes_ref[:, :width].astype(jnp.int32).astype(jnp.float32) * jnp.exp(beside[:, 0:1] * per_step)
    term = beside[:, 1:2] * jnp.exp(beside[:, 2:3] * per_step)
    return value, jnp.broadcast_to(term, beside.shape)


def back_kernel(tiles, keeps, place_ref, *refs):
    grads, terms, refs = refs[:5], refs[5:10], refs[10:]
    head_refs, outs, total_ref = refs[:streams], refs[streams:-1], refs[-1]
    tile = pl.program_id(0)

    @pl.when(tile == 0)
    def _():
        total_ref[...] = jnp.zeros_like(total_ref)

    grad = jnp.concatenate([g[...] for g in grads], axis=0).T
    each = total_ref.shape[0] // streams
    for q, head_ref in enumerate(head_refs):
        total_ref[q * each : (q + 1) * each, :] += dot(head_ref[...], grad)

    @pl.when(tile == tiles - 1)
    def _():
        term = jnp.concatenate([t[...].astype(jnp.float32) for t in terms], axis=0)
        term = jnp.broadcast_to(term[:, 0:1] + term[:, 1:2] + term[:, 2:3], (term.shape[0], tail))
        width = outs[0].shape[1] - tail
        for k, out_ref in enumerate(outs):
            start = pl.multiple_of((place_ref[1] ^ k) * width, width)
            value = total_ref[pl.ds(start, width), :].T
            if k == 0 and keeps:
                out_ref[:, :width] = value
                out_ref[:, width:] = term
            else:
                put_row(out_ref, jnp.concatenate([value, term], axis=1))


def back(grads, head, place, width, group, keeps):
    depth, columns = head.shape
    rows = sum(g.shape[0] for g in grads)
    blocks = max(group // 2, 1)
    part = depth // group
    types = [jnp.float32 if keeps and k == 0 else jnp.int16 for k in range(blocks)]
    across = lambda g: pl.BlockSpec((g.shape[0], width), lambda j, place: (0, j))
    beside = lambda g: pl.BlockSpec((g.shape[0], tail), lambda j, place: (0, columns // tail))
    block = (blocks * part // streams, width)
    return pl.pallas_call(
        functools.partial(back_kernel, columns // width, keeps),
        grid_spec=pltpu.PrefetchScalarGridSpec(
            num_scalar_prefetch=1,
            grid=(columns // width,),
            in_specs=[across(g) for g in grads]
            + [beside(g) for g in grads]
            + [pl.BlockSpec(block, lambda j, place, q=q: (place[0] * streams + q, j)) for q in range(streams)],
            out_specs=[constant(rows, part + tail)] * blocks,
            scratch_shapes=[pltpu.VMEM((blocks * part, rows), jnp.float32)],
        ),
        out_shape=[jax.ShapeDtypeStruct((rows, part + tail), t) for t in types],
        compiler_params=compiler_params(),
        cost_estimate=small_cost(),
        name="grad_rows",
    )(place, *grads, *grads, *[head] * streams)


def group_kernel(place_ref, keep_ref, *refs):
    total_ref = refs[-1]
    count = place_ref.shape[0] - 1
    out_ref, sends, received = refs[-2 - count], refs[-1 - count : -1], refs[: -2 - count]
    width = keep_ref.shape[1] - tail
    total, term = keep_ref[:, :width], keep_ref[:, width:]
    for codes_ref in received:
        more, more_term = take_row(codes_ref)
        total, term = total + more, term + more_term
    total_ref[:, :width] = total
    total_ref[:, width:] = term
    rows = out_ref.shape[0]
    block = lambda b: total_ref[pl.ds(pl.multiple_of(b * rows, rows), rows), :]
    out_ref[...] = block(place_ref[0])
    for k, send_ref in enumerate(sends, 1):
        put_row(send_ref, block(place_ref[k]))


def group_sum(place, keep, received):
    blocks = place.shape[0]
    rows, width = keep.shape
    each = (rows // blocks, width)
    return pl.pallas_call(
        group_kernel,
        in_specs=[pl.BlockSpec(memory_space=pltpu.SMEM)]
        + [pl.BlockSpec(memory_space=pltpu.VMEM)] * (1 + len(received)),
        out_specs=[pl.BlockSpec(memory_space=pltpu.VMEM)] * blocks,
        out_shape=[jax.ShapeDtypeStruct(each, jnp.float32)]
        + [jax.ShapeDtypeStruct(each, jnp.int16)] * (blocks - 1),
        scratch_shapes=[pltpu.VMEM((rows, width), jnp.float32)],
        compiler_params=compiler_params(),
        cost_estimate=small_cost(),
        name="group_sum",
    )(place, keep, *received)


def last_kernel(keep_ref, *refs):
    width = keep_ref.shape[1] - tail
    total, term = keep_ref[:, :width], keep_ref[:, width:]
    for codes_ref in refs[:-1]:
        more, more_term = take_row(codes_ref)
        total, term = total + more, term + more_term
    put_row(refs[-1], jnp.concatenate([total, term], axis=1))


def last_sum(keep, received):
    return pl.pallas_call(
        last_kernel,
        in_specs=[pl.BlockSpec(memory_space=pltpu.VMEM)] * (1 + len(received)),
        out_specs=pl.BlockSpec(memory_space=pltpu.VMEM),
        out_shape=jax.ShapeDtypeStruct(keep.shape, jnp.int16),
        compiler_params=compiler_params(),
        cost_estimate=small_cost(),
        name="last_sum",
    )(keep, *received)


def after(value, *others):
    return lax.optimization_barrier((value, *others))[0]


def shards(hidden, head, gain, refusal_ids, refusal_count, loss_scale):
    row_count, model_width = hidden.shape
    depth, vocab_local = head.shape
    list_length = refusal_ids.shape[1]
    prompt_size = lax.axis_size("prompt")
    vocab_size = lax.axis_size("vocab")
    group = vocab_size // prompt_size
    width = min(1024, vocab_local // 2)
    tiles = vocab_local // width
    half = row_count // 2
    me = lax.axis_index("prompt")
    shard = lax.axis_index("vocab")
    to_x, to_y, to_far = ([(p, p ^ k) for p in range(prompt_size)] for k in (1, 2, 3))
    send = lambda value, pairs: lax.ppermute(value, "prompt", pairs)

    hidden_f = hidden.astype(jnp.float32)
    inverse_rms = lax.rsqrt(jnp.mean(hidden_f * hidden_f, axis=1, keepdims=True) + epsilon)
    normed = (hidden_f * inverse_rms * gain).astype(jnp.bfloat16)
    columns = lambda p: lax.dynamic_slice_in_dim(normed, p * depth, depth, 1)
    rows_far = send(columns(me ^ 3), to_far)
    rows_x = send(columns(me ^ 1), to_x)
    rows_y = send(columns(me ^ 2), to_y)
    own = own_logits(columns(me), head, width)
    rows_far = after(rows_far, rows_x, rows_y, own)

    by_x, by_y = [], []
    for skip in (0, tiles // 2):
        first, second = far_codes(rows_far, head, width, skip, tiles // 2)
        by_x.append(send(first, to_x))
        by_y.append(send(second, to_y))
    sums_x_a, sums_y_a = [], []
    for c, skip in enumerate((0, tiles // 2)):
        codes_x, codes_y = near_codes(
            0, rows_x, rows_y, head, [by_x[c]], [by_y[c]], width, skip, tiles // 2
        )
        sums_x_a.append(send(codes_x, to_x))
        sums_y_a.append(send(codes_y, to_y))
    rows_x = after(rows_x, codes_x, sums_x_a[0], sums_y_a[0])
    codes_x, codes_y = near_codes(1, rows_x, rows_y, head, by_x, by_y, width, 0, tiles)
    halves = ((sums_x_a, sums_y_a), ([send(codes_x, to_x)], [send(codes_y, to_y)]))

    in_list = jnp.arange(list_length)[None, :] < refusal_count[:, None]
    ids = jnp.where(in_list, refusal_ids - shard * vocab_local, -1)

    block, member = shard // group, shard % group
    spread = max(group // 2, 1)
    place_other = jnp.stack([(member // spread) ^ 1, member % spread]).astype(jnp.int32)
    place_mine = jnp.stack([member // spread, member % spread]).astype(jnp.int32)
    place_block = jnp.stack([block ^ k ^ me for k in range(prompt_size)]).astype(jnp.int32)
    to_member = [[(v, v ^ k) for v in range(vocab_size)] for k in range(1, group)]
    to_block = [
        [(v, ((v // group) ^ k) * group + v % group) for v in range(vocab_size)]
        for k in range(1, prompt_size)
    ]
    moves = []
    for p in range(prompt_size):
        for r in range(prompt_size):
            for i in range(group):
                moves.append((p * vocab_size + r * group + i, r * vocab_size + p * group + i))

    quarter = half // 2
    infos, grads = [], []
    for part, (sums_x, sums_y) in enumerate(halves):
        logits, listed, stats = row_stats(part, own, sums_x, sums_y, after(ids, *infos), width)
        stats = lax.all_gather(stats, "vocab", axis=0)
        grad, info = logit_grads(part, logits, listed, stats, loss_scale[:, None], width)
        infos.append(info)
        grads.append(grad)
    log_refusal = jnp.concatenate([info[:, 0] for info in infos])

    gathering, waits_other, waits_mine, grad_cols = [], [], [], []
    waits_send = [infos[-1]]
    for grad in grads:
        sent = after(grad, *gathering)
        grad_x, grad_y = send(sent, to_x), send(sent, to_y)
        passed_x, passed_y = after(grad_y, *waits_send)[:quarter], after(grad_x, *waits_send)[quarter:]
        gathering = [send(passed_x, to_x), send(passed_y, to_y)]
        parts = (grad, grad_x, grad_y, *gathering)
        others = back(parts, head, after(place_other, *waits_other), width, group, False)
        received = [lax.ppermute(c, "vocab", to) for c, to in zip(others, to_member[spread - 1 :])]
        keep, *codes = back(parts, head, after(place_mine, *others, *waits_mine), width, group, True)
        received += [lax.ppermute(c, "vocab", to) for c, to in zip(codes, to_member)]
        waits_send = [keep]
        keep, *codes = group_sum(place_block, keep, received)
        received = [lax.ppermute(c, "vocab", to) for c, to in zip(codes, to_block)]
        codes = last_sum(keep, received)
        waits_other, waits_mine = received, [codes]
        grad_cols.append(lax.ppermute(codes, ("prompt", "vocab"), moves))

    slice_width = model_width // vocab_size
    col_start = shard * slice_width
    codes = jnp.concatenate(grad_cols)
    power = codes[:, slice_width : slice_width + 1].astype(jnp.float32)
    grad_cols = codes[:, :slice_width].astype(jnp.float32) * jnp.exp(power * per_step)
    term = codes[:, slice_width + 1 : slice_width + 3].astype(jnp.float32)
    row_term = term[:, 0] * jnp.exp(term[:, 1] * per_step)
    hidden_cols = lax.dynamic_slice_in_dim(hidden, col_start, slice_width, 1).astype(jnp.float32)
    gain_cols = lax.dynamic_slice_in_dim(gain, col_start, slice_width, 0)
    grad_hidden = (
        inverse_rms * gain_cols * grad_cols
        - hidden_cols * (inverse_rms * inverse_rms / model_width) * row_term[:, None]
    )
    return (grad_hidden, log_refusal)


def solution(mesh):
    return jax.shard_map(
        shards,
        mesh=mesh,
        in_specs=(
            P("prompt", None),
            P("prompt", "vocab"),
            P(),
            P("prompt", None),
            P("prompt"),
            P("prompt"),
        ),
        out_specs=(P("prompt", "vocab"), P("prompt")),
        check_vma=False,
    )
```

```python
import functools
import math

import jax
import jax.numpy as jnp
from jax import lax
from jax.experimental import pallas as pl
from jax.experimental.pallas import tpu as pltpu
from jax.sharding import PartitionSpec as P

epsilon = 1e-05
lowest = -1e30
tail = 128
steps = 64
code_top = 32000.0
per_step = math.log(2.0) / steps
megabyte = 1024 * 1024


def encode(value):
    top = jnp.max(jnp.abs(value), axis=1, keepdims=True)
    power = jnp.ceil(jnp.log(jnp.maximum(top, 1e-30) * (1.0 / code_top)) * (1.0 / per_step))
    code = jnp.round(value * jnp.exp(power * -per_step))
    return code.astype(jnp.int32).astype(jnp.int16), power


def decode(codes_ref, tile, width, vocab_local, rows=slice(None)):
    powers = codes_ref[rows, vocab_local : vocab_local + tail].astype(jnp.int32).astype(jnp.float32)
    lane = lax.broadcasted_iota(jnp.int32, powers.shape, 1)
    power = jnp.sum(jnp.where(lane == tile, powers, 0.0), axis=1, keepdims=True)
    start = tile * width
    if not isinstance(start, int):
        start = pl.multiple_of(start, width)
    codes = codes_ref[rows, pl.ds(start, width)].astype(jnp.int32).astype(jnp.float32)
    return codes * jnp.exp(power * per_step)


def put(out_ref, powers_ref, rows, tile, width, vocab_local, value):
    code, power = encode(value)
    out_ref[:, pl.ds(pl.multiple_of(tile * width, width), width)] = code
    lane = lax.broadcasted_iota(jnp.int32, (value.shape[0], tail), 1)
    powers = jnp.where(lane >= tile, power, powers_ref[rows, :])
    powers_ref[rows, :] = powers
    out_ref[:, vocab_local:] = powers.astype(jnp.int32).astype(jnp.int16)


def dot(a, b):
    return jnp.dot(a, b, preferred_element_type=jnp.float32)


def compiler_params():
    return pltpu.CompilerParams(vmem_limit_bytes=28 * megabyte)


def small_cost():
    return pl.CostEstimate(flops=1024, bytes_accessed=1024, transcendentals=0)


def constant(*shape):
    return pl.BlockSpec(shape, lambda *_: (0,) * len(shape))


def far_kernel(width, x_ref, head_ref, first_ref, second_ref, powers_ref):
    tile = pl.program_id(0)
    columns = first_ref.shape[1] - tail
    value = dot(x_ref[...], head_ref[...])
    q = value.shape[0] // 4
    first = jnp.concatenate([value[:q], value[2 * q : 3 * q]], axis=0)
    second = jnp.concatenate([value[q : 2 * q], value[3 * q :]], axis=0)
    put(first_ref, powers_ref, slice(0, 2 * q), tile, width, columns, first)
    put(second_ref, powers_ref, slice(2 * q, 4 * q), tile, width, columns, second)


def far_codes(rows_in, head, width, skip, tiles):
    rows, depth = rows_in.shape
    columns = tiles * width
    return pl.pallas_call(
        functools.partial(far_kernel, width),
        grid=(tiles,),
        in_specs=[
            constant(rows, depth),
            pl.BlockSpec((depth, width), lambda j: (0, j + skip)),
        ],
        out_specs=[constant(rows // 2, columns + tail)] * 2,
        out_shape=[jax.ShapeDtypeStruct((rows // 2, columns + tail), jnp.int16)] * 2,
        scratch_shapes=[pltpu.VMEM((rows, tail), jnp.float32)],
        compiler_params=compiler_params(),
        cost_estimate=small_cost(),
        name="far_codes",
    )(rows_in, head)


def near_kernel(width, x_ref, y_ref, head_ref, by_x_ref, by_y_ref, to_x_ref, to_y_ref, powers_ref):
    tile = pl.program_id(0)
    rows = x_ref.shape[0]
    half = rows // 2
    columns = to_x_ref.shape[1] - tail
    value = dot(jnp.concatenate([x_ref[...], y_ref[...]], axis=0), head_ref[...])
    more_x = decode(by_y_ref, tile, width, columns)
    more_y = decode(by_x_ref, tile, width, columns)
    for_x = jnp.concatenate([value[:half], value[half:rows] + more_x], axis=0)
    for_y = jnp.concatenate([value[rows : rows + half] + more_y, value[rows + half :]], axis=0)
    put(to_x_ref, powers_ref, slice(0, rows), tile, width, columns, for_x)
    put(to_y_ref, powers_ref, slice(rows, 2 * rows), tile, width, columns, for_y)


def near_codes(part, rows_x, rows_y, head, by_x, by_y, width, skip, tiles):
    depth = head.shape[0]
    rows = rows_x.shape[0] // 2
    columns = tiles * width
    return pl.pallas_call(
        functools.partial(near_kernel, width),
        grid=(tiles,),
        in_specs=[pl.BlockSpec((rows, depth), lambda j: (part, 0))] * 2
        + [pl.BlockSpec((depth, width), lambda j: (0, j + skip))]
        + [pl.BlockSpec((rows // 2, columns + tail), lambda j: (part, 0))] * 2,
        out_specs=[constant(rows, columns + tail)] * 2,
        out_shape=[jax.ShapeDtypeStruct((rows, columns + tail), jnp.int16)] * 2,
        scratch_shapes=[pltpu.VMEM((2 * rows, tail), jnp.float32)],
        compiler_params=compiler_params(),
        cost_estimate=small_cost(),
        name="near_codes",
    )(rows_x, rows_y, head, by_x, by_y)


def own_kernel(x_ref, head_ref, out_ref):
    out_ref[...] = dot(x_ref[...], head_ref[...])


def own_logits(rows_in, head, width):
    rows, depth = rows_in.shape
    columns = head.shape[1]
    return pl.pallas_call(
        own_kernel,
        grid=(columns // width,),
        in_specs=[
            constant(rows, depth),
            pl.BlockSpec((depth, width), lambda j: (0, j)),
        ],
        out_specs=pl.BlockSpec((rows, width), lambda j: (0, j)),
        out_shape=jax.ShapeDtypeStruct((rows, columns), jnp.float32),
        compiler_params=compiler_params(),
        cost_estimate=small_cost(),
        name="own_logits",
    )(rows_in, head)


def members(ids, start, width):
    rows = ids.shape[0]
    column = lax.broadcasted_iota(jnp.int32, (rows, width), 1) + start
    found = column == ids[:, 0:1]
    for k in range(1, ids.shape[1]):
        found = found | (column == ids[:, k : k + 1])
    return found


def stats_kernel(width, parts, *refs):
    own_ref, by_x_refs, by_y_refs = refs[0], refs[1 : 1 + parts], refs[1 + parts : 1 + 2 * parts]
    ids_ref, logits_ref, listed_ref, out_ref = refs[1 + 2 * parts :]
    rows, columns = logits_ref.shape
    each = columns // parts
    ids = ids_ref[...]
    top_all = jnp.full((rows, width), lowest, jnp.float32)
    top_ref = jnp.full((rows, width), lowest, jnp.float32)
    for start in range(0, columns, width):
        at = slice(start, start + width)
        where, inner = start // each, start % each // width
        piece = own_ref[:, at] + decode(by_x_refs[where], inner, width, each)
        piece = piece + decode(by_y_refs[where], inner, width, each)
        listed = jnp.where(members(ids, start, width), piece, lowest)
        logits_ref[:, at] = piece
        listed_ref[:, at] = listed
        top_all = jnp.maximum(top_all, piece)
        top_ref = jnp.maximum(top_ref, listed)
    peak_all = jnp.max(top_all, axis=1, keepdims=True)
    peak_ref = jnp.max(top_ref, axis=1, keepdims=True)
    sum_all = jnp.zeros((rows, width), jnp.float32)
    sum_ref = jnp.zeros((rows, width), jnp.float32)
    for start in range(0, columns, width):
        at = slice(start, start + width)
        sum_all = sum_all + jnp.exp(logits_ref[:, at] - peak_all)
        sum_ref = sum_ref + jnp.exp(listed_ref[:, at] - peak_ref)
    sum_all = jnp.sum(sum_all, axis=1, keepdims=True)
    sum_ref = jnp.sum(sum_ref, axis=1, keepdims=True)
    lane = lax.broadcasted_iota(jnp.int32, out_ref.shape, 1)
    out_ref[...] = jnp.where(
        lane == 0, peak_all, jnp.where(lane == 1, peak_ref, jnp.where(lane == 2, sum_all, sum_ref))
    )


def row_stats(part, own, by_x, by_y, ids, width):
    rows = by_x[0].shape[0]
    parts = len(by_x)
    columns = own.shape[1]
    block = min(rows, 16)
    skip = part * (rows // block)
    across = lambda array: pl.BlockSpec((block, array.shape[1]), lambda i: (i, 0))
    return pl.pallas_call(
        functools.partial(stats_kernel, width, parts),
        grid=(rows // block,),
        in_specs=[pl.BlockSpec((block, columns), lambda i: (i + skip, 0))]
        + [across(a) for a in (*by_x, *by_y)]
        + [pl.BlockSpec((block, ids.shape[1]), lambda i: (i + skip, 0))],
        out_specs=[
            pl.BlockSpec((block, columns), lambda i: (i, 0)),
            pl.BlockSpec((block, columns), lambda i: (i, 0)),
            pl.BlockSpec((block, 128), lambda i: (i, 0)),
        ],
        out_shape=[
            jax.ShapeDtypeStruct((rows, columns), jnp.float32),
            jax.ShapeDtypeStruct((rows, columns), jnp.float32),
            jax.ShapeDtypeStruct((rows, 128), jnp.float32),
        ],
        compiler_params=compiler_params(),
        cost_estimate=small_cost(),
        name="row_stats",
    )(own, *by_x, *by_y, ids)


def grad_kernel(width, logits_ref, listed_ref, stats_ref, scale_ref, out_ref, info_ref):
    rows, columns = logits_ref.shape
    stats = [stats_ref[v] for v in range(stats_ref.shape[0])]
    peaks = functools.reduce(jnp.maximum, [s[:, :2] for s in stats])
    sums = functools.reduce(jnp.add, [s[:, 2:4] * jnp.exp(s[:, :2] - peaks) for s in stats])
    lse = peaks + jnp.log(sums)
    lse_all, lse_ref = lse[:, 0:1], lse[:, 1:2]
    scale = scale_ref[...]
    term = jnp.zeros((rows, width), jnp.float32)
    for start in range(0, columns, width):
        at = slice(start, start + width)
        piece = logits_ref[:, at]
        grad = scale * (jnp.exp(listed_ref[:, at] - lse_ref) - jnp.exp(piece - lse_all))
        grad = grad.astype(jnp.bfloat16)
        out_ref[:, at] = grad
        term = term + grad.astype(jnp.float32) * piece
    lane = lax.broadcasted_iota(jnp.int32, info_ref.shape, 1)
    info_ref[...] = jnp.broadcast_to(lse_ref - lse_all, info_ref.shape)
    term = jnp.sum(term, axis=1, keepdims=True)
    high = term.astype(jnp.bfloat16).astype(jnp.float32)
    middle = (term - high).astype(jnp.bfloat16).astype(jnp.float32)
    low = term - high - middle
    term = jnp.where(lane == 0, high, jnp.where(lane == 1, middle, jnp.where(lane == 2, low, 0.0)))
    out_ref[:, columns:] = term.astype(jnp.bfloat16)


def logit_grads(part, logits, listed, stats, scale, width):
    rows, columns = logits.shape
    block = min(rows, 16)
    skip = part * (rows // block)
    return pl.pallas_call(
        functools.partial(grad_kernel, width),
        grid=(rows // block,),
        in_specs=[
            pl.BlockSpec((block, columns), lambda i: (i, 0)),
            pl.BlockSpec((block, columns), lambda i: (i, 0)),
            pl.BlockSpec((stats.shape[0], block, 128), lambda i: (0, i, 0)),
            pl.BlockSpec((block, 1), lambda i: (i + skip, 0)),
        ],
        out_specs=[
            pl.BlockSpec((block, columns + tail), lambda i: (i, 0)),
            pl.BlockSpec((block, 128), lambda i: (i, 0)),
        ],
        out_shape=[
            jax.ShapeDtypeStruct((rows, columns + tail), jnp.bfloat16),
            jax.ShapeDtypeStruct((rows, 128), jnp.float32),
        ],
        compiler_params=compiler_params(),
        cost_estimate=small_cost(),
        name="logit_grads",
    )(logits, listed, stats, scale)


def put_row(out_ref, value):
    width = value.shape[1] - tail
    code, power = encode(value[:, :width])
    term, term_power = encode(value[:, width : width + 1])
    lane = lax.broadcasted_iota(jnp.int32, (value.shape[0], tail), 1)
    beside = jnp.where(lane == 0, power, jnp.where(lane == 1, term.astype(jnp.int32).astype(jnp.float32), term_power))
    out_ref[:, :width] = code
    out_ref[:, width:] = beside.astype(jnp.int32).astype(jnp.int16)


def take_row(codes_ref):
    width = codes_ref.shape[1] - tail
    beside = codes_ref[:, width:].astype(jnp.int32).astype(jnp.float32)
    value = codes_ref[:, :width].astype(jnp.int32).astype(jnp.float32) * jnp.exp(beside[:, 0:1] * per_step)
    term = beside[:, 1:2] * jnp.exp(beside[:, 2:3] * per_step)
    return value, jnp.broadcast_to(term, beside.shape)


def back_kernel(tiles, keeps, place_ref, grad_ref, beside_ref, head_ref, *refs):
    outs, total_ref = refs[:-1], refs[-1]
    tile = pl.program_id(0)

    @pl.when(tile == 0)
    def _():
        total_ref[...] = jnp.zeros_like(total_ref)

    total_ref[...] += lax.dot_general(
        grad_ref[...], head_ref[...], (((1,), (1,)), ((), ())), preferred_element_type=jnp.float32
    )

    @pl.when(tile == tiles - 1)
    def _():
        term = beside_ref[...].astype(jnp.float32)
        term = jnp.broadcast_to(term[:, 0:1] + term[:, 1:2] + term[:, 2:3], term.shape)
        width = outs[0].shape[1] - tail
        for k, out_ref in enumerate(outs):
            start = pl.multiple_of((place_ref[1] ^ k) * width, width)
            value = total_ref[:, pl.ds(start, width)]
            if k == 0 and keeps:
                out_ref[:, :width] = value
                out_ref[:, width:] = term
            else:
                put_row(out_ref, jnp.concatenate([value, term], axis=1))


def back(grad, head, place, width, group, keeps):
    depth, columns = head.shape
    rows = grad.shape[0]
    blocks = max(group // 2, 1)
    part = depth // group
    types = [jnp.float32 if keeps and k == 0 else jnp.int16 for k in range(blocks)]
    return pl.pallas_call(
        functools.partial(back_kernel, columns // width, keeps),
        grid_spec=pltpu.PrefetchScalarGridSpec(
            num_scalar_prefetch=1,
            grid=(columns // width,),
            in_specs=[
                pl.BlockSpec((rows, width), lambda j, place: (0, j)),
                pl.BlockSpec((rows, tail), lambda j, place: (0, columns // tail)),
                pl.BlockSpec((blocks * part, width), lambda j, place: (place[0], j)),
            ],
            out_specs=[constant(rows, part + tail)] * blocks,
            scratch_shapes=[pltpu.VMEM((rows, blocks * part), jnp.float32)],
        ),
        out_shape=[jax.ShapeDtypeStruct((rows, part + tail), t) for t in types],
        compiler_params=compiler_params(),
        cost_estimate=small_cost(),
        name="grad_rows",
    )(place, grad, grad, head)


def group_kernel(place_ref, keep_ref, *refs):
    total_ref = refs[-1]
    count = place_ref.shape[0] - 1
    out_ref, sends, received = refs[-2 - count], refs[-1 - count : -1], refs[: -2 - count]
    width = keep_ref.shape[1] - tail
    total, term = keep_ref[:, :width], keep_ref[:, width:]
    for codes_ref in received:
        more, more_term = take_row(codes_ref)
        total, term = total + more, term + more_term
    total_ref[:, :width] = total
    total_ref[:, width:] = term
    rows = out_ref.shape[0]
    block = lambda b: total_ref[pl.ds(pl.multiple_of(b * rows, rows), rows), :]
    out_ref[...] = block(place_ref[0])
    for k, send_ref in enumerate(sends, 1):
        put_row(send_ref, block(place_ref[k]))


def group_sum(place, keep, received):
    blocks = place.shape[0]
    rows, width = keep.shape
    each = (rows // blocks, width)
    return pl.pallas_call(
        group_kernel,
        in_specs=[pl.BlockSpec(memory_space=pltpu.SMEM)]
        + [pl.BlockSpec(memory_space=pltpu.VMEM)] * (1 + len(received)),
        out_specs=[pl.BlockSpec(memory_space=pltpu.VMEM)] * blocks,
        out_shape=[jax.ShapeDtypeStruct(each, jnp.float32)]
        + [jax.ShapeDtypeStruct(each, jnp.int16)] * (blocks - 1),
        scratch_shapes=[pltpu.VMEM((rows, width), jnp.float32)],
        compiler_params=compiler_params(),
        cost_estimate=small_cost(),
        name="group_sum",
    )(place, keep, *received)


def last_kernel(keep_ref, *refs):
    width = keep_ref.shape[1] - tail
    total, term = keep_ref[:, :width], keep_ref[:, width:]
    for codes_ref in refs[:-1]:
        more, more_term = take_row(codes_ref)
        total, term = total + more, term + more_term
    put_row(refs[-1], jnp.concatenate([total, term], axis=1))


def last_sum(keep, received):
    return pl.pallas_call(
        last_kernel,
        in_specs=[pl.BlockSpec(memory_space=pltpu.VMEM)] * (1 + len(received)),
        out_specs=pl.BlockSpec(memory_space=pltpu.VMEM),
        out_shape=jax.ShapeDtypeStruct(keep.shape, jnp.int16),
        compiler_params=compiler_params(),
        cost_estimate=small_cost(),
        name="last_sum",
    )(keep, *received)


def after(value, *others):
    return lax.optimization_barrier((value, *others))[0]


def shards(hidden, head, gain, refusal_ids, refusal_count, loss_scale):
    row_count, model_width = hidden.shape
    depth, vocab_local = head.shape
    list_length = refusal_ids.shape[1]
    prompt_size = lax.axis_size("prompt")
    vocab_size = lax.axis_size("vocab")
    group = vocab_size // prompt_size
    width = min(1024, vocab_local // 2)
    tiles = vocab_local // width
    half = row_count // 2
    me = lax.axis_index("prompt")
    shard = lax.axis_index("vocab")
    to_x, to_y, to_far = ([(p, p ^ k) for p in range(prompt_size)] for k in (1, 2, 3))
    send = lambda value, pairs: lax.ppermute(value, "prompt", pairs)

    hidden_f = hidden.astype(jnp.float32)
    inverse_rms = lax.rsqrt(jnp.mean(hidden_f * hidden_f, axis=1, keepdims=True) + epsilon)
    normed = (hidden_f * inverse_rms * gain).astype(jnp.bfloat16)
    columns = lambda p: lax.dynamic_slice_in_dim(normed, p * depth, depth, 1)
    rows_far = send(columns(me ^ 3), to_far)
    beside = ((0, 0), (0, tail))
    rows_x = send(jnp.pad(columns(me ^ 1), beside), to_x)
    rows_y = send(jnp.pad(columns(me ^ 2), beside), to_y)
    own = own_logits(columns(me), head, width)
    first_tiles = tiles // 2
    column_parts = ((0, first_tiles), (first_tiles, tiles - first_tiles))
    by_x, by_y = [], []
    for (skip, count), waits in zip(column_parts, ([own], [rows_x, rows_y])):
        first, second = far_codes(after(rows_far, *waits), head, width, skip, count)
        by_x.append(send(first, to_x))
        by_y.append(send(second, to_y))
    halves = []
    for part in range(2):
        sums_x, sums_y = [], []
        for c, (skip, count) in enumerate(column_parts):
            codes_x, codes_y = near_codes(part, rows_x, rows_y, head, by_x[c], by_y[c], width, skip, count)
            sums_x.append(send(codes_x, to_x))
            sums_y.append(send(codes_y, to_y))
        halves.append((sums_x, sums_y))
        rows_x = after(rows_x, codes_x, sums_x[0], sums_y[0])

    in_list = jnp.arange(list_length)[None, :] < refusal_count[:, None]
    ids = jnp.where(in_list, refusal_ids - shard * vocab_local, -1)

    block, member = shard // group, shard % group
    spread = max(group // 2, 1)
    place_other = jnp.stack([(member // spread) ^ 1, member % spread]).astype(jnp.int32)
    place_mine = jnp.stack([member // spread, member % spread]).astype(jnp.int32)
    place_block = jnp.stack([block ^ k ^ me for k in range(prompt_size)]).astype(jnp.int32)
    to_member = [[(v, v ^ k) for v in range(vocab_size)] for k in range(1, group)]
    to_block = [
        [(v, ((v // group) ^ k) * group + v % group) for v in range(vocab_size)]
        for k in range(1, prompt_size)
    ]
    moves = []
    for p in range(prompt_size):
        for r in range(prompt_size):
            for i in range(group):
                moves.append((p * vocab_size + r * group + i, r * vocab_size + p * group + i))

    quarter = half // 2
    infos, grads = [], []
    for part, (sums_x, sums_y) in enumerate(halves):
        logits, listed, stats = row_stats(part, own, sums_x, sums_y, after(ids, *infos), width)
        stats = lax.all_gather(stats, "vocab", axis=0)
        grad, info = logit_grads(part, logits, listed, stats, loss_scale[:, None], width)
        infos.append(info)
        grads.append(grad)
    log_refusal = jnp.concatenate([info[:, 0] for info in infos])

    def neighbours(grad, *waits):
        sent = after(grad, *waits)
        return grad, send(sent, to_x), send(sent, to_y)

    def diagonal(grad_x, grad_y, *waits):
        passed_x, passed_y = after(grad_y, *waits)[:quarter], after(grad_x, *waits)[quarter:]
        return (passed_x, passed_y), [send(passed_x, to_x), send(passed_y, to_y)]

    def gradient(rows, waits_other=(), waits_mine=()):
        rows = jnp.concatenate(rows)
        others = back(rows, head, after(place_other, *waits_other), width, group, False)
        received = [lax.ppermute(c, "vocab", to) for c, to in zip(others, to_member[spread - 1 :])]
        keep, *codes = back(rows, head, after(place_mine, *others, *waits_mine), width, group, True)
        received += [lax.ppermute(c, "vocab", to) for c, to in zip(codes, to_member)]
        return keep, received

    def blocks(keep, received, *waits):
        keep, *codes = group_sum(after(place_block, *waits), keep, received)
        return keep, [lax.ppermute(c, "vocab", to) for c, to in zip(codes, to_block)]

    rows_a = neighbours(grads[0])
    _, far_a = diagonal(*rows_a[1:], infos[1])
    rows_b = neighbours(grads[1], *far_a)
    keep_a, received_a = gradient((*rows_a, *far_a))
    passed, far_b = diagonal(*rows_b[1:], keep_a)
    keep_a, received_a = blocks(keep_a, received_a, *passed)
    sum_a = last_sum(keep_a, received_a)
    keep_b, received_b = gradient((*rows_b, *far_b), received_a, [sum_a])
    sum_b = last_sum(*blocks(keep_b, received_b))
    grad_cols = [lax.ppermute(total, ("prompt", "vocab"), moves) for total in (sum_a, sum_b)]

    slice_width = model_width // vocab_size
    col_start = shard * slice_width
    codes = jnp.concatenate(grad_cols)
    power = codes[:, slice_width : slice_width + 1].astype(jnp.float32)
    grad_cols = codes[:, :slice_width].astype(jnp.float32) * jnp.exp(power * per_step)
    term = codes[:, slice_width + 1 : slice_width + 3].astype(jnp.float32)
    row_term = term[:, 0] * jnp.exp(term[:, 1] * per_step)
    hidden_cols = lax.dynamic_slice_in_dim(hidden, col_start, slice_width, 1).astype(jnp.float32)
    gain_cols = lax.dynamic_slice_in_dim(gain, col_start, slice_width, 0)
    grad_hidden = (
        inverse_rms * gain_cols * grad_cols
        - hidden_cols * (inverse_rms * inverse_rms / model_width) * row_term[:, None]
    )
    return (grad_hidden, log_refusal)


def solution(mesh):
    return jax.shard_map(
        shards,
        mesh=mesh,
        in_specs=(
            P("prompt", None),
            P("prompt", "vocab"),
            P(),
            P("prompt", None),
            P("prompt"),
            P("prompt"),
        ),
        out_specs=(P("prompt", "vocab"), P("prompt")),
        check_vma=False,
    )
```

```python
import functools
import math

import jax
import jax.numpy as jnp
from jax import lax
from jax.experimental import pallas as pl
from jax.experimental.pallas import tpu as pltpu
from jax.sharding import PartitionSpec as P

epsilon = 1e-05
lowest = -1e30
tail = 128
steps = 64
code_top = 32000.0
per_step = math.log(2.0) / steps
megabyte = 1024 * 1024


def encode(value):
    top = jnp.max(jnp.abs(value), axis=1, keepdims=True)
    power = jnp.ceil(jnp.log(jnp.maximum(top, 1e-30) * (1.0 / code_top)) * (1.0 / per_step))
    code = jnp.round(value * jnp.exp(power * -per_step))
    return code.astype(jnp.int32).astype(jnp.int16), power


def decode(codes_ref, tile, width, vocab_local, rows=slice(None)):
    powers = codes_ref[rows, vocab_local : vocab_local + tail].astype(jnp.int32).astype(jnp.float32)
    lane = lax.broadcasted_iota(jnp.int32, powers.shape, 1)
    power = jnp.sum(jnp.where(lane == tile, powers, 0.0), axis=1, keepdims=True)
    start = tile * width
    if not isinstance(start, int):
        start = pl.multiple_of(start, width)
    codes = codes_ref[rows, pl.ds(start, width)].astype(jnp.int32).astype(jnp.float32)
    return codes * jnp.exp(power * per_step)


def put(out_ref, powers_ref, rows, tile, width, vocab_local, value):
    code, power = encode(value)
    out_ref[:, pl.ds(pl.multiple_of(tile * width, width), width)] = code
    lane = lax.broadcasted_iota(jnp.int32, (value.shape[0], tail), 1)
    powers = jnp.where(lane >= tile, power, powers_ref[rows, :])
    powers_ref[rows, :] = powers
    out_ref[:, vocab_local:] = powers.astype(jnp.int32).astype(jnp.int16)


def dot(a, b):
    return jnp.dot(a, b, preferred_element_type=jnp.float32)


def compiler_params():
    return pltpu.CompilerParams(vmem_limit_bytes=28 * megabyte)


def small_cost():
    return pl.CostEstimate(flops=1024, bytes_accessed=1024, transcendentals=0)


head_spec = pl.BlockSpec(memory_space=pl.ANY)


def head_scratch(rows, width, tiles):
    slots = min(tiles, 16 * megabyte // (2 * rows * width))
    return [pltpu.VMEM((slots, rows, width), jnp.bfloat16), pltpu.SemaphoreType.DMA((slots,))]


class Tiles:
    def __init__(self, head_ref, slots_ref, sems_ref, first_row, skip, tiles):
        self.slots, rows, width = slots_ref.shape
        self.tiles, self.slots_ref = tiles, slots_ref

        def copy(tile):
            slot = lax.rem(tile, self.slots)
            column = pl.multiple_of((tile + skip) * width, width)
            source = head_ref.at[pl.ds(first_row, rows), pl.ds(column, width)]
            return pltpu.make_async_copy(source, slots_ref.at[slot], sems_ref.at[slot])

        self.copy = copy

    def get(self, tile):
        @pl.when(tile == 0)
        def _():
            for first in range(self.slots):
                self.copy(first).start()

        self.copy(tile).wait()
        return self.slots_ref[lax.rem(tile, self.slots)]

    def release(self, tile):
        if self.slots < self.tiles:

            @pl.when(tile + self.slots < self.tiles)
            def _():
                self.copy(tile + self.slots).start()


def constant(*shape):
    return pl.BlockSpec(shape, lambda *_: (0,) * len(shape))


def far_kernel(width, skip, tiles, x_ref, head_ref, first_ref, second_ref, powers_ref, slots_ref, sems_ref):
    tile = pl.program_id(0)
    head = Tiles(head_ref, slots_ref, sems_ref, 0, skip, tiles)
    columns = first_ref.shape[1] - tail
    value = dot(x_ref[...], head.get(tile))
    head.release(tile)
    q = value.shape[0] // 4
    first = jnp.concatenate([value[:q], value[2 * q : 3 * q]], axis=0)
    second = jnp.concatenate([value[q : 2 * q], value[3 * q :]], axis=0)
    put(first_ref, powers_ref, slice(0, 2 * q), tile, width, columns, first)
    put(second_ref, powers_ref, slice(2 * q, 4 * q), tile, width, columns, second)


def far_codes(rows_in, head, width, skip, tiles):
    rows, depth = rows_in.shape
    columns = tiles * width
    return pl.pallas_call(
        functools.partial(far_kernel, width, skip, tiles),
        grid=(tiles,),
        in_specs=[constant(rows, depth), head_spec],
        out_specs=[constant(rows // 2, columns + tail)] * 2,
        out_shape=[jax.ShapeDtypeStruct((rows // 2, columns + tail), jnp.int16)] * 2,
        scratch_shapes=[pltpu.VMEM((rows, tail), jnp.float32)] + head_scratch(depth, width, tiles),
        compiler_params=compiler_params(),
        cost_estimate=small_cost(),
        name="far_codes",
    )(rows_in, head)


def near_kernel(width, skip, tiles, x_ref, y_ref, head_ref, by_x_ref, by_y_ref, to_x_ref, to_y_ref, *refs):
    powers_ref, slots_ref, sems_ref = refs
    tile = pl.program_id(0)
    head = Tiles(head_ref, slots_ref, sems_ref, 0, skip, tiles)
    rows = x_ref.shape[0]
    half = rows // 2
    columns = to_x_ref.shape[1] - tail
    value = dot(jnp.concatenate([x_ref[...], y_ref[...]], axis=0), head.get(tile))
    head.release(tile)
    more_x = decode(by_y_ref, tile, width, columns)
    more_y = decode(by_x_ref, tile, width, columns)
    for_x = jnp.concatenate([value[:half], value[half:rows] + more_x], axis=0)
    for_y = jnp.concatenate([value[rows : rows + half] + more_y, value[rows + half :]], axis=0)
    put(to_x_ref, powers_ref, slice(0, rows), tile, width, columns, for_x)
    put(to_y_ref, powers_ref, slice(rows, 2 * rows), tile, width, columns, for_y)


def near_codes(part, rows_x, rows_y, head, by_x, by_y, width, skip, tiles):
    depth = head.shape[0]
    rows = rows_x.shape[0] // 2
    columns = tiles * width
    return pl.pallas_call(
        functools.partial(near_kernel, width, skip, tiles),
        grid=(tiles,),
        in_specs=[pl.BlockSpec((rows, depth), lambda j: (part, 0))] * 2
        + [head_spec]
        + [pl.BlockSpec((rows // 2, columns + tail), lambda j: (part, 0))] * 2,
        out_specs=[constant(rows, columns + tail)] * 2,
        out_shape=[jax.ShapeDtypeStruct((rows, columns + tail), jnp.int16)] * 2,
        scratch_shapes=[pltpu.VMEM((2 * rows, tail), jnp.float32)] + head_scratch(depth, width, tiles),
        compiler_params=compiler_params(),
        cost_estimate=small_cost(),
        name="near_codes",
    )(rows_x, rows_y, head, by_x, by_y)


def own_kernel(tiles, x_ref, head_ref, out_ref, slots_ref, sems_ref):
    tile = pl.program_id(0)
    head = Tiles(head_ref, slots_ref, sems_ref, 0, 0, tiles)
    out_ref[...] = dot(x_ref[...], head.get(tile))
    head.release(tile)


def own_logits(rows_in, head, width):
    rows, depth = rows_in.shape
    columns = head.shape[1]
    return pl.pallas_call(
        functools.partial(own_kernel, columns // width),
        grid=(columns // width,),
        in_specs=[constant(rows, depth), head_spec],
        out_specs=pl.BlockSpec((rows, width), lambda j: (0, j)),
        out_shape=jax.ShapeDtypeStruct((rows, columns), jnp.float32),
        scratch_shapes=head_scratch(depth, width, columns // width),
        compiler_params=compiler_params(),
        cost_estimate=small_cost(),
        name="own_logits",
    )(rows_in, head)


def members(ids, start, width):
    rows = ids.shape[0]
    column = lax.broadcasted_iota(jnp.int32, (rows, width), 1) + start
    found = column == ids[:, 0:1]
    for k in range(1, ids.shape[1]):
        found = found | (column == ids[:, k : k + 1])
    return found


def stats_kernel(width, parts, *refs):
    own_ref, by_x_refs, by_y_refs = refs[0], refs[1 : 1 + parts], refs[1 + parts : 1 + 2 * parts]
    ids_ref, logits_ref, listed_ref, out_ref = refs[1 + 2 * parts :]
    rows, columns = logits_ref.shape
    each = columns // parts
    ids = ids_ref[...]
    top_all = jnp.full((rows, width), lowest, jnp.float32)
    top_ref = jnp.full((rows, width), lowest, jnp.float32)
    for start in range(0, columns, width):
        at = slice(start, start + width)
        where, inner = start // each, start % each // width
        piece = own_ref[:, at] + decode(by_x_refs[where], inner, width, each)
        piece = piece + decode(by_y_refs[where], inner, width, each)
        listed = jnp.where(members(ids, start, width), piece, lowest)
        logits_ref[:, at] = piece
        listed_ref[:, at] = listed
        top_all = jnp.maximum(top_all, piece)
        top_ref = jnp.maximum(top_ref, listed)
    peak_all = jnp.max(top_all, axis=1, keepdims=True)
    peak_ref = jnp.max(top_ref, axis=1, keepdims=True)
    sum_all = jnp.zeros((rows, width), jnp.float32)
    sum_ref = jnp.zeros((rows, width), jnp.float32)
    for start in range(0, columns, width):
        at = slice(start, start + width)
        sum_all = sum_all + jnp.exp(logits_ref[:, at] - peak_all)
        sum_ref = sum_ref + jnp.exp(listed_ref[:, at] - peak_ref)
    sum_all = jnp.sum(sum_all, axis=1, keepdims=True)
    sum_ref = jnp.sum(sum_ref, axis=1, keepdims=True)
    lane = lax.broadcasted_iota(jnp.int32, out_ref.shape, 1)
    out_ref[...] = jnp.where(
        lane == 0, peak_all, jnp.where(lane == 1, peak_ref, jnp.where(lane == 2, sum_all, sum_ref))
    )


def row_stats(part, own, by_x, by_y, ids, width):
    rows = by_x[0].shape[0]
    parts = len(by_x)
    columns = own.shape[1]
    block = min(rows, 16)
    skip = part * (rows // block)
    across = lambda array: pl.BlockSpec((block, array.shape[1]), lambda i: (i, 0))
    return pl.pallas_call(
        functools.partial(stats_kernel, width, parts),
        grid=(rows // block,),
        in_specs=[pl.BlockSpec((block, columns), lambda i: (i + skip, 0))]
        + [across(a) for a in (*by_x, *by_y)]
        + [pl.BlockSpec((block, ids.shape[1]), lambda i: (i + skip, 0))],
        out_specs=[
            pl.BlockSpec((block, columns), lambda i: (i, 0)),
            pl.BlockSpec((block, columns), lambda i: (i, 0)),
            pl.BlockSpec((block, 128), lambda i: (i, 0)),
        ],
        out_shape=[
            jax.ShapeDtypeStruct((rows, columns), jnp.float32),
            jax.ShapeDtypeStruct((rows, columns), jnp.float32),
            jax.ShapeDtypeStruct((rows, 128), jnp.float32),
        ],
        compiler_params=compiler_params(),
        cost_estimate=small_cost(),
        name="row_stats",
    )(own, *by_x, *by_y, ids)


def grad_kernel(width, logits_ref, listed_ref, stats_ref, scale_ref, out_ref, info_ref):
    rows, columns = logits_ref.shape
    stats = [stats_ref[v] for v in range(stats_ref.shape[0])]
    peaks = functools.reduce(jnp.maximum, [s[:, :2] for s in stats])
    sums = functools.reduce(jnp.add, [s[:, 2:4] * jnp.exp(s[:, :2] - peaks) for s in stats])
    lse = peaks + jnp.log(sums)
    lse_all, lse_ref = lse[:, 0:1], lse[:, 1:2]
    scale = scale_ref[...]
    term = jnp.zeros((rows, width), jnp.float32)
    for start in range(0, columns, width):
        at = slice(start, start + width)
        piece = logits_ref[:, at]
        grad = scale * (jnp.exp(listed_ref[:, at] - lse_ref) - jnp.exp(piece - lse_all))
        grad = grad.astype(jnp.bfloat16)
        out_ref[:, at] = grad
        term = term + grad.astype(jnp.float32) * piece
    lane = lax.broadcasted_iota(jnp.int32, info_ref.shape, 1)
    info_ref[...] = jnp.broadcast_to(lse_ref - lse_all, info_ref.shape)
    term = jnp.sum(term, axis=1, keepdims=True)
    high = term.astype(jnp.bfloat16).astype(jnp.float32)
    middle = (term - high).astype(jnp.bfloat16).astype(jnp.float32)
    low = term - high - middle
    term = jnp.where(lane == 0, high, jnp.where(lane == 1, middle, jnp.where(lane == 2, low, 0.0)))
    out_ref[:, columns:] = term.astype(jnp.bfloat16)


def logit_grads(part, logits, listed, stats, scale, width):
    rows, columns = logits.shape
    block = min(rows, 16)
    skip = part * (rows // block)
    return pl.pallas_call(
        functools.partial(grad_kernel, width),
        grid=(rows // block,),
        in_specs=[
            pl.BlockSpec((block, columns), lambda i: (i, 0)),
            pl.BlockSpec((block, columns), lambda i: (i, 0)),
            pl.BlockSpec((stats.shape[0], block, 128), lambda i: (0, i, 0)),
            pl.BlockSpec((block, 1), lambda i: (i + skip, 0)),
        ],
        out_specs=[
            pl.BlockSpec((block, columns + tail), lambda i: (i, 0)),
            pl.BlockSpec((block, 128), lambda i: (i, 0)),
        ],
        out_shape=[
            jax.ShapeDtypeStruct((rows, columns + tail), jnp.bfloat16),
            jax.ShapeDtypeStruct((rows, 128), jnp.float32),
        ],
        compiler_params=compiler_params(),
        cost_estimate=small_cost(),
        name="logit_grads",
    )(logits, listed, stats, scale)


def put_row(out_ref, value):
    width = value.shape[1] - tail
    code, power = encode(value[:, :width])
    term, term_power = encode(value[:, width : width + 1])
    lane = lax.broadcasted_iota(jnp.int32, (value.shape[0], tail), 1)
    beside = jnp.where(lane == 0, power, jnp.where(lane == 1, term.astype(jnp.int32).astype(jnp.float32), term_power))
    out_ref[:, :width] = code
    out_ref[:, width:] = beside.astype(jnp.int32).astype(jnp.int16)


def take_row(codes_ref):
    width = codes_ref.shape[1] - tail
    beside = codes_ref[:, width:].astype(jnp.int32).astype(jnp.float32)
    value = codes_ref[:, :width].astype(jnp.int32).astype(jnp.float32) * jnp.exp(beside[:, 0:1] * per_step)
    term = beside[:, 1:2] * jnp.exp(beside[:, 2:3] * per_step)
    return value, jnp.broadcast_to(term, beside.shape)


def back_kernel(tiles, keeps, place_ref, grad_ref, beside_ref, head_ref, *refs):
    outs, (total_ref, slots_ref, sems_ref) = refs[:-3], refs[-3:]
    tile = pl.program_id(0)
    rows = slots_ref.shape[1]
    head = Tiles(head_ref, slots_ref, sems_ref, pl.multiple_of(place_ref[0] * rows, rows), 0, tiles)

    @pl.when(tile == 0)
    def _():
        total_ref[...] = jnp.zeros_like(total_ref)

    total_ref[...] += lax.dot_general(
        grad_ref[...], head.get(tile), (((1,), (1,)), ((), ())), preferred_element_type=jnp.float32
    )
    head.release(tile)

    @pl.when(tile == tiles - 1)
    def _():
        term = beside_ref[...].astype(jnp.float32)
        term = jnp.broadcast_to(term[:, 0:1] + term[:, 1:2] + term[:, 2:3], term.shape)
        width = outs[0].shape[1] - tail
        for k, out_ref in enumerate(outs):
            start = pl.multiple_of((place_ref[1] ^ k) * width, width)
            value = total_ref[:, pl.ds(start, width)]
            if k == 0 and keeps:
                out_ref[:, :width] = value
                out_ref[:, width:] = term
            else:
                put_row(out_ref, jnp.concatenate([value, term], axis=1))


def back(grad, head, place, width, group, keeps):
    depth, columns = head.shape
    rows = grad.shape[0]
    blocks = max(group // 2, 1)
    part = depth // group
    types = [jnp.float32 if keeps and k == 0 else jnp.int16 for k in range(blocks)]
    return pl.pallas_call(
        functools.partial(back_kernel, columns // width, keeps),
        grid_spec=pltpu.PrefetchScalarGridSpec(
            num_scalar_prefetch=1,
            grid=(columns // width,),
            in_specs=[
                pl.BlockSpec((rows, width), lambda j, place: (0, j)),
                pl.BlockSpec((rows, tail), lambda j, place: (0, columns // tail)),
                head_spec,
            ],
            out_specs=[constant(rows, part + tail)] * blocks,
            scratch_shapes=[pltpu.VMEM((rows, blocks * part), jnp.float32)]
            + head_scratch(blocks * part, width, columns // width),
        ),
        out_shape=[jax.ShapeDtypeStruct((rows, part + tail), t) for t in types],
        compiler_params=compiler_params(),
        cost_estimate=small_cost(),
        name="grad_rows",
    )(place, grad, grad, head)


def group_kernel(place_ref, keep_ref, *refs):
    total_ref = refs[-1]
    count = place_ref.shape[0] - 1
    out_ref, sends, received = refs[-2 - count], refs[-1 - count : -1], refs[: -2 - count]
    width = keep_ref.shape[1] - tail
    total, term = keep_ref[:, :width], keep_ref[:, width:]
    for codes_ref in received:
        more, more_term = take_row(codes_ref)
        total, term = total + more, term + more_term
    total_ref[:, :width] = total
    total_ref[:, width:] = term
    rows = out_ref.shape[0]
    block = lambda b: total_ref[pl.ds(pl.multiple_of(b * rows, rows), rows), :]
    out_ref[...] = block(place_ref[0])
    for k, send_ref in enumerate(sends, 1):
        put_row(send_ref, block(place_ref[k]))


def group_sum(place, keep, received):
    blocks = place.shape[0]
    rows, width = keep.shape
    each = (rows // blocks, width)
    return pl.pallas_call(
        group_kernel,
        in_specs=[pl.BlockSpec(memory_space=pltpu.SMEM)]
        + [pl.BlockSpec(memory_space=pltpu.VMEM)] * (1 + len(received)),
        out_specs=[pl.BlockSpec(memory_space=pltpu.VMEM)] * blocks,
        out_shape=[jax.ShapeDtypeStruct(each, jnp.float32)]
        + [jax.ShapeDtypeStruct(each, jnp.int16)] * (blocks - 1),
        scratch_shapes=[pltpu.VMEM((rows, width), jnp.float32)],
        compiler_params=compiler_params(),
        cost_estimate=small_cost(),
        name="group_sum",
    )(place, keep, *received)


def last_kernel(keep_ref, *refs):
    width = keep_ref.shape[1] - tail
    total, term = keep_ref[:, :width], keep_ref[:, width:]
    for codes_ref in refs[:-1]:
        more, more_term = take_row(codes_ref)
        total, term = total + more, term + more_term
    put_row(refs[-1], jnp.concatenate([total, term], axis=1))


def last_sum(keep, received):
    return pl.pallas_call(
        last_kernel,
        in_specs=[pl.BlockSpec(memory_space=pltpu.VMEM)] * (1 + len(received)),
        out_specs=pl.BlockSpec(memory_space=pltpu.VMEM),
        out_shape=jax.ShapeDtypeStruct(keep.shape, jnp.int16),
        compiler_params=compiler_params(),
        cost_estimate=small_cost(),
        name="last_sum",
    )(keep, *received)


def after(value, *others):
    return lax.optimization_barrier((value, *others))[0]


def shards(hidden, head, gain, refusal_ids, refusal_count, loss_scale):
    row_count, model_width = hidden.shape
    depth, vocab_local = head.shape
    list_length = refusal_ids.shape[1]
    prompt_size = lax.axis_size("prompt")
    vocab_size = lax.axis_size("vocab")
    group = vocab_size // prompt_size
    width = min(1024, vocab_local // 2)
    tiles = vocab_local // width
    half = row_count // 2
    me = lax.axis_index("prompt")
    shard = lax.axis_index("vocab")
    to_x, to_y, to_far = ([(p, p ^ k) for p in range(prompt_size)] for k in (1, 2, 3))
    send = lambda value, pairs: lax.ppermute(value, "prompt", pairs)

    hidden_f = hidden.astype(jnp.float32)
    inverse_rms = lax.rsqrt(jnp.mean(hidden_f * hidden_f, axis=1, keepdims=True) + epsilon)
    normed = (hidden_f * inverse_rms * gain).astype(jnp.bfloat16)
    columns = lambda p: lax.dynamic_slice_in_dim(normed, p * depth, depth, 1)
    rows_far = send(columns(me ^ 3), to_far)
    beside = ((0, 0), (0, tail))
    rows_x = send(jnp.pad(columns(me ^ 1), beside), to_x)
    rows_y = send(jnp.pad(columns(me ^ 2), beside), to_y)
    own = own_logits(columns(me), head, width)
    first_tiles = tiles // 2
    column_parts = ((0, first_tiles), (first_tiles, tiles - first_tiles))
    by_x, by_y = [], []
    for (skip, count), waits in zip(column_parts, ([own], [rows_x, rows_y])):
        first, second = far_codes(after(rows_far, *waits), head, width, skip, count)
        by_x.append(send(first, to_x))
        by_y.append(send(second, to_y))
    halves = []
    for part in range(2):
        sums_x, sums_y = [], []
        for c, (skip, count) in enumerate(column_parts):
            codes_x, codes_y = near_codes(part, rows_x, rows_y, head, by_x[c], by_y[c], width, skip, count)
            sums_x.append(send(codes_x, to_x))
            sums_y.append(send(codes_y, to_y))
        halves.append((sums_x, sums_y))
        rows_x = after(rows_x, codes_x, sums_x[0], sums_y[0])

    in_list = jnp.arange(list_length)[None, :] < refusal_count[:, None]
    ids = jnp.where(in_list, refusal_ids - shard * vocab_local, -1)

    block, member = shard // group, shard % group
    spread = max(group // 2, 1)
    place_other = jnp.stack([(member // spread) ^ 1, member % spread]).astype(jnp.int32)
    place_mine = jnp.stack([member // spread, member % spread]).astype(jnp.int32)
    place_block = jnp.stack([block ^ k ^ me for k in range(prompt_size)]).astype(jnp.int32)
    to_member = [[(v, v ^ k) for v in range(vocab_size)] for k in range(1, group)]
    to_block = [
        [(v, ((v // group) ^ k) * group + v % group) for v in range(vocab_size)]
        for k in range(1, prompt_size)
    ]
    moves = []
    for p in range(prompt_size):
        for r in range(prompt_size):
            for i in range(group):
                moves.append((p * vocab_size + r * group + i, r * vocab_size + p * group + i))

    quarter = half // 2
    infos, grads = [], []
    for part, (sums_x, sums_y) in enumerate(halves):
        logits, listed, stats = row_stats(part, own, sums_x, sums_y, after(ids, *infos), width)
        stats = lax.all_gather(stats, "vocab", axis=0)
        grad, info = logit_grads(part, logits, listed, stats, loss_scale[:, None], width)
        infos.append(info)
        grads.append(grad)
    log_refusal = jnp.concatenate([info[:, 0] for info in infos])

    def neighbours(grad, *waits):
        sent = after(grad, *waits)
        return grad, send(sent, to_x), send(sent, to_y)

    def diagonal(grad_x, grad_y, *waits):
        passed_x, passed_y = after(grad_y, *waits)[:quarter], after(grad_x, *waits)[quarter:]
        return (passed_x, passed_y), [send(passed_x, to_x), send(passed_y, to_y)]

    def gradient(rows, waits_other=(), waits_mine=()):
        rows = jnp.concatenate(rows)
        others = back(rows, head, after(place_other, *waits_other), width, group, False)
        received = [lax.ppermute(c, "vocab", to) for c, to in zip(others, to_member[spread - 1 :])]
        keep, *codes = back(rows, head, after(place_mine, *others, *waits_mine), width, group, True)
        received += [lax.ppermute(c, "vocab", to) for c, to in zip(codes, to_member)]
        return keep, received

    def blocks(keep, received, *waits):
        keep, *codes = group_sum(after(place_block, *waits), keep, received)
        return keep, [lax.ppermute(c, "vocab", to) for c, to in zip(codes, to_block)]

    rows_a = neighbours(grads[0])
    _, far_a = diagonal(*rows_a[1:], infos[1])
    rows_b = neighbours(grads[1], *far_a)
    keep_a, received_a = gradient((*rows_a, *far_a))
    passed, far_b = diagonal(*rows_b[1:], keep_a)
    keep_a, received_a = blocks(keep_a, received_a, *passed)
    sum_a = last_sum(keep_a, received_a)
    keep_b, received_b = gradient((*rows_b, *far_b), received_a, [sum_a])
    sum_b = last_sum(*blocks(keep_b, received_b))
    grad_cols = [lax.ppermute(total, ("prompt", "vocab"), moves) for total in (sum_a, sum_b)]

    slice_width = model_width // vocab_size
    col_start = shard * slice_width
    codes = jnp.concatenate(grad_cols)
    power = codes[:, slice_width : slice_width + 1].astype(jnp.float32)
    grad_cols = codes[:, :slice_width].astype(jnp.float32) * jnp.exp(power * per_step)
    term = codes[:, slice_width + 1 : slice_width + 3].astype(jnp.float32)
    row_term = term[:, 0] * jnp.exp(term[:, 1] * per_step)
    hidden_cols = lax.dynamic_slice_in_dim(hidden, col_start, slice_width, 1).astype(jnp.float32)
    gain_cols = lax.dynamic_slice_in_dim(gain, col_start, slice_width, 0)
    grad_hidden = (
        inverse_rms * gain_cols * grad_cols
        - hidden_cols * (inverse_rms * inverse_rms / model_width) * row_term[:, None]
    )
    return (grad_hidden, log_refusal)


def solution(mesh):
    return jax.shard_map(
        shards,
        mesh=mesh,
        in_specs=(
            P("prompt", None),
            P("prompt", "vocab"),
            P(),
            P("prompt", None),
            P("prompt"),
            P("prompt"),
        ),
        out_specs=(P("prompt", "vocab"), P("prompt")),
        check_vma=False,
    )
```

```python
import functools
import math

import jax
import jax.numpy as jnp
from jax import lax
from jax.experimental import pallas as pl
from jax.experimental.pallas import tpu as pltpu
from jax.sharding import PartitionSpec as P

epsilon = 1e-05
lowest = -1e30
tail = 128
steps = 64
code_top = 32000.0
per_step = math.log(2.0) / steps
megabyte = 1024 * 1024


def encode(value):
    top = jnp.max(jnp.abs(value), axis=1, keepdims=True)
    power = jnp.ceil(jnp.log(jnp.maximum(top, 1e-30) * (1.0 / code_top)) * (1.0 / per_step))
    code = jnp.round(value * jnp.exp(power * -per_step))
    return code.astype(jnp.int32).astype(jnp.int16), power


def decode(codes_ref, tile, width, vocab_local, rows=slice(None)):
    powers = codes_ref[rows, vocab_local : vocab_local + tail].astype(jnp.int32).astype(jnp.float32)
    lane = lax.broadcasted_iota(jnp.int32, powers.shape, 1)
    power = jnp.sum(jnp.where(lane == tile, powers, 0.0), axis=1, keepdims=True)
    start = tile * width
    if not isinstance(start, int):
        start = pl.multiple_of(start, width)
    codes = codes_ref[rows, pl.ds(start, width)].astype(jnp.int32).astype(jnp.float32)
    return codes * jnp.exp(power * per_step)


def put(out_ref, powers_ref, rows, tile, width, vocab_local, value):
    code, power = encode(value)
    out_ref[:, pl.ds(pl.multiple_of(tile * width, width), width)] = code
    lane = lax.broadcasted_iota(jnp.int32, (value.shape[0], tail), 1)
    powers = jnp.where(lane >= tile, power, powers_ref[rows, :])
    powers_ref[rows, :] = powers
    out_ref[:, vocab_local:] = powers.astype(jnp.int32).astype(jnp.int16)


def dot(a, b):
    return jnp.dot(a, b, preferred_element_type=jnp.float32)


def compiler_params():
    return pltpu.CompilerParams(vmem_limit_bytes=28 * megabyte)


def small_cost():
    return pl.CostEstimate(flops=1024, bytes_accessed=1024, transcendentals=0)


head_spec = pl.BlockSpec(memory_space=pl.ANY)


def head_scratch(rows, width, tiles):
    slots = min(tiles, 16 * megabyte // (2 * rows * width))
    return [pltpu.VMEM((slots, rows, width), jnp.bfloat16), pltpu.SemaphoreType.DMA((slots,))]


class Tiles:
    def __init__(self, head_ref, slots_ref, sems_ref, first_row, skip, tiles):
        self.slots, rows, width = slots_ref.shape
        self.tiles, self.slots_ref = tiles, slots_ref

        def copy(tile):
            slot = lax.rem(tile, self.slots)
            column = pl.multiple_of((tile + skip) * width, width)
            source = head_ref.at[pl.ds(first_row, rows), pl.ds(column, width)]
            return pltpu.make_async_copy(source, slots_ref.at[slot], sems_ref.at[slot])

        self.copy = copy

    def get(self, tile):
        @pl.when(tile == 0)
        def _():
            for first in range(self.slots):
                self.copy(first).start()

        self.copy(tile).wait()
        return self.slots_ref[lax.rem(tile, self.slots)]

    def release(self, tile):
        if self.slots < self.tiles:

            @pl.when(tile + self.slots < self.tiles)
            def _():
                self.copy(tile + self.slots).start()


def constant(*shape):
    return pl.BlockSpec(shape, lambda *_: (0,) * len(shape))


def far_kernel(width, skip, tiles, x_ref, head_ref, first_ref, second_ref, powers_ref, slots_ref, sems_ref):
    tile = pl.program_id(0)
    head = Tiles(head_ref, slots_ref, sems_ref, 0, skip, tiles)
    columns = first_ref.shape[1] - tail
    value = dot(x_ref[...], head.get(tile))
    head.release(tile)
    q = value.shape[0] // 4
    first = jnp.concatenate([value[:q], value[2 * q : 3 * q]], axis=0)
    second = jnp.concatenate([value[q : 2 * q], value[3 * q :]], axis=0)
    put(first_ref, powers_ref, slice(0, 2 * q), tile, width, columns, first)
    put(second_ref, powers_ref, slice(2 * q, 4 * q), tile, width, columns, second)


def far_codes(rows_in, head, width, skip, tiles):
    rows, depth = rows_in.shape
    columns = tiles * width
    return pl.pallas_call(
        functools.partial(far_kernel, width, skip, tiles),
        grid=(tiles,),
        in_specs=[constant(rows, depth), head_spec],
        out_specs=[constant(rows // 2, columns + tail)] * 2,
        out_shape=[jax.ShapeDtypeStruct((rows // 2, columns + tail), jnp.int16)] * 2,
        scratch_shapes=[pltpu.VMEM((rows, tail), jnp.float32)] + head_scratch(depth, width, tiles),
        compiler_params=compiler_params(),
        cost_estimate=small_cost(),
        name="far_codes",
    )(rows_in, head)


def near_kernel(width, skip, tiles, x_ref, y_ref, head_ref, by_x_ref, by_y_ref, to_x_ref, to_y_ref, *refs):
    powers_ref, slots_ref, sems_ref = refs
    tile = pl.program_id(0)
    head = Tiles(head_ref, slots_ref, sems_ref, 0, skip, tiles)
    rows = x_ref.shape[0]
    half = rows // 2
    columns = to_x_ref.shape[1] - tail
    value = dot(jnp.concatenate([x_ref[...], y_ref[...]], axis=0), head.get(tile))
    head.release(tile)
    more_x = decode(by_y_ref, tile, width, columns)
    more_y = decode(by_x_ref, tile, width, columns)
    for_x = jnp.concatenate([value[:half], value[half:rows] + more_x], axis=0)
    for_y = jnp.concatenate([value[rows : rows + half] + more_y, value[rows + half :]], axis=0)
    put(to_x_ref, powers_ref, slice(0, rows), tile, width, columns, for_x)
    put(to_y_ref, powers_ref, slice(rows, 2 * rows), tile, width, columns, for_y)


def near_codes(part, rows_x, rows_y, head, by_x, by_y, width, skip, tiles):
    depth = head.shape[0]
    rows = rows_x.shape[0] // 2
    columns = tiles * width
    return pl.pallas_call(
        functools.partial(near_kernel, width, skip, tiles),
        grid=(tiles,),
        in_specs=[pl.BlockSpec((rows, depth), lambda j: (part, 0))] * 2
        + [head_spec]
        + [pl.BlockSpec((rows // 2, columns + tail), lambda j: (part, 0))] * 2,
        out_specs=[constant(rows, columns + tail)] * 2,
        out_shape=[jax.ShapeDtypeStruct((rows, columns + tail), jnp.int16)] * 2,
        scratch_shapes=[pltpu.VMEM((2 * rows, tail), jnp.float32)] + head_scratch(depth, width, tiles),
        compiler_params=compiler_params(),
        cost_estimate=small_cost(),
        name="near_codes",
    )(rows_x, rows_y, head, by_x, by_y)


def own_kernel(tiles, x_ref, head_ref, out_ref, slots_ref, sems_ref):
    tile = pl.program_id(0)
    head = Tiles(head_ref, slots_ref, sems_ref, 0, 0, tiles)
    out_ref[...] = dot(x_ref[...], head.get(tile))
    head.release(tile)


def own_logits(rows_in, head, width):
    rows, depth = rows_in.shape
    columns = head.shape[1]
    return pl.pallas_call(
        functools.partial(own_kernel, columns // width),
        grid=(columns // width,),
        in_specs=[constant(rows, depth), head_spec],
        out_specs=pl.BlockSpec((rows, width), lambda j: (0, j)),
        out_shape=jax.ShapeDtypeStruct((rows, columns), jnp.float32),
        scratch_shapes=head_scratch(depth, width, columns // width),
        compiler_params=compiler_params(),
        cost_estimate=small_cost(),
        name="own_logits",
    )(rows_in, head)


def members(ids, start, width):
    rows = ids.shape[0]
    column = lax.broadcasted_iota(jnp.int32, (rows, width), 1) + start
    found = column == ids[:, 0:1]
    for k in range(1, ids.shape[1]):
        found = found | (column == ids[:, k : k + 1])
    return found


def stats_kernel(width, parts, *refs):
    own_ref, by_x_refs, by_y_refs = refs[0], refs[1 : 1 + parts], refs[1 + parts : 1 + 2 * parts]
    ids_ref, logits_ref, listed_ref, out_ref = refs[1 + 2 * parts :]
    rows, columns = logits_ref.shape
    each = columns // parts
    ids = ids_ref[...]
    top_all = jnp.full((rows, width), lowest, jnp.float32)
    top_ref = jnp.full((rows, width), lowest, jnp.float32)
    for start in range(0, columns, width):
        at = slice(start, start + width)
        where, inner = start // each, start % each // width
        piece = own_ref[:, at] + decode(by_x_refs[where], inner, width, each)
        piece = piece + decode(by_y_refs[where], inner, width, each)
        listed = jnp.where(members(ids, start, width), piece, lowest)
        logits_ref[:, at] = piece
        listed_ref[:, at] = listed
        top_all = jnp.maximum(top_all, piece)
        top_ref = jnp.maximum(top_ref, listed)
    peak_all = jnp.max(top_all, axis=1, keepdims=True)
    peak_ref = jnp.max(top_ref, axis=1, keepdims=True)
    sum_all = jnp.zeros((rows, width), jnp.float32)
    sum_ref = jnp.zeros((rows, width), jnp.float32)
    for start in range(0, columns, width):
        at = slice(start, start + width)
        sum_all = sum_all + jnp.exp(logits_ref[:, at] - peak_all)
        sum_ref = sum_ref + jnp.exp(listed_ref[:, at] - peak_ref)
    sum_all = jnp.sum(sum_all, axis=1, keepdims=True)
    sum_ref = jnp.sum(sum_ref, axis=1, keepdims=True)
    lane = lax.broadcasted_iota(jnp.int32, out_ref.shape, 1)
    out_ref[...] = jnp.where(
        lane == 0, peak_all, jnp.where(lane == 1, peak_ref, jnp.where(lane == 2, sum_all, sum_ref))
    )


def row_stats(part, own, by_x, by_y, ids, width):
    rows = by_x[0].shape[0]
    parts = len(by_x)
    columns = own.shape[1]
    block = min(rows, 16)
    skip = part * (rows // block)
    across = lambda array: pl.BlockSpec((block, array.shape[1]), lambda i: (i, 0))
    return pl.pallas_call(
        functools.partial(stats_kernel, width, parts),
        grid=(rows // block,),
        in_specs=[pl.BlockSpec((block, columns), lambda i: (i + skip, 0))]
        + [across(a) for a in (*by_x, *by_y)]
        + [pl.BlockSpec((block, ids.shape[1]), lambda i: (i + skip, 0))],
        out_specs=[
            pl.BlockSpec((block, columns), lambda i: (i, 0)),
            pl.BlockSpec((block, columns), lambda i: (i, 0)),
            pl.BlockSpec((block, 128), lambda i: (i, 0)),
        ],
        out_shape=[
            jax.ShapeDtypeStruct((rows, columns), jnp.float32),
            jax.ShapeDtypeStruct((rows, columns), jnp.float32),
            jax.ShapeDtypeStruct((rows, 128), jnp.float32),
        ],
        compiler_params=compiler_params(),
        cost_estimate=small_cost(),
        name="row_stats",
    )(own, *by_x, *by_y, ids)


def grad_kernel(width, logits_ref, listed_ref, stats_ref, scale_ref, out_ref, info_ref):
    rows, columns = logits_ref.shape
    stats = [stats_ref[v] for v in range(stats_ref.shape[0])]
    peaks = functools.reduce(jnp.maximum, [s[:, :2] for s in stats])
    sums = functools.reduce(jnp.add, [s[:, 2:4] * jnp.exp(s[:, :2] - peaks) for s in stats])
    lse = peaks + jnp.log(sums)
    lse_all, lse_ref = lse[:, 0:1], lse[:, 1:2]
    scale = scale_ref[...]
    term = jnp.zeros((rows, width), jnp.float32)
    for start in range(0, columns, width):
        at = slice(start, start + width)
        piece = logits_ref[:, at]
        grad = scale * (jnp.exp(listed_ref[:, at] - lse_ref) - jnp.exp(piece - lse_all))
        grad = grad.astype(jnp.bfloat16)
        out_ref[:, at] = grad
        term = term + grad.astype(jnp.float32) * piece
    lane = lax.broadcasted_iota(jnp.int32, info_ref.shape, 1)
    info_ref[...] = jnp.broadcast_to(lse_ref - lse_all, info_ref.shape)
    term = jnp.sum(term, axis=1, keepdims=True)
    high = term.astype(jnp.bfloat16).astype(jnp.float32)
    middle = (term - high).astype(jnp.bfloat16).astype(jnp.float32)
    low = term - high - middle
    term = jnp.where(lane == 0, high, jnp.where(lane == 1, middle, jnp.where(lane == 2, low, 0.0)))
    out_ref[:, columns:] = term.astype(jnp.bfloat16)


def logit_grads(part, logits, listed, stats, scale, width):
    rows, columns = logits.shape
    block = min(rows, 16)
    skip = part * (rows // block)
    return pl.pallas_call(
        functools.partial(grad_kernel, width),
        grid=(rows // block,),
        in_specs=[
            pl.BlockSpec((block, columns), lambda i: (i, 0)),
            pl.BlockSpec((block, columns), lambda i: (i, 0)),
            pl.BlockSpec((stats.shape[0], block, 128), lambda i: (0, i, 0)),
            pl.BlockSpec((block, 1), lambda i: (i + skip, 0)),
        ],
        out_specs=[
            pl.BlockSpec((block, columns + tail), lambda i: (i, 0)),
            pl.BlockSpec((block, 128), lambda i: (i, 0)),
        ],
        out_shape=[
            jax.ShapeDtypeStruct((rows, columns + tail), jnp.bfloat16),
            jax.ShapeDtypeStruct((rows, 128), jnp.float32),
        ],
        compiler_params=compiler_params(),
        cost_estimate=small_cost(),
        name="logit_grads",
    )(logits, listed, stats, scale)


def put_row(out_ref, value):
    width = value.shape[1] - tail
    code, power = encode(value[:, :width])
    term, term_power = encode(value[:, width : width + 1])
    lane = lax.broadcasted_iota(jnp.int32, (value.shape[0], tail), 1)
    beside = jnp.where(lane == 0, power, jnp.where(lane == 1, term.astype(jnp.int32).astype(jnp.float32), term_power))
    out_ref[:, :width] = code
    out_ref[:, width:] = beside.astype(jnp.int32).astype(jnp.int16)


def take_row(codes_ref):
    width = codes_ref.shape[1] - tail
    beside = codes_ref[:, width:].astype(jnp.int32).astype(jnp.float32)
    value = codes_ref[:, :width].astype(jnp.int32).astype(jnp.float32) * jnp.exp(beside[:, 0:1] * per_step)
    term = beside[:, 1:2] * jnp.exp(beside[:, 2:3] * per_step)
    return value, jnp.broadcast_to(term, beside.shape)


def back_kernel(tiles, keeps, place_ref, grad_ref, beside_ref, head_ref, *refs):
    outs, (total_ref, slots_ref, sems_ref) = refs[:-3], refs[-3:]
    tile = pl.program_id(0)
    rows = slots_ref.shape[1]
    head = Tiles(head_ref, slots_ref, sems_ref, pl.multiple_of(place_ref[0] * rows, rows), 0, tiles)

    @pl.when(tile == 0)
    def _():
        total_ref[...] = jnp.zeros_like(total_ref)

    total_ref[...] += dot(head.get(tile), grad_ref[...].T)
    head.release(tile)

    @pl.when(tile == tiles - 1)
    def _():
        term = beside_ref[...].astype(jnp.float32)
        term = jnp.broadcast_to(term[:, 0:1] + term[:, 1:2] + term[:, 2:3], term.shape)
        width = outs[0].shape[1] - tail
        for k, out_ref in enumerate(outs):
            start = pl.multiple_of((place_ref[1] ^ k) * width, width)
            value = total_ref[pl.ds(start, width), :].T
            if k == 0 and keeps:
                out_ref[:, :width] = value
                out_ref[:, width:] = term
            else:
                put_row(out_ref, jnp.concatenate([value, term], axis=1))


def back(grad, head, place, width, group, keeps):
    depth, columns = head.shape
    rows = grad.shape[0]
    blocks = max(group // 2, 1)
    part = depth // group
    types = [jnp.float32 if keeps and k == 0 else jnp.int16 for k in range(blocks)]
    return pl.pallas_call(
        functools.partial(back_kernel, columns // width, keeps),
        grid_spec=pltpu.PrefetchScalarGridSpec(
            num_scalar_prefetch=1,
            grid=(columns // width,),
            in_specs=[
                pl.BlockSpec((rows, width), lambda j, place: (0, j)),
                pl.BlockSpec((rows, tail), lambda j, place: (0, columns // tail)),
                head_spec,
            ],
            out_specs=[constant(rows, part + tail)] * blocks,
            scratch_shapes=[pltpu.VMEM((blocks * part, rows), jnp.float32)]
            + head_scratch(blocks * part, width, columns // width),
        ),
        out_shape=[jax.ShapeDtypeStruct((rows, part + tail), t) for t in types],
        compiler_params=compiler_params(),
        cost_estimate=small_cost(),
        name="grad_rows",
    )(place, grad, grad, head)


def group_kernel(place_ref, keep_ref, *refs):
    total_ref = refs[-1]
    count = place_ref.shape[0] - 1
    out_ref, sends, received = refs[-2 - count], refs[-1 - count : -1], refs[: -2 - count]
    width = keep_ref.shape[1] - tail
    total, term = keep_ref[:, :width], keep_ref[:, width:]
    for codes_ref in received:
        more, more_term = take_row(codes_ref)
        total, term = total + more, term + more_term
    total_ref[:, :width] = total
    total_ref[:, width:] = term
    rows = out_ref.shape[0]
    block = lambda b: total_ref[pl.ds(pl.multiple_of(b * rows, rows), rows), :]
    out_ref[...] = block(place_ref[0])
    for k, send_ref in enumerate(sends, 1):
        put_row(send_ref, block(place_ref[k]))


def group_sum(place, keep, received):
    blocks = place.shape[0]
    rows, width = keep.shape
    each = (rows // blocks, width)
    return pl.pallas_call(
        group_kernel,
        in_specs=[pl.BlockSpec(memory_space=pltpu.SMEM)]
        + [pl.BlockSpec(memory_space=pltpu.VMEM)] * (1 + len(received)),
        out_specs=[pl.BlockSpec(memory_space=pltpu.VMEM)] * blocks,
        out_shape=[jax.ShapeDtypeStruct(each, jnp.float32)]
        + [jax.ShapeDtypeStruct(each, jnp.int16)] * (blocks - 1),
        scratch_shapes=[pltpu.VMEM((rows, width), jnp.float32)],
        compiler_params=compiler_params(),
        cost_estimate=small_cost(),
        name="group_sum",
    )(place, keep, *received)


def last_kernel(keep_ref, *refs):
    width = keep_ref.shape[1] - tail
    total, term = keep_ref[:, :width], keep_ref[:, width:]
    for codes_ref in refs[:-1]:
        more, more_term = take_row(codes_ref)
        total, term = total + more, term + more_term
    put_row(refs[-1], jnp.concatenate([total, term], axis=1))


def last_sum(keep, received):
    return pl.pallas_call(
        last_kernel,
        in_specs=[pl.BlockSpec(memory_space=pltpu.VMEM)] * (1 + len(received)),
        out_specs=pl.BlockSpec(memory_space=pltpu.VMEM),
        out_shape=jax.ShapeDtypeStruct(keep.shape, jnp.int16),
        compiler_params=compiler_params(),
        cost_estimate=small_cost(),
        name="last_sum",
    )(keep, *received)


def after(value, *others):
    return lax.optimization_barrier((value, *others))[0]


def shards(hidden, head, gain, refusal_ids, refusal_count, loss_scale):
    row_count, model_width = hidden.shape
    depth, vocab_local = head.shape
    list_length = refusal_ids.shape[1]
    prompt_size = lax.axis_size("prompt")
    vocab_size = lax.axis_size("vocab")
    group = vocab_size // prompt_size
    width = min(1024, vocab_local // 2)
    tiles = vocab_local // width
    half = row_count // 2
    me = lax.axis_index("prompt")
    shard = lax.axis_index("vocab")
    to_x, to_y, to_far = ([(p, p ^ k) for p in range(prompt_size)] for k in (1, 2, 3))
    send = lambda value, pairs: lax.ppermute(value, "prompt", pairs)

    hidden_f = hidden.astype(jnp.float32)
    inverse_rms = lax.rsqrt(jnp.mean(hidden_f * hidden_f, axis=1, keepdims=True) + epsilon)
    normed = (hidden_f * inverse_rms * gain).astype(jnp.bfloat16)
    columns = lambda p: lax.dynamic_slice_in_dim(normed, p * depth, depth, 1)
    rows_far = send(columns(me ^ 3), to_far)
    beside = ((0, 0), (0, tail))
    rows_x = send(jnp.pad(columns(me ^ 1), beside), to_x)
    rows_y = send(jnp.pad(columns(me ^ 2), beside), to_y)
    own = own_logits(columns(me), head, width)
    first_tiles = tiles // 2
    column_parts = ((0, first_tiles), (first_tiles, tiles - first_tiles))
    by_x, by_y = [], []
    for (skip, count), waits in zip(column_parts, ([own], [rows_x, rows_y])):
        first, second = far_codes(after(rows_far, *waits), head, width, skip, count)
        by_x.append(send(first, to_x))
        by_y.append(send(second, to_y))
    halves = []
    for part in range(2):
        sums_x, sums_y = [], []
        for c, (skip, count) in enumerate(column_parts):
            codes_x, codes_y = near_codes(part, rows_x, rows_y, head, by_x[c], by_y[c], width, skip, count)
            sums_x.append(send(codes_x, to_x))
            sums_y.append(send(codes_y, to_y))
        halves.append((sums_x, sums_y))
        rows_x = after(rows_x, codes_x, sums_x[0], sums_y[0])

    in_list = jnp.arange(list_length)[None, :] < refusal_count[:, None]
    ids = jnp.where(in_list, refusal_ids - shard * vocab_local, -1)

    block, member = shard // group, shard % group
    spread = max(group // 2, 1)
    place_other = jnp.stack([(member // spread) ^ 1, member % spread]).astype(jnp.int32)
    place_mine = jnp.stack([member // spread, member % spread]).astype(jnp.int32)
    place_block = jnp.stack([block ^ k ^ me for k in range(prompt_size)]).astype(jnp.int32)
    to_member = [[(v, v ^ k) for v in range(vocab_size)] for k in range(1, group)]
    to_block = [
        [(v, ((v // group) ^ k) * group + v % group) for v in range(vocab_size)]
        for k in range(1, prompt_size)
    ]
    moves = []
    for p in range(prompt_size):
        for r in range(prompt_size):
            for i in range(group):
                moves.append((p * vocab_size + r * group + i, r * vocab_size + p * group + i))

    quarter = half // 2
    infos, grads = [], []
    for part, (sums_x, sums_y) in enumerate(halves):
        logits, listed, stats = row_stats(part, own, sums_x, sums_y, after(ids, *infos), width)
        stats = lax.all_gather(stats, "vocab", axis=0)
        grad, info = logit_grads(part, logits, listed, stats, loss_scale[:, None], width)
        infos.append(info)
        grads.append(grad)
    log_refusal = jnp.concatenate([info[:, 0] for info in infos])

    def neighbours(grad, *waits):
        sent = after(grad, *waits)
        return grad, send(sent, to_x), send(sent, to_y)

    def diagonal(grad_x, grad_y, *waits):
        passed_x, passed_y = after(grad_y, *waits)[:quarter], after(grad_x, *waits)[quarter:]
        return (passed_x, passed_y), [send(passed_x, to_x), send(passed_y, to_y)]

    def gradient(rows, waits_other=(), waits_mine=()):
        rows = jnp.concatenate(rows)
        others = back(rows, head, after(place_other, *waits_other), width, group, False)
        received = [lax.ppermute(c, "vocab", to) for c, to in zip(others, to_member[spread - 1 :])]
        keep, *codes = back(rows, head, after(place_mine, *others, *waits_mine), width, group, True)
        received += [lax.ppermute(c, "vocab", to) for c, to in zip(codes, to_member)]
        return keep, received

    def blocks(keep, received, *waits):
        keep, *codes = group_sum(after(place_block, *waits), keep, received)
        return keep, [lax.ppermute(c, "vocab", to) for c, to in zip(codes, to_block)]

    rows_a = neighbours(grads[0])
    _, far_a = diagonal(*rows_a[1:], infos[1])
    rows_b = neighbours(grads[1], *far_a)
    keep_a, received_a = gradient((*rows_a, *far_a))
    passed, far_b = diagonal(*rows_b[1:], keep_a)
    keep_a, received_a = blocks(keep_a, received_a, *passed)
    sum_a = last_sum(keep_a, received_a)
    keep_b, received_b = gradient((*rows_b, *far_b), received_a, [sum_a])
    sum_b = last_sum(*blocks(keep_b, received_b))
    codes = lax.ppermute(jnp.concatenate([sum_a, sum_b]), ("prompt", "vocab"), moves)

    slice_width = model_width // vocab_size
    col_start = shard * slice_width
    power = codes[:, slice_width : slice_width + 1].astype(jnp.float32)
    grad_cols = codes[:, :slice_width].astype(jnp.float32) * jnp.exp(power * per_step)
    term = codes[:, slice_width + 1 : slice_width + 3].astype(jnp.float32)
    row_term = term[:, 0] * jnp.exp(term[:, 1] * per_step)
    hidden_cols = lax.dynamic_slice_in_dim(hidden, col_start, slice_width, 1).astype(jnp.float32)
    gain_cols = lax.dynamic_slice_in_dim(gain, col_start, slice_width, 0)
    grad_hidden = (
        inverse_rms * gain_cols * grad_cols
        - hidden_cols * (inverse_rms * inverse_rms / model_width) * row_term[:, None]
    )
    return (grad_hidden, log_refusal)


def solution(mesh):
    return jax.shard_map(
        shards,
        mesh=mesh,
        in_specs=(
            P("prompt", None),
            P("prompt", "vocab"),
            P(),
            P("prompt", None),
            P("prompt"),
            P("prompt"),
        ),
        out_specs=(P("prompt", "vocab"), P("prompt")),
        check_vma=False,
    )
```

```python
import functools
import math

import jax
import jax.numpy as jnp
from jax import lax
from jax.experimental import pallas as pl
from jax.experimental.pallas import tpu as pltpu
from jax.sharding import PartitionSpec as P

epsilon = 1e-05
lowest = -1e30
tail = 128
steps = 64
code_top = 32000.0
per_step = math.log(2.0) / steps
megabyte = 1024 * 1024


def encode(value):
    top = jnp.max(jnp.abs(value), axis=1, keepdims=True)
    power = jnp.ceil(jnp.log(jnp.maximum(top, 1e-30) * (1.0 / code_top)) * (1.0 / per_step))
    code = jnp.round(value * jnp.exp(power * -per_step))
    return code.astype(jnp.int32).astype(jnp.int16), power


def decode(codes_ref, tile, width, vocab_local, rows=slice(None)):
    powers = codes_ref[rows, vocab_local : vocab_local + tail].astype(jnp.int32).astype(jnp.float32)
    lane = lax.broadcasted_iota(jnp.int32, powers.shape, 1)
    power = jnp.sum(jnp.where(lane == tile, powers, 0.0), axis=1, keepdims=True)
    start = tile * width
    if not isinstance(start, int):
        start = pl.multiple_of(start, width)
    codes = codes_ref[rows, pl.ds(start, width)].astype(jnp.int32).astype(jnp.float32)
    return codes * jnp.exp(power * per_step)


def put(out_ref, powers_ref, rows, tile, width, vocab_local, value):
    code, power = encode(value)
    out_ref[:, pl.ds(pl.multiple_of(tile * width, width), width)] = code
    lane = lax.broadcasted_iota(jnp.int32, (value.shape[0], tail), 1)
    powers = jnp.where(lane >= tile, power, powers_ref[rows, :])
    powers_ref[rows, :] = powers
    out_ref[:, vocab_local:] = powers.astype(jnp.int32).astype(jnp.int16)


def dot(a, b):
    return jnp.dot(a, b, preferred_element_type=jnp.float32)


def compiler_params():
    return pltpu.CompilerParams(vmem_limit_bytes=28 * megabyte)


def small_cost():
    return pl.CostEstimate(flops=1024, bytes_accessed=1024, transcendentals=0)


head_spec = pl.BlockSpec(memory_space=pl.ANY)


def head_scratch(rows, width, tiles):
    slots = min(tiles, 16 * megabyte // (2 * rows * width))
    return [pltpu.VMEM((slots, rows, width), jnp.bfloat16), pltpu.SemaphoreType.DMA((slots,))]


class Tiles:
    def __init__(self, head_ref, slots_ref, sems_ref, first_row, skip, tiles):
        self.slots, rows, width = slots_ref.shape
        self.tiles, self.slots_ref = tiles, slots_ref

        def copy(tile):
            slot = lax.rem(tile, self.slots)
            column = pl.multiple_of((tile + skip) * width, width)
            source = head_ref.at[pl.ds(first_row, rows), pl.ds(column, width)]
            return pltpu.make_async_copy(source, slots_ref.at[slot], sems_ref.at[slot])

        self.copy = copy

    def get(self, tile):
        @pl.when(tile == 0)
        def _():
            for first in range(self.slots):
                self.copy(first).start()

        self.copy(tile).wait()
        return self.slots_ref[lax.rem(tile, self.slots)]

    def release(self, tile):
        if self.slots < self.tiles:

            @pl.when(tile + self.slots < self.tiles)
            def _():
                self.copy(tile + self.slots).start()


def constant(*shape):
    return pl.BlockSpec(shape, lambda *_: (0,) * len(shape))


def far_kernel(width, skip, tiles, x_ref, head_ref, first_ref, second_ref, powers_ref, slots_ref, sems_ref):
    tile = pl.program_id(0)
    head = Tiles(head_ref, slots_ref, sems_ref, 0, skip, tiles)
    columns = first_ref.shape[1] - tail
    value = dot(x_ref[...], head.get(tile))
    head.release(tile)
    q = value.shape[0] // 4
    first = jnp.concatenate([value[:q], value[2 * q : 3 * q]], axis=0)
    second = jnp.concatenate([value[q : 2 * q], value[3 * q :]], axis=0)
    put(first_ref, powers_ref, slice(0, 2 * q), tile, width, columns, first)
    put(second_ref, powers_ref, slice(2 * q, 4 * q), tile, width, columns, second)


def far_codes(rows_in, head, width, skip, tiles):
    rows, depth = rows_in.shape
    columns = tiles * width
    return pl.pallas_call(
        functools.partial(far_kernel, width, skip, tiles),
        grid=(tiles,),
        in_specs=[constant(rows, depth), head_spec],
        out_specs=[constant(rows // 2, columns + tail)] * 2,
        out_shape=[jax.ShapeDtypeStruct((rows // 2, columns + tail), jnp.int16)] * 2,
        scratch_shapes=[pltpu.VMEM((rows, tail), jnp.float32)] + head_scratch(depth, width, tiles),
        compiler_params=compiler_params(),
        cost_estimate=small_cost(),
        name="far_codes",
    )(rows_in, head)


def near_kernel(width, skip, tiles, x_ref, y_ref, head_ref, by_x_ref, by_y_ref, *refs):
    to_x_refs, to_y_refs, (powers_ref, slots_ref, sems_ref) = refs[:2], refs[2:4], refs[4:]
    tile = pl.program_id(0)
    head = Tiles(head_ref, slots_ref, sems_ref, 0, skip, tiles)
    rows = x_ref.shape[0]
    columns = tiles * width
    value = dot(jnp.concatenate([x_ref[...], y_ref[...]], axis=0), head.get(tile))
    head.release(tile)
    more_x = decode(by_y_ref, tile, width, columns)
    more_y = decode(by_x_ref, tile, width, columns)
    part, half = rows // 2, rows // 4
    for p in range(2):
        for_x, for_y = value[p * part : (p + 1) * part], value[rows + p * part : rows + (p + 1) * part]
        add = slice(p * half, (p + 1) * half)
        for_x = jnp.concatenate([for_x[:half], for_x[half:] + more_x[add]], axis=0)
        for_y = jnp.concatenate([for_y[:half] + more_y[add], for_y[half:]], axis=0)
        for q, out_ref, out in ((0, to_x_refs[p], for_x), (2, to_y_refs[p], for_y)):
            kept = slice((p + q) * part, (p + q + 1) * part)
            put(out_ref, powers_ref, kept, tile, width, columns, out)


def near_codes(rows_x, rows_y, head, by_x, by_y, width, skip, tiles):
    rows, depth = rows_x.shape[0], head.shape[0]
    columns = tiles * width
    shape = (rows // 2, columns + tail)
    return pl.pallas_call(
        functools.partial(near_kernel, width, skip, tiles),
        grid=(tiles,),
        in_specs=[constant(rows, depth)] * 2 + [head_spec] + [constant(*shape)] * 2,
        out_specs=[constant(*shape)] * 4,
        out_shape=[jax.ShapeDtypeStruct(shape, jnp.int16)] * 4,
        scratch_shapes=[pltpu.VMEM((2 * rows, tail), jnp.float32)] + head_scratch(depth, width, tiles),
        compiler_params=compiler_params(),
        cost_estimate=small_cost(),
        name="near_codes",
    )(rows_x, rows_y, head, by_x, by_y)


def own_kernel(tiles, x_ref, head_ref, out_ref, slots_ref, sems_ref):
    tile = pl.program_id(0)
    head = Tiles(head_ref, slots_ref, sems_ref, 0, 0, tiles)
    out_ref[...] = dot(x_ref[...], head.get(tile))
    head.release(tile)


def own_logits(rows_in, head, width):
    rows, depth = rows_in.shape
    columns = head.shape[1]
    return pl.pallas_call(
        functools.partial(own_kernel, columns // width),
        grid=(columns // width,),
        in_specs=[constant(rows, depth), head_spec],
        out_specs=pl.BlockSpec((rows, width), lambda j: (0, j)),
        out_shape=jax.ShapeDtypeStruct((rows, columns), jnp.float32),
        scratch_shapes=head_scratch(depth, width, columns // width),
        compiler_params=compiler_params(),
        cost_estimate=small_cost(),
        name="own_logits",
    )(rows_in, head)


def members(ids, start, width):
    rows = ids.shape[0]
    column = lax.broadcasted_iota(jnp.int32, (rows, width), 1) + start
    found = column == ids[:, 0:1]
    for k in range(1, ids.shape[1]):
        found = found | (column == ids[:, k : k + 1])
    return found


def stats_kernel(width, parts, *refs):
    own_ref, by_x_refs, by_y_refs = refs[0], refs[1 : 1 + parts], refs[1 + parts : 1 + 2 * parts]
    ids_ref, logits_ref, listed_ref, out_ref = refs[1 + 2 * parts :]
    rows, columns = logits_ref.shape
    each = columns // parts
    ids = ids_ref[...]
    top_all = jnp.full((rows, width), lowest, jnp.float32)
    top_ref = jnp.full((rows, width), lowest, jnp.float32)
    for start in range(0, columns, width):
        at = slice(start, start + width)
        where, inner = start // each, start % each // width
        piece = own_ref[:, at] + decode(by_x_refs[where], inner, width, each)
        piece = piece + decode(by_y_refs[where], inner, width, each)
        listed = jnp.where(members(ids, start, width), piece, lowest)
        logits_ref[:, at] = piece
        listed_ref[:, at] = listed
        top_all = jnp.maximum(top_all, piece)
        top_ref = jnp.maximum(top_ref, listed)
    peak_all = jnp.max(top_all, axis=1, keepdims=True)
    peak_ref = jnp.max(top_ref, axis=1, keepdims=True)
    sum_all = jnp.zeros((rows, width), jnp.float32)
    sum_ref = jnp.zeros((rows, width), jnp.float32)
    for start in range(0, columns, width):
        at = slice(start, start + width)
        sum_all = sum_all + jnp.exp(logits_ref[:, at] - peak_all)
        sum_ref = sum_ref + jnp.exp(listed_ref[:, at] - peak_ref)
    sum_all = jnp.sum(sum_all, axis=1, keepdims=True)
    sum_ref = jnp.sum(sum_ref, axis=1, keepdims=True)
    lane = lax.broadcasted_iota(jnp.int32, out_ref.shape, 1)
    out_ref[...] = jnp.where(
        lane == 0, peak_all, jnp.where(lane == 1, peak_ref, jnp.where(lane == 2, sum_all, sum_ref))
    )


def row_stats(part, own, by_x, by_y, ids, width):
    rows = by_x[0].shape[0]
    parts = len(by_x)
    columns = own.shape[1]
    block = min(rows, 16)
    skip = part * (rows // block)
    across = lambda array: pl.BlockSpec((block, array.shape[1]), lambda i: (i, 0))
    return pl.pallas_call(
        functools.partial(stats_kernel, width, parts),
        grid=(rows // block,),
        in_specs=[pl.BlockSpec((block, columns), lambda i: (i + skip, 0))]
        + [across(a) for a in (*by_x, *by_y)]
        + [pl.BlockSpec((block, ids.shape[1]), lambda i: (i + skip, 0))],
        out_specs=[
            pl.BlockSpec((block, columns), lambda i: (i, 0)),
            pl.BlockSpec((block, columns), lambda i: (i, 0)),
            pl.BlockSpec((block, 128), lambda i: (i, 0)),
        ],
        out_shape=[
            jax.ShapeDtypeStruct((rows, columns), jnp.float32),
            jax.ShapeDtypeStruct((rows, columns), jnp.float32),
            jax.ShapeDtypeStruct((rows, 128), jnp.float32),
        ],
        compiler_params=compiler_params(),
        cost_estimate=small_cost(),
        name="row_stats",
    )(own, *by_x, *by_y, ids)


def grad_kernel(width, logits_ref, listed_ref, stats_ref, scale_ref, out_ref, info_ref):
    rows, columns = logits_ref.shape
    stats = [stats_ref[v] for v in range(stats_ref.shape[0])]
    peaks = functools.reduce(jnp.maximum, [s[:, :2] for s in stats])
    sums = functools.reduce(jnp.add, [s[:, 2:4] * jnp.exp(s[:, :2] - peaks) for s in stats])
    lse = peaks + jnp.log(sums)
    lse_all, lse_ref = lse[:, 0:1], lse[:, 1:2]
    scale = scale_ref[...]
    term = jnp.zeros((rows, width), jnp.float32)
    for start in range(0, columns, width):
        at = slice(start, start + width)
        piece = logits_ref[:, at]
        grad = scale * (jnp.exp(listed_ref[:, at] - lse_ref) - jnp.exp(piece - lse_all))
        grad = grad.astype(jnp.bfloat16)
        out_ref[:, at] = grad
        term = term + grad.astype(jnp.float32) * piece
    lane = lax.broadcasted_iota(jnp.int32, info_ref.shape, 1)
    info_ref[...] = jnp.broadcast_to(lse_ref - lse_all, info_ref.shape)
    term = jnp.sum(term, axis=1, keepdims=True)
    high = term.astype(jnp.bfloat16).astype(jnp.float32)
    middle = (term - high).astype(jnp.bfloat16).astype(jnp.float32)
    low = term - high - middle
    term = jnp.where(lane == 0, high, jnp.where(lane == 1, middle, jnp.where(lane == 2, low, 0.0)))
    out_ref[:, columns:] = term.astype(jnp.bfloat16)


def logit_grads(part, logits, listed, stats, scale, width):
    rows, columns = logits.shape
    block = min(rows, 16)
    skip = part * (rows // block)
    return pl.pallas_call(
        functools.partial(grad_kernel, width),
        grid=(rows // block,),
        in_specs=[
            pl.BlockSpec((block, columns), lambda i: (i, 0)),
            pl.BlockSpec((block, columns), lambda i: (i, 0)),
            pl.BlockSpec((stats.shape[0], block, 128), lambda i: (0, i, 0)),
            pl.BlockSpec((block, 1), lambda i: (i + skip, 0)),
        ],
        out_specs=[
            pl.BlockSpec((block, columns + tail), lambda i: (i, 0)),
            pl.BlockSpec((block, 128), lambda i: (i, 0)),
        ],
        out_shape=[
            jax.ShapeDtypeStruct((rows, columns + tail), jnp.bfloat16),
            jax.ShapeDtypeStruct((rows, 128), jnp.float32),
        ],
        compiler_params=compiler_params(),
        cost_estimate=small_cost(),
        name="logit_grads",
    )(logits, listed, stats, scale)


def put_row(out_ref, value):
    width = value.shape[1] - tail
    code, power = encode(value[:, :width])
    term, term_power = encode(value[:, width : width + 1])
    lane = lax.broadcasted_iota(jnp.int32, (value.shape[0], tail), 1)
    beside = jnp.where(lane == 0, power, jnp.where(lane == 1, term.astype(jnp.int32).astype(jnp.float32), term_power))
    out_ref[:, :width] = code
    out_ref[:, width:] = beside.astype(jnp.int32).astype(jnp.int16)


def take_row(codes_ref):
    width = codes_ref.shape[1] - tail
    beside = codes_ref[:, width:].astype(jnp.int32).astype(jnp.float32)
    value = codes_ref[:, :width].astype(jnp.int32).astype(jnp.float32) * jnp.exp(beside[:, 0:1] * per_step)
    term = beside[:, 1:2] * jnp.exp(beside[:, 2:3] * per_step)
    return value, jnp.broadcast_to(term, beside.shape)


def back_kernel(tiles, keeps, place_ref, grad_ref, beside_ref, head_ref, *refs):
    outs, (total_ref, slots_ref, sems_ref) = refs[:-3], refs[-3:]
    tile = pl.program_id(0)
    rows = slots_ref.shape[1]
    head = Tiles(head_ref, slots_ref, sems_ref, pl.multiple_of(place_ref[0] * rows, rows), 0, tiles)

    @pl.when(tile == 0)
    def _():
        total_ref[...] = jnp.zeros_like(total_ref)

    total_ref[...] += lax.dot_general(
        grad_ref[...], head.get(tile), (((1,), (1,)), ((), ())), preferred_element_type=jnp.float32
    )
    head.release(tile)

    @pl.when(tile == tiles - 1)
    def _():
        term = beside_ref[...].astype(jnp.float32)
        term = jnp.broadcast_to(term[:, 0:1] + term[:, 1:2] + term[:, 2:3], term.shape)
        width = outs[0].shape[1] - tail
        for k, out_ref in enumerate(outs):
            start = pl.multiple_of((place_ref[1] ^ k) * width, width)
            value = total_ref[:, pl.ds(start, width)]
            if k == 0 and keeps:
                out_ref[:, :width] = value
                out_ref[:, width:] = term
            else:
                put_row(out_ref, jnp.concatenate([value, term], axis=1))


def back(grad, head, place, width, group, keeps):
    depth, columns = head.shape
    rows = grad.shape[0]
    blocks = max(group // 2, 1)
    part = depth // group
    types = [jnp.float32 if keeps and k == 0 else jnp.int16 for k in range(blocks)]
    return pl.pallas_call(
        functools.partial(back_kernel, columns // width, keeps),
        grid_spec=pltpu.PrefetchScalarGridSpec(
            num_scalar_prefetch=1,
            grid=(columns // width,),
            in_specs=[
                pl.BlockSpec((rows, width), lambda j, place: (0, j)),
                pl.BlockSpec((rows, tail), lambda j, place: (0, columns // tail)),
                head_spec,
            ],
            out_specs=[constant(rows, part + tail)] * blocks,
            scratch_shapes=[pltpu.VMEM((rows, blocks * part), jnp.float32)]
            + head_scratch(blocks * part, width, columns // width),
        ),
        out_shape=[jax.ShapeDtypeStruct((rows, part + tail), t) for t in types],
        compiler_params=compiler_params(),
        cost_estimate=small_cost(),
        name="grad_rows",
    )(place, grad, grad, head)


def group_kernel(place_ref, keep_ref, *refs):
    total_ref = refs[-1]
    count = place_ref.shape[0] - 1
    out_ref, sends, received = refs[-2 - count], refs[-1 - count : -1], refs[: -2 - count]
    width = keep_ref.shape[1] - tail
    total, term = keep_ref[:, :width], keep_ref[:, width:]
    for codes_ref in received:
        more, more_term = take_row(codes_ref)
        total, term = total + more, term + more_term
    total_ref[:, :width] = total
    total_ref[:, width:] = term
    rows = out_ref.shape[0]
    block = lambda b: total_ref[pl.ds(pl.multiple_of(b * rows, rows), rows), :]
    out_ref[...] = block(place_ref[0])
    for k, send_ref in enumerate(sends, 1):
        put_row(send_ref, block(place_ref[k]))


def group_sum(place, keep, received):
    blocks = place.shape[0]
    rows, width = keep.shape
    each = (rows // blocks, width)
    return pl.pallas_call(
        group_kernel,
        in_specs=[pl.BlockSpec(memory_space=pltpu.SMEM)]
        + [pl.BlockSpec(memory_space=pltpu.VMEM)] * (1 + len(received)),
        out_specs=[pl.BlockSpec(memory_space=pltpu.VMEM)] * blocks,
        out_shape=[jax.ShapeDtypeStruct(each, jnp.float32)]
        + [jax.ShapeDtypeStruct(each, jnp.int16)] * (blocks - 1),
        scratch_shapes=[pltpu.VMEM((rows, width), jnp.float32)],
        compiler_params=compiler_params(),
        cost_estimate=small_cost(),
        name="group_sum",
    )(place, keep, *received)


def last_kernel(keep_ref, *refs):
    width = keep_ref.shape[1] - tail
    total, term = keep_ref[:, :width], keep_ref[:, width:]
    for codes_ref in refs[:-1]:
        more, more_term = take_row(codes_ref)
        total, term = total + more, term + more_term
    put_row(refs[-1], jnp.concatenate([total, term], axis=1))


def last_sum(keep, received):
    return pl.pallas_call(
        last_kernel,
        in_specs=[pl.BlockSpec(memory_space=pltpu.VMEM)] * (1 + len(received)),
        out_specs=pl.BlockSpec(memory_space=pltpu.VMEM),
        out_shape=jax.ShapeDtypeStruct(keep.shape, jnp.int16),
        compiler_params=compiler_params(),
        cost_estimate=small_cost(),
        name="last_sum",
    )(keep, *received)


def after(value, *others):
    return lax.optimization_barrier((value, *others))[0]


def shards(hidden, head, gain, refusal_ids, refusal_count, loss_scale):
    row_count, model_width = hidden.shape
    depth, vocab_local = head.shape
    list_length = refusal_ids.shape[1]
    prompt_size = lax.axis_size("prompt")
    vocab_size = lax.axis_size("vocab")
    group = vocab_size // prompt_size
    width = min(1024, vocab_local // 2)
    tiles = vocab_local // width
    half = row_count // 2
    me = lax.axis_index("prompt")
    shard = lax.axis_index("vocab")
    to_x, to_y, to_far = ([(p, p ^ k) for p in range(prompt_size)] for k in (1, 2, 3))
    send = lambda value, pairs: lax.ppermute(value, "prompt", pairs)

    hidden_f = hidden.astype(jnp.float32)
    inverse_rms = lax.rsqrt(jnp.mean(hidden_f * hidden_f, axis=1, keepdims=True) + epsilon)
    normed = (hidden_f * inverse_rms * gain).astype(jnp.bfloat16)
    columns = lambda p: lax.dynamic_slice_in_dim(normed, p * depth, depth, 1)
    rows_far = send(columns(me ^ 3), to_far)
    beside = ((0, 0), (0, tail))
    rows_x = send(jnp.pad(columns(me ^ 1), beside), to_x)
    rows_y = send(jnp.pad(columns(me ^ 2), beside), to_y)
    own = own_logits(columns(me), head, width)
    first_tiles = tiles // 2
    column_parts = ((0, first_tiles), (first_tiles, tiles - first_tiles))
    by_x, by_y = [], []
    for (skip, count), waits in zip(column_parts, ([own], [rows_x, rows_y])):
        first, second = far_codes(after(rows_far, *waits), head, width, skip, count)
        by_x.append(send(first, to_x))
        by_y.append(send(second, to_y))
    codes = [
        near_codes(rows_x, rows_y, head, by_x[c], by_y[c], width, skip, count)
        for c, (skip, count) in enumerate(column_parts)
    ]
    halves = []
    for part in range(2):
        waits = codes[1][:1] if part else []
        sums_x = [send(after(c[part], *waits), to_x) for c in codes]
        sums_y = [send(after(c[2 + part], *waits), to_y) for c in codes]
        halves.append((sums_x, sums_y))

    in_list = jnp.arange(list_length)[None, :] < refusal_count[:, None]
    ids = jnp.where(in_list, refusal_ids - shard * vocab_local, -1)

    block, member = shard // group, shard % group
    spread = max(group // 2, 1)
    place_other = jnp.stack([(member // spread) ^ 1, member % spread]).astype(jnp.int32)
    place_mine = jnp.stack([member // spread, member % spread]).astype(jnp.int32)
    place_block = jnp.stack([block ^ k ^ me for k in range(prompt_size)]).astype(jnp.int32)
    to_member = [[(v, v ^ k) for v in range(vocab_size)] for k in range(1, group)]
    to_block = [
        [(v, ((v // group) ^ k) * group + v % group) for v in range(vocab_size)]
        for k in range(1, prompt_size)
    ]
    moves = []
    for p in range(prompt_size):
        for r in range(prompt_size):
            for i in range(group):
                moves.append((p * vocab_size + r * group + i, r * vocab_size + p * group + i))

    quarter = half // 2
    infos, grads = [], []
    for part, (sums_x, sums_y) in enumerate(halves):
        logits, listed, stats = row_stats(part, own, sums_x, sums_y, after(ids, *infos), width)
        stats = lax.all_gather(stats, "vocab", axis=0)
        grad, info = logit_grads(part, logits, listed, stats, loss_scale[:, None], width)
        infos.append(info)
        grads.append(grad)
    log_refusal = jnp.concatenate([info[:, 0] for info in infos])

    def neighbours(grad, *waits):
        sent = after(grad, *waits)
        return grad, send(sent, to_x), send(sent, to_y)

    def diagonal(grad_x, grad_y, *waits):
        passed_x, passed_y = after(grad_y, *waits)[:quarter], after(grad_x, *waits)[quarter:]
        return (passed_x, passed_y), [send(passed_x, to_x), send(passed_y, to_y)]

    def gradient(rows, waits_other=(), waits_mine=()):
        rows = jnp.concatenate(rows)
        others = back(rows, head, after(place_other, *waits_other), width, group, False)
        received = [lax.ppermute(c, "vocab", to) for c, to in zip(others, to_member[spread - 1 :])]
        keep, *codes = back(rows, head, after(place_mine, *others, *waits_mine), width, group, True)
        received += [lax.ppermute(c, "vocab", to) for c, to in zip(codes, to_member)]
        return keep, received

    def blocks(keep, received, *waits):
        keep, *codes = group_sum(after(place_block, *waits), keep, received)
        return keep, [lax.ppermute(c, "vocab", to) for c, to in zip(codes, to_block)]

    rows_a = neighbours(grads[0])
    _, far_a = diagonal(*rows_a[1:], infos[1])
    rows_b = neighbours(grads[1], *far_a)
    keep_a, received_a = gradient((*rows_a, *far_a))
    passed, far_b = diagonal(*rows_b[1:], keep_a)
    keep_a, received_a = blocks(keep_a, received_a, *passed)
    sum_a = last_sum(keep_a, received_a)
    keep_b, received_b = gradient((*rows_b, *far_b), received_a, [sum_a])
    sum_b = last_sum(*blocks(keep_b, received_b))
    grad_cols = [lax.ppermute(total, ("prompt", "vocab"), moves) for total in (sum_a, sum_b)]

    slice_width = model_width // vocab_size
    col_start = shard * slice_width
    codes = jnp.concatenate(grad_cols)
    power = codes[:, slice_width : slice_width + 1].astype(jnp.float32)
    grad_cols = codes[:, :slice_width].astype(jnp.float32) * jnp.exp(power * per_step)
    term = codes[:, slice_width + 1 : slice_width + 3].astype(jnp.float32)
    row_term = term[:, 0] * jnp.exp(term[:, 1] * per_step)
    hidden_cols = lax.dynamic_slice_in_dim(hidden, col_start, slice_width, 1).astype(jnp.float32)
    gain_cols = lax.dynamic_slice_in_dim(gain, col_start, slice_width, 0)
    grad_hidden = (
        inverse_rms * gain_cols * grad_cols
        - hidden_cols * (inverse_rms * inverse_rms / model_width) * row_term[:, None]
    )
    return (grad_hidden, log_refusal)


def solution(mesh):
    return jax.shard_map(
        shards,
        mesh=mesh,
        in_specs=(
            P("prompt", None),
            P("prompt", "vocab"),
            P(),
            P("prompt", None),
            P("prompt"),
            P("prompt"),
        ),
        out_specs=(P("prompt", "vocab"), P("prompt")),
        check_vma=False,
    )
```

```python
import functools
import math

import jax
import jax.numpy as jnp
from jax import lax
from jax.experimental import pallas as pl
from jax.experimental.pallas import tpu as pltpu
from jax.sharding import PartitionSpec as P

epsilon = 1e-05
lowest = -1e30
tail = 128
steps = 64
code_top = 32000.0
per_step = math.log(2.0) / steps
megabyte = 1024 * 1024


def encode(value):
    top = jnp.max(jnp.abs(value), axis=1, keepdims=True)
    power = jnp.ceil(jnp.log(jnp.maximum(top, 1e-30) * (1.0 / code_top)) * (1.0 / per_step))
    code = jnp.round(value * jnp.exp(power * -per_step))
    return code.astype(jnp.int32).astype(jnp.int16), power


def decode(codes_ref, tile, width, vocab_local, rows=slice(None)):
    powers = codes_ref[rows, vocab_local : vocab_local + tail].astype(jnp.int32).astype(jnp.float32)
    lane = lax.broadcasted_iota(jnp.int32, powers.shape, 1)
    power = jnp.sum(jnp.where(lane == tile, powers, 0.0), axis=1, keepdims=True)
    start = tile * width
    if not isinstance(start, int):
        start = pl.multiple_of(start, width)
    codes = codes_ref[rows, pl.ds(start, width)].astype(jnp.int32).astype(jnp.float32)
    return codes * jnp.exp(power * per_step)


def put(out_ref, powers_ref, rows, tile, width, vocab_local, value):
    code, power = encode(value)
    out_ref[:, pl.ds(pl.multiple_of(tile * width, width), width)] = code
    lane = lax.broadcasted_iota(jnp.int32, (value.shape[0], tail), 1)
    powers = jnp.where(lane >= tile, power, powers_ref[rows, :])
    powers_ref[rows, :] = powers
    out_ref[:, vocab_local:] = powers.astype(jnp.int32).astype(jnp.int16)


def dot(a, b):
    return jnp.dot(a, b, preferred_element_type=jnp.float32)


def compiler_params():
    return pltpu.CompilerParams(vmem_limit_bytes=24 * megabyte)


def small_cost():
    return pl.CostEstimate(flops=1024, bytes_accessed=1024, transcendentals=0)


head_spec = pl.BlockSpec(memory_space=pl.ANY)


def head_scratch(rows, width, tiles):
    slots = min(tiles, 12 * megabyte // (2 * rows * width))
    return [pltpu.VMEM((slots, rows, width), jnp.bfloat16), pltpu.SemaphoreType.DMA((slots,))]


class Tiles:
    def __init__(self, head_ref, slots_ref, sems_ref, first_row, skip, tiles):
        self.slots, rows, width = slots_ref.shape
        self.tiles, self.slots_ref = tiles, slots_ref

        def copy(tile):
            slot = lax.rem(tile, self.slots)
            column = pl.multiple_of((tile + skip) * width, width)
            source = head_ref.at[pl.ds(first_row, rows), pl.ds(column, width)]
            return pltpu.make_async_copy(source, slots_ref.at[slot], sems_ref.at[slot])

        self.copy = copy

    def get(self, tile):
        @pl.when(tile == 0)
        def _():
            for first in range(self.slots):
                self.copy(first).start()

        self.copy(tile).wait()
        return self.slots_ref[lax.rem(tile, self.slots)]

    def release(self, tile):
        if self.slots < self.tiles:

            @pl.when(tile + self.slots < self.tiles)
            def _():
                self.copy(tile + self.slots).start()


def constant(*shape):
    return pl.BlockSpec(shape, lambda *_: (0,) * len(shape))


def far_kernel(width, skip, tiles, x_ref, head_ref, first_ref, second_ref, powers_ref, slots_ref, sems_ref):
    tile = pl.program_id(0)
    head = Tiles(head_ref, slots_ref, sems_ref, 0, skip, tiles)
    columns = first_ref.shape[1] - tail
    value = dot(x_ref[...], head.get(tile))
    head.release(tile)
    q = value.shape[0] // 4
    first = jnp.concatenate([value[:q], value[2 * q : 3 * q]], axis=0)
    second = jnp.concatenate([value[q : 2 * q], value[3 * q :]], axis=0)
    put(first_ref, powers_ref, slice(0, 2 * q), tile, width, columns, first)
    put(second_ref, powers_ref, slice(2 * q, 4 * q), tile, width, columns, second)


def far_codes(rows_in, head, width, skip, tiles):
    rows, depth = rows_in.shape[0], head.shape[0]
    columns = tiles * width
    return pl.pallas_call(
        functools.partial(far_kernel, width, skip, tiles),
        grid=(tiles,),
        in_specs=[constant(rows, depth), head_spec],
        out_specs=[constant(rows // 2, columns + tail)] * 2,
        out_shape=[jax.ShapeDtypeStruct((rows // 2, columns + tail), jnp.int16)] * 2,
        scratch_shapes=[pltpu.VMEM((rows, tail), jnp.float32)] + head_scratch(depth, width, tiles),
        compiler_params=compiler_params(),
        cost_estimate=small_cost(),
        name="far_codes",
    )(rows_in, head)


def near_kernel(width, skip, tiles, x_ref, y_ref, head_ref, by_x_ref, by_y_ref, *refs):
    to_x_refs, to_y_refs, (powers_ref, slots_ref, sems_ref) = refs[:2], refs[2:4], refs[4:]
    tile = pl.program_id(0)
    head = Tiles(head_ref, slots_ref, sems_ref, 0, skip, tiles)
    rows = x_ref.shape[0]
    columns = tiles * width
    value = dot(jnp.concatenate([x_ref[...], y_ref[...]], axis=0), head.get(tile))
    head.release(tile)
    more_x = decode(by_y_ref, tile, width, columns)
    more_y = decode(by_x_ref, tile, width, columns)
    part, half = rows // 2, rows // 4
    for p in range(2):
        for_x, for_y = value[p * part : (p + 1) * part], value[rows + p * part : rows + (p + 1) * part]
        add = slice(p * half, (p + 1) * half)
        for_x = jnp.concatenate([for_x[:half], for_x[half:] + more_x[add]], axis=0)
        for_y = jnp.concatenate([for_y[:half] + more_y[add], for_y[half:]], axis=0)
        for q, out_ref, out in ((0, to_x_refs[p], for_x), (2, to_y_refs[p], for_y)):
            kept = slice((p + q) * part, (p + q + 1) * part)
            put(out_ref, powers_ref, kept, tile, width, columns, out)


def near_codes(rows_x, rows_y, head, by_x, by_y, width, skip, tiles):
    rows, depth = rows_x.shape[0], head.shape[0]
    columns = tiles * width
    shape = (rows // 2, columns + tail)
    return pl.pallas_call(
        functools.partial(near_kernel, width, skip, tiles),
        grid=(tiles,),
        in_specs=[constant(rows, depth)] * 2 + [head_spec] + [constant(*shape)] * 2,
        out_specs=[constant(*shape)] * 4,
        out_shape=[jax.ShapeDtypeStruct(shape, jnp.int16)] * 4,
        scratch_shapes=[pltpu.VMEM((2 * rows, tail), jnp.float32)] + head_scratch(depth, width, tiles),
        compiler_params=compiler_params(),
        cost_estimate=small_cost(),
        name="near_codes",
    )(rows_x, rows_y, head, by_x, by_y)


def own_kernel(tiles, x_ref, head_ref, out_ref, slots_ref, sems_ref):
    tile = pl.program_id(0)
    head = Tiles(head_ref, slots_ref, sems_ref, 0, 0, tiles)
    out_ref[...] = dot(x_ref[...], head.get(tile))
    head.release(tile)


def own_logits(rows_in, head, width):
    rows, depth = rows_in.shape
    columns = head.shape[1]
    return pl.pallas_call(
        functools.partial(own_kernel, columns // width),
        grid=(columns // width,),
        in_specs=[constant(rows, depth), head_spec],
        out_specs=pl.BlockSpec((rows, width), lambda j: (0, j)),
        out_shape=jax.ShapeDtypeStruct((rows, columns), jnp.float32),
        scratch_shapes=head_scratch(depth, width, columns // width),
        compiler_params=compiler_params(),
        cost_estimate=small_cost(),
        name="own_logits",
    )(rows_in, head)


def members(ids, start, width):
    rows = ids.shape[0]
    column = lax.broadcasted_iota(jnp.int32, (rows, width), 1) + start
    found = column == ids[:, 0:1]
    for k in range(1, ids.shape[1]):
        found = found | (column == ids[:, k : k + 1])
    return found


def stats_kernel(width, parts, *refs):
    own_ref, by_x_refs, by_y_refs = refs[0], refs[1 : 1 + parts], refs[1 + parts : 1 + 2 * parts]
    ids_ref, logits_ref, listed_ref, out_ref = refs[1 + 2 * parts :]
    rows, columns = logits_ref.shape
    each = columns // parts
    ids = ids_ref[...]
    top_all = jnp.full((rows, width), lowest, jnp.float32)
    top_ref = jnp.full((rows, width), lowest, jnp.float32)
    for start in range(0, columns, width):
        at = slice(start, start + width)
        where, inner = start // each, start % each // width
        piece = own_ref[:, at] + decode(by_x_refs[where], inner, width, each)
        piece = piece + decode(by_y_refs[where], inner, width, each)
        listed = jnp.where(members(ids, start, width), piece, lowest)
        logits_ref[:, at] = piece
        listed_ref[:, at] = listed
        top_all = jnp.maximum(top_all, piece)
        top_ref = jnp.maximum(top_ref, listed)
    peak_all = jnp.max(top_all, axis=1, keepdims=True)
    peak_ref = jnp.max(top_ref, axis=1, keepdims=True)
    sum_all = jnp.zeros((rows, width), jnp.float32)
    sum_ref = jnp.zeros((rows, width), jnp.float32)
    for start in range(0, columns, width):
        at = slice(start, start + width)
        sum_all = sum_all + jnp.exp(logits_ref[:, at] - peak_all)
        sum_ref = sum_ref + jnp.exp(listed_ref[:, at] - peak_ref)
    sum_all = jnp.sum(sum_all, axis=1, keepdims=True)
    sum_ref = jnp.sum(sum_ref, axis=1, keepdims=True)
    lane = lax.broadcasted_iota(jnp.int32, out_ref.shape, 1)
    out_ref[...] = jnp.where(
        lane == 0, peak_all, jnp.where(lane == 1, peak_ref, jnp.where(lane == 2, sum_all, sum_ref))
    )


def row_stats(part, own, by_x, by_y, ids, width):
    rows = by_x[0].shape[0]
    parts = len(by_x)
    columns = own.shape[1]
    block = min(rows, 16)
    skip = part * (rows // block)
    across = lambda array: pl.BlockSpec((block, array.shape[1]), lambda i: (i, 0))
    return pl.pallas_call(
        functools.partial(stats_kernel, width, parts),
        grid=(rows // block,),
        in_specs=[pl.BlockSpec((block, columns), lambda i: (i + skip, 0))]
        + [across(a) for a in (*by_x, *by_y)]
        + [pl.BlockSpec((block, ids.shape[1]), lambda i: (i + skip, 0))],
        out_specs=[
            pl.BlockSpec((block, columns), lambda i: (i, 0)),
            pl.BlockSpec((block, columns), lambda i: (i, 0)),
            pl.BlockSpec((block, 128), lambda i: (i, 0)),
        ],
        out_shape=[
            jax.ShapeDtypeStruct((rows, columns), jnp.float32),
            jax.ShapeDtypeStruct((rows, columns), jnp.float32),
            jax.ShapeDtypeStruct((rows, 128), jnp.float32),
        ],
        compiler_params=compiler_params(),
        cost_estimate=small_cost(),
        name="row_stats",
    )(own, *by_x, *by_y, ids)


def grad_kernel(width, logits_ref, listed_ref, stats_ref, scale_ref, out_ref, info_ref):
    rows, columns = logits_ref.shape
    stats = [stats_ref[v] for v in range(stats_ref.shape[0])]
    peaks = functools.reduce(jnp.maximum, [s[:, :2] for s in stats])
    sums = functools.reduce(jnp.add, [s[:, 2:4] * jnp.exp(s[:, :2] - peaks) for s in stats])
    lse = peaks + jnp.log(sums)
    lse_all, lse_ref = lse[:, 0:1], lse[:, 1:2]
    scale = scale_ref[...]
    term = jnp.zeros((rows, width), jnp.float32)
    for start in range(0, columns, width):
        at = slice(start, start + width)
        piece = logits_ref[:, at]
        grad = scale * (jnp.exp(listed_ref[:, at] - lse_ref) - jnp.exp(piece - lse_all))
        grad = grad.astype(jnp.bfloat16)
        out_ref[:, at] = grad
        term = term + grad.astype(jnp.float32) * piece
    lane = lax.broadcasted_iota(jnp.int32, info_ref.shape, 1)
    info_ref[...] = jnp.broadcast_to(lse_ref - lse_all, info_ref.shape)
    term = jnp.sum(term, axis=1, keepdims=True)
    high = term.astype(jnp.bfloat16).astype(jnp.float32)
    middle = (term - high).astype(jnp.bfloat16).astype(jnp.float32)
    low = term - high - middle
    term = jnp.where(lane == 0, high, jnp.where(lane == 1, middle, jnp.where(lane == 2, low, 0.0)))
    out_ref[:, columns:] = term.astype(jnp.bfloat16)


def logit_grads(part, logits, listed, stats, scale, width):
    rows, columns = logits.shape
    block = min(rows, 16)
    skip = part * (rows // block)
    return pl.pallas_call(
        functools.partial(grad_kernel, width),
        grid=(rows // block,),
        in_specs=[
            pl.BlockSpec((block, columns), lambda i: (i, 0)),
            pl.BlockSpec((block, columns), lambda i: (i, 0)),
            pl.BlockSpec((stats.shape[0], block, 128), lambda i: (0, i, 0)),
            pl.BlockSpec((block, 1), lambda i: (i + skip, 0)),
        ],
        out_specs=[
            pl.BlockSpec((block, columns + tail), lambda i: (i, 0)),
            pl.BlockSpec((block, 128), lambda i: (i, 0)),
        ],
        out_shape=[
            jax.ShapeDtypeStruct((rows, columns + tail), jnp.bfloat16),
            jax.ShapeDtypeStruct((rows, 128), jnp.float32),
        ],
        compiler_params=compiler_params(),
        cost_estimate=small_cost(),
        name="logit_grads",
    )(logits, listed, stats, scale)


def put_row(out_ref, value):
    width = value.shape[1] - tail
    code, power = encode(value[:, :width])
    term, term_power = encode(value[:, width : width + 1])
    lane = lax.broadcasted_iota(jnp.int32, (value.shape[0], tail), 1)
    beside = jnp.where(lane == 0, power, jnp.where(lane == 1, term.astype(jnp.int32).astype(jnp.float32), term_power))
    out_ref[:, :width] = code
    out_ref[:, width:] = beside.astype(jnp.int32).astype(jnp.int16)


def take_row(codes_ref):
    width = codes_ref.shape[1] - tail
    beside = codes_ref[:, width:].astype(jnp.int32).astype(jnp.float32)
    value = codes_ref[:, :width].astype(jnp.int32).astype(jnp.float32) * jnp.exp(beside[:, 0:1] * per_step)
    term = beside[:, 1:2] * jnp.exp(beside[:, 2:3] * per_step)
    return value, jnp.broadcast_to(term, beside.shape)


def back_kernel(tiles, keeps, place_ref, grad_ref, beside_ref, head_ref, *refs):
    outs, (total_ref, slots_ref, sems_ref) = refs[:-3], refs[-3:]
    tile = pl.program_id(0)
    rows = slots_ref.shape[1]
    head = Tiles(head_ref, slots_ref, sems_ref, pl.multiple_of(place_ref[0] * rows, rows), 0, tiles)

    @pl.when(tile == 0)
    def _():
        total_ref[...] = jnp.zeros_like(total_ref)

    total_ref[...] += lax.dot_general(
        grad_ref[...], head.get(tile), (((1,), (1,)), ((), ())), preferred_element_type=jnp.float32
    )
    head.release(tile)

    @pl.when(tile == tiles - 1)
    def _():
        term = beside_ref[...].astype(jnp.float32)
        term = jnp.broadcast_to(term[:, 0:1] + term[:, 1:2] + term[:, 2:3], term.shape)
        width = outs[0].shape[1] - tail
        for k, out_ref in enumerate(outs):
            start = pl.multiple_of((place_ref[1] ^ k) * width, width)
            value = total_ref[:, pl.ds(start, width)]
            if k == 0 and keeps:
                out_ref[:, :width] = value
                out_ref[:, width:] = term
            else:
                put_row(out_ref, jnp.concatenate([value, term], axis=1))


def back(grad, head, place, width, group, keeps):
    depth, columns = head.shape
    rows = grad.shape[0]
    blocks = max(group // 2, 1)
    part = depth // group
    types = [jnp.float32 if keeps and k == 0 else jnp.int16 for k in range(blocks)]
    return pl.pallas_call(
        functools.partial(back_kernel, columns // width, keeps),
        grid_spec=pltpu.PrefetchScalarGridSpec(
            num_scalar_prefetch=1,
            grid=(columns // width,),
            in_specs=[
                pl.BlockSpec((rows, width), lambda j, place: (0, j)),
                pl.BlockSpec((rows, tail), lambda j, place: (0, columns // tail)),
                head_spec,
            ],
            out_specs=[constant(rows, part + tail)] * blocks,
            scratch_shapes=[pltpu.VMEM((rows, blocks * part), jnp.float32)]
            + head_scratch(blocks * part, width, columns // width),
        ),
        out_shape=[jax.ShapeDtypeStruct((rows, part + tail), t) for t in types],
        compiler_params=compiler_params(),
        cost_estimate=small_cost(),
        name="grad_rows",
    )(place, grad, grad, head)


def group_kernel(place_ref, keep_ref, *refs):
    total_ref = refs[-1]
    count = place_ref.shape[0] - 1
    out_ref, sends, received = refs[-2 - count], refs[-1 - count : -1], refs[: -2 - count]
    width = keep_ref.shape[1] - tail
    total, term = keep_ref[:, :width], keep_ref[:, width:]
    for codes_ref in received:
        more, more_term = take_row(codes_ref)
        total, term = total + more, term + more_term
    total_ref[:, :width] = total
    total_ref[:, width:] = term
    rows = out_ref.shape[0]
    block = lambda b: total_ref[pl.ds(pl.multiple_of(b * rows, rows), rows), :]
    out_ref[...] = block(place_ref[0])
    for k, send_ref in enumerate(sends, 1):
        put_row(send_ref, block(place_ref[k]))


def group_sum(place, keep, received):
    blocks = place.shape[0]
    rows, width = keep.shape
    each = (rows // blocks, width)
    return pl.pallas_call(
        group_kernel,
        in_specs=[pl.BlockSpec(memory_space=pltpu.SMEM)]
        + [pl.BlockSpec(memory_space=pltpu.VMEM)] * (1 + len(received)),
        out_specs=[pl.BlockSpec(memory_space=pltpu.VMEM)] * blocks,
        out_shape=[jax.ShapeDtypeStruct(each, jnp.float32)]
        + [jax.ShapeDtypeStruct(each, jnp.int16)] * (blocks - 1),
        scratch_shapes=[pltpu.VMEM((rows, width), jnp.float32)],
        compiler_params=compiler_params(),
        cost_estimate=small_cost(),
        name="group_sum",
    )(place, keep, *received)


def last_kernel(keep_ref, *refs):
    width = keep_ref.shape[1] - tail
    total, term = keep_ref[:, :width], keep_ref[:, width:]
    for codes_ref in refs[:-1]:
        more, more_term = take_row(codes_ref)
        total, term = total + more, term + more_term
    put_row(refs[-1], jnp.concatenate([total, term], axis=1))


def last_sum(keep, received):
    return pl.pallas_call(
        last_kernel,
        in_specs=[pl.BlockSpec(memory_space=pltpu.VMEM)] * (1 + len(received)),
        out_specs=pl.BlockSpec(memory_space=pltpu.VMEM),
        out_shape=jax.ShapeDtypeStruct(keep.shape, jnp.int16),
        compiler_params=compiler_params(),
        cost_estimate=small_cost(),
        name="last_sum",
    )(keep, *received)


def after(value, *others):
    return lax.optimization_barrier((value, *others))[0]


def shards(hidden, head, gain, refusal_ids, refusal_count, loss_scale):
    row_count, model_width = hidden.shape
    depth, vocab_local = head.shape
    list_length = refusal_ids.shape[1]
    prompt_size = lax.axis_size("prompt")
    vocab_size = lax.axis_size("vocab")
    group = vocab_size // prompt_size
    width = min(1024, vocab_local // 2)
    tiles = vocab_local // width
    half = row_count // 2
    me = lax.axis_index("prompt")
    shard = lax.axis_index("vocab")
    to_x, to_y, to_far = ([(p, p ^ k) for p in range(prompt_size)] for k in (1, 2, 3))
    send = lambda value, pairs: lax.ppermute(value, "prompt", pairs)

    hidden_f = hidden.astype(jnp.float32)
    inverse_rms = lax.rsqrt(jnp.mean(hidden_f * hidden_f, axis=1, keepdims=True) + epsilon)
    normed = (hidden_f * inverse_rms * gain).astype(jnp.bfloat16)
    columns = lambda p: lax.dynamic_slice_in_dim(normed, p * depth, depth, 1)
    wider = lambda p, more: jnp.pad(columns(p), ((0, 0), (0, more)))
    rows_far = send(wider(me ^ 3, 2 * tail), to_far)
    rows_x = send(wider(me ^ 1, tail), to_x)
    rows_y = send(wider(me ^ 2, tail), to_y)
    own = own_logits(columns(me), head, width)
    first_tiles = tiles // 2
    column_parts = ((0, first_tiles), (first_tiles, tiles - first_tiles))
    by_x, by_y = [], []
    for (skip, count), waits in zip(column_parts, ([own], [rows_x, rows_y])):
        first, second = far_codes(after(rows_far, *waits), head, width, skip, count)
        by_x.append(send(first, to_x))
        by_y.append(send(second, to_y))
    codes = [
        near_codes(rows_x, rows_y, head, by_x[c], by_y[c], width, skip, count)
        for c, (skip, count) in enumerate(column_parts)
    ]
    halves = []
    for part in range(2):
        waits = [codes[1][0], sums_x[0], sums_y[0]] if part else []
        sums_x = [send(after(c[part], *waits), to_x) for c in codes]
        sums_y = [send(after(c[2 + part], *waits), to_y) for c in codes]
        halves.append((sums_x, sums_y))

    in_list = jnp.arange(list_length)[None, :] < refusal_count[:, None]
    ids = jnp.where(in_list, refusal_ids - shard * vocab_local, -1)

    block, member = shard // group, shard % group
    spread = max(group // 2, 1)
    place_other = jnp.stack([(member // spread) ^ 1, member % spread]).astype(jnp.int32)
    place_mine = jnp.stack([member // spread, member % spread]).astype(jnp.int32)
    place_block = jnp.stack([block ^ k ^ me for k in range(prompt_size)]).astype(jnp.int32)
    to_member = [[(v, v ^ k) for v in range(vocab_size)] for k in range(1, group)]
    to_block = [
        [(v, ((v // group) ^ k) * group + v % group) for v in range(vocab_size)]
        for k in range(1, prompt_size)
    ]
    moves = []
    for p in range(prompt_size):
        for r in range(prompt_size):
            for i in range(group):
                moves.append((p * vocab_size + r * group + i, r * vocab_size + p * group + i))

    quarter = half // 2
    infos, grads = [], []
    for part, (sums_x, sums_y) in enumerate(halves):
        logits, listed, stats = row_stats(part, own, sums_x, sums_y, after(ids, *infos), width)
        stats = lax.all_gather(stats, "vocab", axis=0)
        grad, info = logit_grads(part, logits, listed, stats, loss_scale[:, None], width)
        infos.append(info)
        grads.append(grad)
    log_refusal = jnp.concatenate([info[:, 0] for info in infos])

    def neighbours(grad, *waits):
        sent = after(grad, *waits)
        return grad, send(sent, to_x), send(sent, to_y)

    def diagonal(grad_x, grad_y, *waits):
        passed_x, passed_y = after(grad_y, *waits)[:quarter], after(grad_x, *waits)[quarter:]
        return (passed_x, passed_y), [send(passed_x, to_x), send(passed_y, to_y)]

    def gradient(rows, waits_other=(), waits_mine=()):
        rows = jnp.concatenate(rows)
        others = back(rows, head, after(place_other, *waits_other), width, group, False)
        received = [lax.ppermute(c, "vocab", to) for c, to in zip(others, to_member[spread - 1 :])]
        keep, *codes = back(rows, head, after(place_mine, *others, *waits_mine), width, group, True)
        received += [lax.ppermute(c, "vocab", to) for c, to in zip(codes, to_member)]
        return keep, received

    def blocks(keep, received, *waits):
        keep, *codes = group_sum(after(place_block, *waits), keep, received)
        return keep, [lax.ppermute(c, "vocab", to) for c, to in zip(codes, to_block)]

    rows_a = neighbours(grads[0])
    _, far_a = diagonal(*rows_a[1:], infos[1])
    rows_b = neighbours(grads[1], *far_a)
    keep_a, received_a = gradient((*rows_a, *far_a))
    passed, far_b = diagonal(*rows_b[1:], keep_a)
    keep_a, received_a = blocks(keep_a, received_a, *passed)
    sum_a = last_sum(keep_a, received_a)
    keep_b, received_b = gradient((*rows_b, *far_b), received_a, [sum_a])
    sum_b = last_sum(*blocks(keep_b, received_b))
    grad_cols = [lax.ppermute(total, ("prompt", "vocab"), moves) for total in (sum_a, sum_b)]

    slice_width = model_width // vocab_size
    col_start = shard * slice_width
    codes = jnp.concatenate(grad_cols)
    power = codes[:, slice_width : slice_width + 1].astype(jnp.float32)
    grad_cols = codes[:, :slice_width].astype(jnp.float32) * jnp.exp(power * per_step)
    term = codes[:, slice_width + 1 : slice_width + 3].astype(jnp.float32)
    row_term = term[:, 0] * jnp.exp(term[:, 1] * per_step)
    hidden_cols = lax.dynamic_slice_in_dim(hidden, col_start, slice_width, 1).astype(jnp.float32)
    gain_cols = lax.dynamic_slice_in_dim(gain, col_start, slice_width, 0)
    grad_hidden = (
        inverse_rms * gain_cols * grad_cols
        - hidden_cols * (inverse_rms * inverse_rms / model_width) * row_term[:, None]
    )
    return (grad_hidden, log_refusal)


def solution(mesh):
    return jax.shard_map(
        shards,
        mesh=mesh,
        in_specs=(
            P("prompt", None),
            P("prompt", "vocab"),
            P(),
            P("prompt", None),
            P("prompt"),
            P("prompt"),
        ),
        out_specs=(P("prompt", "vocab"), P("prompt")),
        check_vma=False,
    )
```

```python
import functools
import math

import jax
import jax.numpy as jnp
from jax import lax
from jax.experimental import pallas as pl
from jax.experimental.pallas import tpu as pltpu
from jax.sharding import PartitionSpec as P

epsilon = 1e-05
lowest = -1e30
tail = 128
steps = 64
code_top = 32000.0
per_step = math.log(2.0) / steps
megabyte = 1024 * 1024


def encode(value):
    top = jnp.max(jnp.abs(value), axis=1, keepdims=True)
    power = jnp.ceil(jnp.log(jnp.maximum(top, 1e-30) * (1.0 / code_top)) * (1.0 / per_step))
    code = jnp.round(value * jnp.exp(power * -per_step))
    return code.astype(jnp.int32).astype(jnp.int16), power


def decode(codes_ref, tile, width, vocab_local, rows=slice(None)):
    powers = codes_ref[rows, vocab_local : vocab_local + tail].astype(jnp.int32).astype(jnp.float32)
    lane = lax.broadcasted_iota(jnp.int32, powers.shape, 1)
    power = jnp.sum(jnp.where(lane == tile, powers, 0.0), axis=1, keepdims=True)
    start = tile * width
    if not isinstance(start, int):
        start = pl.multiple_of(start, width)
    codes = codes_ref[rows, pl.ds(start, width)].astype(jnp.int32).astype(jnp.float32)
    return codes * jnp.exp(power * per_step)


def put(out_ref, powers_ref, rows, tile, width, vocab_local, value):
    code, power = encode(value)
    out_ref[:, pl.ds(pl.multiple_of(tile * width, width), width)] = code
    lane = lax.broadcasted_iota(jnp.int32, (value.shape[0], tail), 1)
    powers = jnp.where(lane >= tile, power, powers_ref[rows, :])
    powers_ref[rows, :] = powers
    out_ref[:, vocab_local:] = powers.astype(jnp.int32).astype(jnp.int16)


def dot(a, b):
    return jnp.dot(a, b, preferred_element_type=jnp.float32)


def compiler_params():
    return pltpu.CompilerParams(vmem_limit_bytes=28 * megabyte)


def small_cost():
    return pl.CostEstimate(flops=1024, bytes_accessed=1024, transcendentals=0)


head_spec = pl.BlockSpec(memory_space=pl.ANY)


def head_scratch(rows, width, tiles):
    slots = min(tiles, 16 * megabyte // (2 * rows * width))
    return [pltpu.VMEM((slots, rows, width), jnp.bfloat16), pltpu.SemaphoreType.DMA((slots,))]


class Tiles:
    def __init__(self, head_ref, slots_ref, sems_ref, first_row, skip, tiles):
        self.slots, rows, width = slots_ref.shape
        self.tiles, self.slots_ref = tiles, slots_ref

        def copy(tile):
            slot = lax.rem(tile, self.slots)
            column = pl.multiple_of((tile + skip) * width, width)
            source = head_ref.at[pl.ds(first_row, rows), pl.ds(column, width)]
            return pltpu.make_async_copy(source, slots_ref.at[slot], sems_ref.at[slot])

        self.copy = copy

    def get(self, tile):
        @pl.when(tile == 0)
        def _():
            for first in range(self.slots):
                self.copy(first).start()

        self.copy(tile).wait()
        return self.slots_ref[lax.rem(tile, self.slots)]

    def release(self, tile):
        if self.slots < self.tiles:

            @pl.when(tile + self.slots < self.tiles)
            def _():
                self.copy(tile + self.slots).start()


def constant(*shape):
    return pl.BlockSpec(shape, lambda *_: (0,) * len(shape))


def far_kernel(width, skip, tiles, x_ref, head_ref, first_ref, second_ref, powers_ref, slots_ref, sems_ref):
    tile = pl.program_id(0)
    head = Tiles(head_ref, slots_ref, sems_ref, 0, skip, tiles)
    columns = first_ref.shape[1] - tail
    value = dot(x_ref[...], head.get(tile))
    head.release(tile)
    q = value.shape[0] // 4
    first = jnp.concatenate([value[:q], value[2 * q : 3 * q]], axis=0)
    second = jnp.concatenate([value[q : 2 * q], value[3 * q :]], axis=0)
    put(first_ref, powers_ref, slice(0, 2 * q), tile, width, columns, first)
    put(second_ref, powers_ref, slice(2 * q, 4 * q), tile, width, columns, second)


def far_codes(rows_in, head, width, skip, tiles):
    rows, depth = rows_in.shape
    columns = tiles * width
    return pl.pallas_call(
        functools.partial(far_kernel, width, skip, tiles),
        grid=(tiles,),
        in_specs=[constant(rows, depth), head_spec],
        out_specs=[constant(rows // 2, columns + tail)] * 2,
        out_shape=[jax.ShapeDtypeStruct((rows // 2, columns + tail), jnp.int16)] * 2,
        scratch_shapes=[pltpu.VMEM((rows, tail), jnp.float32)] + head_scratch(depth, width, tiles),
        compiler_params=compiler_params(),
        cost_estimate=small_cost(),
        name="far_codes",
    )(rows_in, head)


def near_kernel(width, skip, tiles, x_ref, y_ref, head_ref, by_x_ref, by_y_ref, to_x_ref, to_y_ref, *refs):
    powers_ref, slots_ref, sems_ref = refs
    tile = pl.program_id(0)
    head = Tiles(head_ref, slots_ref, sems_ref, 0, skip, tiles)
    rows = x_ref.shape[0]
    half = rows // 2
    columns = to_x_ref.shape[1] - tail
    value = dot(jnp.concatenate([x_ref[...], y_ref[...]], axis=0), head.get(tile))
    head.release(tile)
    more_x = decode(by_y_ref, tile, width, columns)
    more_y = decode(by_x_ref, tile, width, columns)
    for_x = jnp.concatenate([value[:half], value[half:rows] + more_x], axis=0)
    for_y = jnp.concatenate([value[rows : rows + half] + more_y, value[rows + half :]], axis=0)
    put(to_x_ref, powers_ref, slice(0, rows), tile, width, columns, for_x)
    put(to_y_ref, powers_ref, slice(rows, 2 * rows), tile, width, columns, for_y)


def near_codes(part, rows_x, rows_y, head, by_x, by_y, width, skip, tiles):
    depth = head.shape[0]
    rows = rows_x.shape[0] // 2
    columns = tiles * width
    return pl.pallas_call(
        functools.partial(near_kernel, width, skip, tiles),
        grid=(tiles,),
        in_specs=[pl.BlockSpec((rows, depth), lambda j: (part, 0))] * 2
        + [head_spec]
        + [pl.BlockSpec((rows // 2, columns + tail), lambda j: (part, 0))] * 2,
        out_specs=[constant(rows, columns + tail)] * 2,
        out_shape=[jax.ShapeDtypeStruct((rows, columns + tail), jnp.int16)] * 2,
        scratch_shapes=[pltpu.VMEM((2 * rows, tail), jnp.float32)] + head_scratch(depth, width, tiles),
        compiler_params=compiler_params(),
        cost_estimate=small_cost(),
        name="near_codes",
    )(rows_x, rows_y, head, by_x, by_y)


def own_kernel(tiles, x_ref, head_ref, out_ref, slots_ref, sems_ref):
    tile = pl.program_id(0)
    head = Tiles(head_ref, slots_ref, sems_ref, 0, 0, tiles)
    out_ref[...] = dot(x_ref[...], head.get(tile))
    head.release(tile)


def own_logits(rows_in, head, width):
    rows, depth = rows_in.shape
    columns = head.shape[1]
    return pl.pallas_call(
        functools.partial(own_kernel, columns // width),
        grid=(columns // width,),
        in_specs=[constant(rows, depth), head_spec],
        out_specs=pl.BlockSpec((rows, width), lambda j: (0, j)),
        out_shape=pltpu.HBM((rows, columns), jnp.float32),
        scratch_shapes=head_scratch(depth, width, columns // width),
        compiler_params=compiler_params(),
        cost_estimate=small_cost(),
        name="own_logits",
    )(rows_in, head)


def members(ids, start, width):
    rows = ids.shape[0]
    column = lax.broadcasted_iota(jnp.int32, (rows, width), 1) + start
    found = column == ids[:, 0:1]
    for k in range(1, ids.shape[1]):
        found = found | (column == ids[:, k : k + 1])
    return found


def stats_kernel(width, parts, *refs):
    own_ref, by_x_refs, by_y_refs = refs[0], refs[1 : 1 + parts], refs[1 + parts : 1 + 2 * parts]
    ids_ref, logits_ref, listed_ref, out_ref = refs[1 + 2 * parts :]
    rows, columns = logits_ref.shape
    each = columns // parts
    ids = ids_ref[...]
    top_all = jnp.full((rows, width), lowest, jnp.float32)
    top_ref = jnp.full((rows, width), lowest, jnp.float32)
    for start in range(0, columns, width):
        at = slice(start, start + width)
        where, inner = start // each, start % each // width
        piece = own_ref[:, at] + decode(by_x_refs[where], inner, width, each)
        piece = piece + decode(by_y_refs[where], inner, width, each)
        listed = jnp.where(members(ids, start, width), piece, lowest)
        logits_ref[:, at] = piece
        listed_ref[:, at] = listed
        top_all = jnp.maximum(top_all, piece)
        top_ref = jnp.maximum(top_ref, listed)
    peak_all = jnp.max(top_all, axis=1, keepdims=True)
    peak_ref = jnp.max(top_ref, axis=1, keepdims=True)
    sum_all = jnp.zeros((rows, width), jnp.float32)
    sum_ref = jnp.zeros((rows, width), jnp.float32)
    for start in range(0, columns, width):
        at = slice(start, start + width)
        sum_all = sum_all + jnp.exp(logits_ref[:, at] - peak_all)
        sum_ref = sum_ref + jnp.exp(listed_ref[:, at] - peak_ref)
    sum_all = jnp.sum(sum_all, axis=1, keepdims=True)
    sum_ref = jnp.sum(sum_ref, axis=1, keepdims=True)
    lane = lax.broadcasted_iota(jnp.int32, out_ref.shape, 1)
    out_ref[...] = jnp.where(
        lane == 0, peak_all, jnp.where(lane == 1, peak_ref, jnp.where(lane == 2, sum_all, sum_ref))
    )


def row_stats(part, own, by_x, by_y, ids, width):
    rows = by_x[0].shape[0]
    parts = len(by_x)
    columns = own.shape[1]
    block = min(rows, 16)
    skip = part * (rows // block)
    across = lambda array: pl.BlockSpec((block, array.shape[1]), lambda i: (i, 0))
    return pl.pallas_call(
        functools.partial(stats_kernel, width, parts),
        grid=(rows // block,),
        in_specs=[pl.BlockSpec((block, columns), lambda i: (i + skip, 0))]
        + [across(a) for a in (*by_x, *by_y)]
        + [pl.BlockSpec((block, ids.shape[1]), lambda i: (i + skip, 0))],
        out_specs=[
            pl.BlockSpec((block, columns), lambda i: (i, 0)),
            pl.BlockSpec((block, columns), lambda i: (i, 0)),
            pl.BlockSpec((block, 128), lambda i: (i, 0)),
        ],
        out_shape=[
            jax.ShapeDtypeStruct((rows, columns), jnp.float32),
            jax.ShapeDtypeStruct((rows, columns), jnp.float32),
            jax.ShapeDtypeStruct((rows, 128), jnp.float32),
        ],
        compiler_params=compiler_params(),
        cost_estimate=small_cost(),
        name="row_stats",
    )(own, *by_x, *by_y, ids)


def grad_kernel(width, logits_ref, listed_ref, stats_ref, scale_ref, out_ref, info_ref):
    rows, columns = logits_ref.shape
    stats = [stats_ref[v] for v in range(stats_ref.shape[0])]
    peaks = functools.reduce(jnp.maximum, [s[:, :2] for s in stats])
    sums = functools.reduce(jnp.add, [s[:, 2:4] * jnp.exp(s[:, :2] - peaks) for s in stats])
    lse = peaks + jnp.log(sums)
    lse_all, lse_ref = lse[:, 0:1], lse[:, 1:2]
    scale = scale_ref[...]
    term = jnp.zeros((rows, width), jnp.float32)
    for start in range(0, columns, width):
        at = slice(start, start + width)
        piece = logits_ref[:, at]
        grad = scale * (jnp.exp(listed_ref[:, at] - lse_ref) - jnp.exp(piece - lse_all))
        grad = grad.astype(jnp.bfloat16)
        out_ref[:, at] = grad
        term = term + grad.astype(jnp.float32) * piece
    lane = lax.broadcasted_iota(jnp.int32, info_ref.shape, 1)
    info_ref[...] = jnp.broadcast_to(lse_ref - lse_all, info_ref.shape)
    term = jnp.sum(term, axis=1, keepdims=True)
    high = term.astype(jnp.bfloat16).astype(jnp.float32)
    middle = (term - high).astype(jnp.bfloat16).astype(jnp.float32)
    low = term - high - middle
    term = jnp.where(lane == 0, high, jnp.where(lane == 1, middle, jnp.where(lane == 2, low, 0.0)))
    out_ref[:, columns:] = term.astype(jnp.bfloat16)


def logit_grads(part, logits, listed, stats, scale, width):
    rows, columns = logits.shape
    block = min(rows, 16)
    skip = part * (rows // block)
    return pl.pallas_call(
        functools.partial(grad_kernel, width),
        grid=(rows // block,),
        in_specs=[
            pl.BlockSpec((block, columns), lambda i: (i, 0)),
            pl.BlockSpec((block, columns), lambda i: (i, 0)),
            pl.BlockSpec((stats.shape[0], block, 128), lambda i: (0, i, 0)),
            pl.BlockSpec((block, 1), lambda i: (i + skip, 0)),
        ],
        out_specs=[
            pl.BlockSpec((block, columns + tail), lambda i: (i, 0)),
            pl.BlockSpec((block, 128), lambda i: (i, 0)),
        ],
        out_shape=[
            jax.ShapeDtypeStruct((rows, columns + tail), jnp.bfloat16),
            jax.ShapeDtypeStruct((rows, 128), jnp.float32),
        ],
        compiler_params=compiler_params(),
        cost_estimate=small_cost(),
        name="logit_grads",
    )(logits, listed, stats, scale)


def put_row(out_ref, value):
    width = value.shape[1] - tail
    code, power = encode(value[:, :width])
    term, term_power = encode(value[:, width : width + 1])
    lane = lax.broadcasted_iota(jnp.int32, (value.shape[0], tail), 1)
    beside = jnp.where(lane == 0, power, jnp.where(lane == 1, term.astype(jnp.int32).astype(jnp.float32), term_power))
    out_ref[:, :width] = code
    out_ref[:, width:] = beside.astype(jnp.int32).astype(jnp.int16)


def take_row(codes_ref):
    width = codes_ref.shape[1] - tail
    beside = codes_ref[:, width:].astype(jnp.int32).astype(jnp.float32)
    value = codes_ref[:, :width].astype(jnp.int32).astype(jnp.float32) * jnp.exp(beside[:, 0:1] * per_step)
    term = beside[:, 1:2] * jnp.exp(beside[:, 2:3] * per_step)
    return value, jnp.broadcast_to(term, beside.shape)


def back_kernel(tiles, keeps, place_ref, grad_ref, beside_ref, head_ref, *refs):
    outs, (total_ref, slots_ref, sems_ref) = refs[:-3], refs[-3:]
    tile = pl.program_id(0)
    rows = slots_ref.shape[1]
    head = Tiles(head_ref, slots_ref, sems_ref, pl.multiple_of(place_ref[0] * rows, rows), 0, tiles)

    @pl.when(tile == 0)
    def _():
        total_ref[...] = jnp.zeros_like(total_ref)

    total_ref[...] += lax.dot_general(
        grad_ref[...], head.get(tile), (((1,), (1,)), ((), ())), preferred_element_type=jnp.float32
    )
    head.release(tile)

    @pl.when(tile == tiles - 1)
    def _():
        term = beside_ref[...].astype(jnp.float32)
        term = jnp.broadcast_to(term[:, 0:1] + term[:, 1:2] + term[:, 2:3], term.shape)
        width = outs[0].shape[1] - tail
        for k, out_ref in enumerate(outs):
            start = pl.multiple_of((place_ref[1] ^ k) * width, width)
            value = total_ref[:, pl.ds(start, width)]
            if k == 0 and keeps:
                out_ref[:, :width] = value
                out_ref[:, width:] = term
            else:
                put_row(out_ref, jnp.concatenate([value, term], axis=1))


def back(grad, head, place, width, group, keeps):
    depth, columns = head.shape
    rows = grad.shape[0]
    blocks = max(group // 2, 1)
    part = depth // group
    types = [jnp.float32 if keeps and k == 0 else jnp.int16 for k in range(blocks)]
    return pl.pallas_call(
        functools.partial(back_kernel, columns // width, keeps),
        grid_spec=pltpu.PrefetchScalarGridSpec(
            num_scalar_prefetch=1,
            grid=(columns // width,),
            in_specs=[
                pl.BlockSpec((rows, width), lambda j, place: (0, j)),
                pl.BlockSpec((rows, tail), lambda j, place: (0, columns // tail)),
                head_spec,
            ],
            out_specs=[constant(rows, part + tail)] * blocks,
            scratch_shapes=[pltpu.VMEM((rows, blocks * part), jnp.float32)]
            + head_scratch(blocks * part, width, columns // width),
        ),
        out_shape=[jax.ShapeDtypeStruct((rows, part + tail), t) for t in types],
        compiler_params=compiler_params(),
        cost_estimate=small_cost(),
        name="grad_rows",
    )(place, grad, grad, head)


def group_kernel(place_ref, keep_ref, *refs):
    total_ref = refs[-1]
    count = place_ref.shape[0] - 1
    out_ref, sends, received = refs[-2 - count], refs[-1 - count : -1], refs[: -2 - count]
    width = keep_ref.shape[1] - tail
    total, term = keep_ref[:, :width], keep_ref[:, width:]
    for codes_ref in received:
        more, more_term = take_row(codes_ref)
        total, term = total + more, term + more_term
    total_ref[:, :width] = total
    total_ref[:, width:] = term
    rows = out_ref.shape[0]
    block = lambda b: total_ref[pl.ds(pl.multiple_of(b * rows, rows), rows), :]
    out_ref[...] = block(place_ref[0])
    for k, send_ref in enumerate(sends, 1):
        put_row(send_ref, block(place_ref[k]))


def group_sum(place, keep, received):
    blocks = place.shape[0]
    rows, width = keep.shape
    each = (rows // blocks, width)
    return pl.pallas_call(
        group_kernel,
        in_specs=[pl.BlockSpec(memory_space=pltpu.SMEM)]
        + [pl.BlockSpec(memory_space=pltpu.VMEM)] * (1 + len(received)),
        out_specs=[pl.BlockSpec(memory_space=pltpu.VMEM)] * blocks,
        out_shape=[jax.ShapeDtypeStruct(each, jnp.float32)]
        + [jax.ShapeDtypeStruct(each, jnp.int16)] * (blocks - 1),
        scratch_shapes=[pltpu.VMEM((rows, width), jnp.float32)],
        compiler_params=compiler_params(),
        cost_estimate=small_cost(),
        name="group_sum",
    )(place, keep, *received)


def last_kernel(keep_ref, *refs):
    width = keep_ref.shape[1] - tail
    total, term = keep_ref[:, :width], keep_ref[:, width:]
    for codes_ref in refs[:-1]:
        more, more_term = take_row(codes_ref)
        total, term = total + more, term + more_term
    put_row(refs[-1], jnp.concatenate([total, term], axis=1))


def last_sum(keep, received):
    return pl.pallas_call(
        last_kernel,
        in_specs=[pl.BlockSpec(memory_space=pltpu.VMEM)] * (1 + len(received)),
        out_specs=pl.BlockSpec(memory_space=pltpu.VMEM),
        out_shape=jax.ShapeDtypeStruct(keep.shape, jnp.int16),
        compiler_params=compiler_params(),
        cost_estimate=small_cost(),
        name="last_sum",
    )(keep, *received)


def after(value, *others):
    return lax.optimization_barrier((value, *others))[0]


def shards(hidden, head, gain, refusal_ids, refusal_count, loss_scale):
    row_count, model_width = hidden.shape
    depth, vocab_local = head.shape
    list_length = refusal_ids.shape[1]
    prompt_size = lax.axis_size("prompt")
    vocab_size = lax.axis_size("vocab")
    group = vocab_size // prompt_size
    width = min(1024, vocab_local // 2)
    tiles = vocab_local // width
    half = row_count // 2
    me = lax.axis_index("prompt")
    shard = lax.axis_index("vocab")
    to_x, to_y, to_far = ([(p, p ^ k) for p in range(prompt_size)] for k in (1, 2, 3))
    send = lambda value, pairs: lax.ppermute(value, "prompt", pairs)

    hidden_f = hidden.astype(jnp.float32)
    inverse_rms = lax.rsqrt(jnp.mean(hidden_f * hidden_f, axis=1, keepdims=True) + epsilon)
    normed = (hidden_f * inverse_rms * gain).astype(jnp.bfloat16)
    columns = lambda p: lax.dynamic_slice_in_dim(normed, p * depth, depth, 1)
    rows_far = send(columns(me ^ 3), to_far)
    beside = ((0, 0), (0, tail))
    rows_x = send(jnp.pad(columns(me ^ 1), beside), to_x)
    rows_y = send(jnp.pad(columns(me ^ 2), beside), to_y)
    own = own_logits(columns(me), head, width)
    first_tiles = tiles // 2
    column_parts = ((0, first_tiles), (first_tiles, tiles - first_tiles))
    by_x, by_y = [], []
    for (skip, count), waits in zip(column_parts, ([own], [rows_x, rows_y])):
        first, second = far_codes(after(rows_far, *waits), head, width, skip, count)
        by_x.append(send(first, to_x))
        by_y.append(send(second, to_y))
    halves = []
    for part in range(2):
        sums_x, sums_y = [], []
        for c, (skip, count) in enumerate(column_parts):
            codes_x, codes_y = near_codes(part, rows_x, rows_y, head, by_x[c], by_y[c], width, skip, count)
            sums_x.append(send(codes_x, to_x))
            sums_y.append(send(codes_y, to_y))
        halves.append((sums_x, sums_y))
        rows_x = after(rows_x, codes_x, sums_x[0], sums_y[0])

    in_list = jnp.arange(list_length)[None, :] < refusal_count[:, None]
    ids = jnp.where(in_list, refusal_ids - shard * vocab_local, -1)

    block, member = shard // group, shard % group
    spread = max(group // 2, 1)
    place_other = jnp.stack([(member // spread) ^ 1, member % spread]).astype(jnp.int32)
    place_mine = jnp.stack([member // spread, member % spread]).astype(jnp.int32)
    place_block = jnp.stack([block ^ k ^ me for k in range(prompt_size)]).astype(jnp.int32)
    to_member = [[(v, v ^ k) for v in range(vocab_size)] for k in range(1, group)]
    to_block = [
        [(v, ((v // group) ^ k) * group + v % group) for v in range(vocab_size)]
        for k in range(1, prompt_size)
    ]
    moves = []
    for p in range(prompt_size):
        for r in range(prompt_size):
            for i in range(group):
                moves.append((p * vocab_size + r * group + i, r * vocab_size + p * group + i))

    quarter = half // 2
    infos, grads = [], []
    for part, (sums_x, sums_y) in enumerate(halves):
        logits, listed, stats = row_stats(part, own, sums_x, sums_y, after(ids, *infos), width)
        stats = lax.all_gather(stats, "vocab", axis=0)
        grad, info = logit_grads(part, logits, listed, stats, loss_scale[:, None], width)
        infos.append(info)
        grads.append(grad)
    log_refusal = jnp.concatenate([info[:, 0] for info in infos])

    def neighbours(grad, *waits):
        sent = after(grad, *waits)
        return grad, send(sent, to_x), send(sent, to_y)

    def diagonal(grad_x, grad_y, *waits):
        passed_x, passed_y = after(grad_y, *waits)[:quarter], after(grad_x, *waits)[quarter:]
        return (passed_x, passed_y), [send(passed_x, to_x), send(passed_y, to_y)]

    def gradient(rows, waits_other=(), waits_mine=()):
        rows = jnp.concatenate(rows)
        others = back(rows, head, after(place_other, *waits_other), width, group, False)
        received = [lax.ppermute(c, "vocab", to) for c, to in zip(others, to_member[spread - 1 :])]
        keep, *codes = back(rows, head, after(place_mine, *others, *waits_mine), width, group, True)
        received += [lax.ppermute(c, "vocab", to) for c, to in zip(codes, to_member)]
        return keep, received

    def blocks(keep, received, *waits):
        keep, *codes = group_sum(after(place_block, *waits), keep, received)
        return keep, [lax.ppermute(c, "vocab", to) for c, to in zip(codes, to_block)]

    rows_a = neighbours(grads[0])
    _, far_a = diagonal(*rows_a[1:], infos[1])
    rows_b = neighbours(grads[1], *far_a)
    keep_a, received_a = gradient((*rows_a, *far_a))
    passed, far_b = diagonal(*rows_b[1:], keep_a)
    keep_a, received_a = blocks(keep_a, received_a, *passed)
    sum_a = last_sum(keep_a, received_a)
    keep_b, received_b = gradient((*rows_b, *far_b), received_a, [sum_a])
    sum_b = last_sum(*blocks(keep_b, received_b))
    grad_cols = [lax.ppermute(total, ("prompt", "vocab"), moves) for total in (sum_a, sum_b)]

    slice_width = model_width // vocab_size
    col_start = shard * slice_width
    codes = jnp.concatenate(grad_cols)
    power = codes[:, slice_width : slice_width + 1].astype(jnp.float32)
    grad_cols = codes[:, :slice_width].astype(jnp.float32) * jnp.exp(power * per_step)
    term = codes[:, slice_width + 1 : slice_width + 3].astype(jnp.float32)
    row_term = term[:, 0] * jnp.exp(term[:, 1] * per_step)
    hidden_cols = lax.dynamic_slice_in_dim(hidden, col_start, slice_width, 1).astype(jnp.float32)
    gain_cols = lax.dynamic_slice_in_dim(gain, col_start, slice_width, 0)
    grad_hidden = (
        inverse_rms * gain_cols * grad_cols
        - hidden_cols * (inverse_rms * inverse_rms / model_width) * row_term[:, None]
    )
    return (grad_hidden, log_refusal)


def solution(mesh):
    return jax.shard_map(
        shards,
        mesh=mesh,
        in_specs=(
            P("prompt", None),
            P("prompt", "vocab"),
            P(),
            P("prompt", None),
            P("prompt"),
            P("prompt"),
        ),
        out_specs=(P("prompt", "vocab"), P("prompt")),
        check_vma=False,
    )
```

```python
import functools
import math

import jax
import jax.numpy as jnp
from jax import lax
from jax.experimental import pallas as pl
from jax.experimental.pallas import tpu as pltpu
from jax.sharding import PartitionSpec as P

epsilon = 1e-05
lowest = -1e30
tail = 128
steps = 64
code_top = 32000.0
per_step = math.log(2.0) / steps
megabyte = 1024 * 1024


def encode(value):
    top = jnp.max(jnp.abs(value), axis=1, keepdims=True)
    power = jnp.ceil(jnp.log(jnp.maximum(top, 1e-30) * (1.0 / code_top)) * (1.0 / per_step))
    code = jnp.round(value * jnp.exp(power * -per_step))
    return code.astype(jnp.int32).astype(jnp.int16), power


def decode(codes_ref, tile, width, vocab_local, rows=slice(None)):
    powers = codes_ref[rows, vocab_local : vocab_local + tail].astype(jnp.int32).astype(jnp.float32)
    lane = lax.broadcasted_iota(jnp.int32, powers.shape, 1)
    power = jnp.sum(jnp.where(lane == tile, powers, 0.0), axis=1, keepdims=True)
    start = tile * width
    if not isinstance(start, int):
        start = pl.multiple_of(start, width)
    codes = codes_ref[rows, pl.ds(start, width)].astype(jnp.int32).astype(jnp.float32)
    return codes * jnp.exp(power * per_step)


def put(out_ref, powers_ref, rows, tile, width, vocab_local, value):
    code, power = encode(value)
    out_ref[:, pl.ds(pl.multiple_of(tile * width, width), width)] = code
    lane = lax.broadcasted_iota(jnp.int32, (value.shape[0], tail), 1)
    powers = jnp.where(lane >= tile, power, powers_ref[rows, :])
    powers_ref[rows, :] = powers
    out_ref[:, vocab_local:] = powers.astype(jnp.int32).astype(jnp.int16)


def dot(a, b):
    return jnp.dot(a, b, preferred_element_type=jnp.float32)


def compiler_params():
    return pltpu.CompilerParams(vmem_limit_bytes=28 * megabyte)


def small_cost():
    return pl.CostEstimate(flops=1024, bytes_accessed=1024, transcendentals=0)


head_spec = pl.BlockSpec(memory_space=pl.ANY)


def head_scratch(rows, width, tiles):
    slots = min(tiles, 16 * megabyte // (2 * rows * width))
    return [pltpu.VMEM((slots, rows, width), jnp.bfloat16), pltpu.SemaphoreType.DMA((slots,))]


class Tiles:
    def __init__(self, head_ref, slots_ref, sems_ref, first_row, skip, tiles):
        self.slots, rows, width = slots_ref.shape
        self.tiles, self.slots_ref = tiles, slots_ref

        def copy(tile):
            slot = lax.rem(tile, self.slots)
            column = pl.multiple_of((tile + skip) * width, width)
            source = head_ref.at[pl.ds(first_row, rows), pl.ds(column, width)]
            return pltpu.make_async_copy(source, slots_ref.at[slot], sems_ref.at[slot])

        self.copy = copy

    def get(self, tile):
        @pl.when(tile == 0)
        def _():
            for first in range(self.slots):
                self.copy(first).start()

        self.copy(tile).wait()
        return self.slots_ref[lax.rem(tile, self.slots)]

    def release(self, tile):
        if self.slots < self.tiles:

            @pl.when(tile + self.slots < self.tiles)
            def _():
                self.copy(tile + self.slots).start()


def constant(*shape):
    return pl.BlockSpec(shape, lambda *_: (0,) * len(shape))


def far_kernel(width, skip, tiles, x_ref, head_ref, first_ref, second_ref, powers_ref, slots_ref, sems_ref):
    tile = pl.program_id(0)
    head = Tiles(head_ref, slots_ref, sems_ref, 0, skip, tiles)
    columns = first_ref.shape[1] - tail
    value = dot(x_ref[...], head.get(tile))
    head.release(tile)
    q = value.shape[0] // 4
    first = jnp.concatenate([value[:q], value[2 * q : 3 * q]], axis=0)
    second = jnp.concatenate([value[q : 2 * q], value[3 * q :]], axis=0)
    put(first_ref, powers_ref, slice(0, 2 * q), tile, width, columns, first)
    put(second_ref, powers_ref, slice(2 * q, 4 * q), tile, width, columns, second)


def far_codes(rows_in, head, width, skip, tiles):
    rows, depth = rows_in.shape[0], head.shape[0]
    columns = tiles * width
    return pl.pallas_call(
        functools.partial(far_kernel, width, skip, tiles),
        grid=(tiles,),
        in_specs=[constant(rows, depth), head_spec],
        out_specs=[constant(rows // 2, columns + tail)] * 2,
        out_shape=[jax.ShapeDtypeStruct((rows // 2, columns + tail), jnp.int16)] * 2,
        scratch_shapes=[pltpu.VMEM((rows, tail), jnp.float32)] + head_scratch(depth, width, tiles),
        compiler_params=compiler_params(),
        cost_estimate=small_cost(),
        name="far_codes",
    )(rows_in, head)


def near_kernel(width, skip, tiles, x_ref, y_ref, head_ref, by_x_ref, by_y_ref, *refs):
    to_x_refs, to_y_refs, (powers_ref, slots_ref, sems_ref) = refs[:2], refs[2:4], refs[4:]
    tile = pl.program_id(0)
    head = Tiles(head_ref, slots_ref, sems_ref, 0, skip, tiles)
    rows = x_ref.shape[0]
    columns = tiles * width
    value = dot(jnp.concatenate([x_ref[...], y_ref[...]], axis=0), head.get(tile))
    head.release(tile)
    more_x = decode(by_y_ref, tile, width, columns)
    more_y = decode(by_x_ref, tile, width, columns)
    part, half = rows // 2, rows // 4
    for p in range(2):
        for_x, for_y = value[p * part : (p + 1) * part], value[rows + p * part : rows + (p + 1) * part]
        add = slice(p * half, (p + 1) * half)
        for_x = jnp.concatenate([for_x[:half], for_x[half:] + more_x[add]], axis=0)
        for_y = jnp.concatenate([for_y[:half] + more_y[add], for_y[half:]], axis=0)
        for q, out_ref, out in ((0, to_x_refs[p], for_x), (2, to_y_refs[p], for_y)):
            kept = slice((p + q) * part, (p + q + 1) * part)
            put(out_ref, powers_ref, kept, tile, width, columns, out)


def near_codes(rows_x, rows_y, head, by_x, by_y, width, skip, tiles):
    rows, depth = rows_x.shape[0], head.shape[0]
    columns = tiles * width
    shape = (rows // 2, columns + tail)
    return pl.pallas_call(
        functools.partial(near_kernel, width, skip, tiles),
        grid=(tiles,),
        in_specs=[constant(rows, depth)] * 2 + [head_spec] + [constant(*shape)] * 2,
        out_specs=[constant(*shape)] * 4,
        out_shape=[jax.ShapeDtypeStruct(shape, jnp.int16)] * 4,
        scratch_shapes=[pltpu.VMEM((2 * rows, tail), jnp.float32)] + head_scratch(depth, width, tiles),
        compiler_params=compiler_params(),
        cost_estimate=small_cost(),
        name="near_codes",
    )(rows_x, rows_y, head, by_x, by_y)


def own_kernel(tiles, x_ref, head_ref, out_ref, slots_ref, sems_ref):
    tile = pl.program_id(0)
    head = Tiles(head_ref, slots_ref, sems_ref, 0, 0, tiles)
    out_ref[...] = dot(x_ref[...], head.get(tile))
    head.release(tile)


def own_logits(rows_in, head, width):
    rows, depth = rows_in.shape
    columns = head.shape[1]
    return pl.pallas_call(
        functools.partial(own_kernel, columns // width),
        grid=(columns // width,),
        in_specs=[constant(rows, depth), head_spec],
        out_specs=pl.BlockSpec((rows, width), lambda j: (0, j)),
        out_shape=jax.ShapeDtypeStruct((rows, columns), jnp.float32),
        scratch_shapes=head_scratch(depth, width, columns // width),
        compiler_params=compiler_params(),
        cost_estimate=small_cost(),
        name="own_logits",
    )(rows_in, head)


def members(ids, start, width):
    rows = ids.shape[0]
    column = lax.broadcasted_iota(jnp.int32, (rows, width), 1) + start
    found = column == ids[:, 0:1]
    for k in range(1, ids.shape[1]):
        found = found | (column == ids[:, k : k + 1])
    return found


def stats_kernel(width, parts, *refs):
    own_ref, by_x_refs, by_y_refs = refs[0], refs[1 : 1 + parts], refs[1 + parts : 1 + 2 * parts]
    ids_ref, logits_ref, listed_ref, out_ref = refs[1 + 2 * parts :]
    rows, columns = logits_ref.shape
    each = columns // parts
    ids = ids_ref[...]
    top_all = jnp.full((rows, width), lowest, jnp.float32)
    top_ref = jnp.full((rows, width), lowest, jnp.float32)
    for start in range(0, columns, width):
        at = slice(start, start + width)
        where, inner = start // each, start % each // width
        piece = own_ref[:, at] + decode(by_x_refs[where], inner, width, each)
        piece = piece + decode(by_y_refs[where], inner, width, each)
        listed = jnp.where(members(ids, start, width), piece, lowest)
        logits_ref[:, at] = piece
        listed_ref[:, at] = listed
        top_all = jnp.maximum(top_all, piece)
        top_ref = jnp.maximum(top_ref, listed)
    peak_all = jnp.max(top_all, axis=1, keepdims=True)
    peak_ref = jnp.max(top_ref, axis=1, keepdims=True)
    sum_all = jnp.zeros((rows, width), jnp.float32)
    sum_ref = jnp.zeros((rows, width), jnp.float32)
    for start in range(0, columns, width):
        at = slice(start, start + width)
        sum_all = sum_all + jnp.exp(logits_ref[:, at] - peak_all)
        sum_ref = sum_ref + jnp.exp(listed_ref[:, at] - peak_ref)
    sum_all = jnp.sum(sum_all, axis=1, keepdims=True)
    sum_ref = jnp.sum(sum_ref, axis=1, keepdims=True)
    lane = lax.broadcasted_iota(jnp.int32, out_ref.shape, 1)
    out_ref[...] = jnp.where(
        lane == 0, peak_all, jnp.where(lane == 1, peak_ref, jnp.where(lane == 2, sum_all, sum_ref))
    )


def row_stats(part, own, by_x, by_y, ids, width):
    rows = by_x[0].shape[0]
    parts = len(by_x)
    columns = own.shape[1]
    block = min(rows, 16)
    skip = part * (rows // block)
    across = lambda array: pl.BlockSpec((block, array.shape[1]), lambda i: (i, 0))
    return pl.pallas_call(
        functools.partial(stats_kernel, width, parts),
        grid=(rows // block,),
        in_specs=[pl.BlockSpec((block, columns), lambda i: (i + skip, 0))]
        + [across(a) for a in (*by_x, *by_y)]
        + [pl.BlockSpec((block, ids.shape[1]), lambda i: (i + skip, 0))],
        out_specs=[
            pl.BlockSpec((block, columns), lambda i: (i, 0)),
            pl.BlockSpec((block, columns), lambda i: (i, 0)),
            pl.BlockSpec((block, 128), lambda i: (i, 0)),
        ],
        out_shape=[
            jax.ShapeDtypeStruct((rows, columns), jnp.float32),
            jax.ShapeDtypeStruct((rows, columns), jnp.float32),
            jax.ShapeDtypeStruct((rows, 128), jnp.float32),
        ],
        compiler_params=compiler_params(),
        cost_estimate=small_cost(),
        name="row_stats",
    )(own, *by_x, *by_y, ids)


def grad_kernel(width, logits_ref, listed_ref, stats_ref, scale_ref, out_ref, info_ref):
    rows, columns = logits_ref.shape
    stats = [stats_ref[v] for v in range(stats_ref.shape[0])]
    peaks = functools.reduce(jnp.maximum, [s[:, :2] for s in stats])
    sums = functools.reduce(jnp.add, [s[:, 2:4] * jnp.exp(s[:, :2] - peaks) for s in stats])
    lse = peaks + jnp.log(sums)
    lse_all, lse_ref = lse[:, 0:1], lse[:, 1:2]
    scale = scale_ref[...]
    term = jnp.zeros((rows, width), jnp.float32)
    for start in range(0, columns, width):
        at = slice(start, start + width)
        piece = logits_ref[:, at]
        grad = scale * (jnp.exp(listed_ref[:, at] - lse_ref) - jnp.exp(piece - lse_all))
        grad = grad.astype(jnp.bfloat16)
        out_ref[:, at] = grad
        term = term + grad.astype(jnp.float32) * piece
    lane = lax.broadcasted_iota(jnp.int32, info_ref.shape, 1)
    info_ref[...] = jnp.broadcast_to(lse_ref - lse_all, info_ref.shape)
    term = jnp.sum(term, axis=1, keepdims=True)
    high = term.astype(jnp.bfloat16).astype(jnp.float32)
    middle = (term - high).astype(jnp.bfloat16).astype(jnp.float32)
    low = term - high - middle
    term = jnp.where(lane == 0, high, jnp.where(lane == 1, middle, jnp.where(lane == 2, low, 0.0)))
    out_ref[:, columns:] = term.astype(jnp.bfloat16)


def logit_grads(part, logits, listed, stats, scale, width):
    rows, columns = logits.shape
    block = min(rows, 16)
    skip = part * (rows // block)
    return pl.pallas_call(
        functools.partial(grad_kernel, width),
        grid=(rows // block,),
        in_specs=[
            pl.BlockSpec((block, columns), lambda i: (i, 0)),
            pl.BlockSpec((block, columns), lambda i: (i, 0)),
            pl.BlockSpec((stats.shape[0], block, 128), lambda i: (0, i, 0)),
            pl.BlockSpec((block, 1), lambda i: (i + skip, 0)),
        ],
        out_specs=[
            pl.BlockSpec((block, columns + tail), lambda i: (i, 0)),
            pl.BlockSpec((block, 128), lambda i: (i, 0)),
        ],
        out_shape=[
            jax.ShapeDtypeStruct((rows, columns + tail), jnp.bfloat16),
            jax.ShapeDtypeStruct((rows, 128), jnp.float32),
        ],
        compiler_params=compiler_params(),
        cost_estimate=small_cost(),
        name="logit_grads",
    )(logits, listed, stats, scale)


def put_row(out_ref, value):
    width = value.shape[1] - tail
    code, power = encode(value[:, :width])
    term, term_power = encode(value[:, width : width + 1])
    lane = lax.broadcasted_iota(jnp.int32, (value.shape[0], tail), 1)
    beside = jnp.where(lane == 0, power, jnp.where(lane == 1, term.astype(jnp.int32).astype(jnp.float32), term_power))
    out_ref[:, :width] = code
    out_ref[:, width:] = beside.astype(jnp.int32).astype(jnp.int16)


def take_row(codes_ref):
    width = codes_ref.shape[1] - tail
    beside = codes_ref[:, width:].astype(jnp.int32).astype(jnp.float32)
    value = codes_ref[:, :width].astype(jnp.int32).astype(jnp.float32) * jnp.exp(beside[:, 0:1] * per_step)
    term = beside[:, 1:2] * jnp.exp(beside[:, 2:3] * per_step)
    return value, jnp.broadcast_to(term, beside.shape)


def back_kernel(tiles, keeps, place_ref, grad_ref, beside_ref, head_ref, *refs):
    outs, (total_ref, slots_ref, sems_ref) = refs[:-3], refs[-3:]
    tile = pl.program_id(0)
    rows = slots_ref.shape[1]
    head = Tiles(head_ref, slots_ref, sems_ref, pl.multiple_of(place_ref[0] * rows, rows), 0, tiles)

    @pl.when(tile == 0)
    def _():
        total_ref[...] = jnp.zeros_like(total_ref)

    total_ref[...] += lax.dot_general(
        grad_ref[...], head.get(tile), (((1,), (1,)), ((), ())), preferred_element_type=jnp.float32
    )
    head.release(tile)

    @pl.when(tile == tiles - 1)
    def _():
        term = beside_ref[...].astype(jnp.float32)
        term = jnp.broadcast_to(term[:, 0:1] + term[:, 1:2] + term[:, 2:3], term.shape)
        width = outs[0].shape[1] - tail
        for k, out_ref in enumerate(outs):
            start = pl.multiple_of((place_ref[1] ^ k) * width, width)
            value = total_ref[:, pl.ds(start, width)]
            if k == 0 and keeps:
                out_ref[:, :width] = value
                out_ref[:, width:] = term
            else:
                put_row(out_ref, jnp.concatenate([value, term], axis=1))


def back(grad, head, place, width, group, keeps):
    depth, columns = head.shape
    rows = grad.shape[0]
    blocks = max(group // 2, 1)
    part = depth // group
    types = [jnp.float32 if keeps and k == 0 else jnp.int16 for k in range(blocks)]
    return pl.pallas_call(
        functools.partial(back_kernel, columns // width, keeps),
        grid_spec=pltpu.PrefetchScalarGridSpec(
            num_scalar_prefetch=1,
            grid=(columns // width,),
            in_specs=[
                pl.BlockSpec((rows, width), lambda j, place: (0, j)),
                pl.BlockSpec((rows, tail), lambda j, place: (0, columns // tail)),
                head_spec,
            ],
            out_specs=[constant(rows, part + tail)] * blocks,
            scratch_shapes=[pltpu.VMEM((rows, blocks * part), jnp.float32)]
            + head_scratch(blocks * part, width, columns // width),
        ),
        out_shape=[jax.ShapeDtypeStruct((rows, part + tail), t) for t in types],
        compiler_params=compiler_params(),
        cost_estimate=small_cost(),
        name="grad_rows",
    )(place, grad, grad, head)


def group_kernel(place_ref, keep_ref, *refs):
    total_ref = refs[-1]
    count = place_ref.shape[0] - 1
    out_ref, sends, received = refs[-2 - count], refs[-1 - count : -1], refs[: -2 - count]
    width = keep_ref.shape[1] - tail
    total, term = keep_ref[:, :width], keep_ref[:, width:]
    for codes_ref in received:
        more, more_term = take_row(codes_ref)
        total, term = total + more, term + more_term
    total_ref[:, :width] = total
    total_ref[:, width:] = term
    rows = out_ref.shape[0]
    block = lambda b: total_ref[pl.ds(pl.multiple_of(b * rows, rows), rows), :]
    out_ref[...] = block(place_ref[0])
    for k, send_ref in enumerate(sends, 1):
        put_row(send_ref, block(place_ref[k]))


def group_sum(place, keep, received):
    blocks = place.shape[0]
    rows, width = keep.shape
    each = (rows // blocks, width)
    return pl.pallas_call(
        group_kernel,
        in_specs=[pl.BlockSpec(memory_space=pltpu.SMEM)]
        + [pl.BlockSpec(memory_space=pltpu.VMEM)] * (1 + len(received)),
        out_specs=[pl.BlockSpec(memory_space=pltpu.VMEM)] * blocks,
        out_shape=[jax.ShapeDtypeStruct(each, jnp.float32)]
        + [jax.ShapeDtypeStruct(each, jnp.int16)] * (blocks - 1),
        scratch_shapes=[pltpu.VMEM((rows, width), jnp.float32)],
        compiler_params=compiler_params(),
        cost_estimate=small_cost(),
        name="group_sum",
    )(place, keep, *received)


def last_kernel(keep_ref, *refs):
    width = keep_ref.shape[1] - tail
    total, term = keep_ref[:, :width], keep_ref[:, width:]
    for codes_ref in refs[:-1]:
        more, more_term = take_row(codes_ref)
        total, term = total + more, term + more_term
    put_row(refs[-1], jnp.concatenate([total, term], axis=1))


def last_sum(keep, received):
    return pl.pallas_call(
        last_kernel,
        in_specs=[pl.BlockSpec(memory_space=pltpu.VMEM)] * (1 + len(received)),
        out_specs=pl.BlockSpec(memory_space=pltpu.VMEM),
        out_shape=jax.ShapeDtypeStruct(keep.shape, jnp.int16),
        compiler_params=compiler_params(),
        cost_estimate=small_cost(),
        name="last_sum",
    )(keep, *received)


def after(value, *others):
    return lax.optimization_barrier((value, *others))[0]


def shards(hidden, head, gain, refusal_ids, refusal_count, loss_scale):
    row_count, model_width = hidden.shape
    depth, vocab_local = head.shape
    list_length = refusal_ids.shape[1]
    prompt_size = lax.axis_size("prompt")
    vocab_size = lax.axis_size("vocab")
    group = vocab_size // prompt_size
    width = min(1024, vocab_local // 2)
    tiles = vocab_local // width
    half = row_count // 2
    me = lax.axis_index("prompt")
    shard = lax.axis_index("vocab")
    to_x, to_y, to_far = ([(p, p ^ k) for p in range(prompt_size)] for k in (1, 2, 3))
    send = lambda value, pairs: lax.ppermute(value, "prompt", pairs)

    hidden_f = hidden.astype(jnp.float32)
    inverse_rms = lax.rsqrt(jnp.mean(hidden_f * hidden_f, axis=1, keepdims=True) + epsilon)
    normed = (hidden_f * inverse_rms * gain).astype(jnp.bfloat16)
    columns = lambda p: lax.dynamic_slice_in_dim(normed, p * depth, depth, 1)
    wider = lambda p, more: jnp.pad(columns(p), ((0, 0), (0, more)))
    rows_far = send(wider(me ^ 3, 2 * tail), to_far)
    rows_x = send(wider(me ^ 1, tail), to_x)
    rows_y = send(wider(me ^ 2, tail), to_y)
    own = own_logits(columns(me), head, width)
    first_tiles = tiles // 2
    column_parts = ((0, first_tiles), (first_tiles, tiles - first_tiles))
    by_x, by_y = [], []
    for (skip, count), waits in zip(column_parts, ([own], [rows_x, rows_y])):
        first, second = far_codes(after(rows_far, *waits), head, width, skip, count)
        by_x.append(send(first, to_x))
        by_y.append(send(second, to_y))
    codes = [
        near_codes(rows_x, rows_y, head, by_x[c], by_y[c], width, skip, count)
        for c, (skip, count) in enumerate(column_parts)
    ]
    halves = []
    for part in range(2):
        waits = codes[1][:1] if part else []
        sums_x = [send(after(c[part], *waits), to_x) for c in codes]
        sums_y = [send(after(c[2 + part], *waits), to_y) for c in codes]
        halves.append((sums_x, sums_y))

    in_list = jnp.arange(list_length)[None, :] < refusal_count[:, None]
    ids = jnp.where(in_list, refusal_ids - shard * vocab_local, -1)

    block, member = shard // group, shard % group
    spread = max(group // 2, 1)
    place_other = jnp.stack([(member // spread) ^ 1, member % spread]).astype(jnp.int32)
    place_mine = jnp.stack([member // spread, member % spread]).astype(jnp.int32)
    place_block = jnp.stack([block ^ k ^ me for k in range(prompt_size)]).astype(jnp.int32)
    to_member = [[(v, v ^ k) for v in range(vocab_size)] for k in range(1, group)]
    to_block = [
        [(v, ((v // group) ^ k) * group + v % group) for v in range(vocab_size)]
        for k in range(1, prompt_size)
    ]
    moves = []
    for p in range(prompt_size):
        for r in range(prompt_size):
            for i in range(group):
                moves.append((p * vocab_size + r * group + i, r * vocab_size + p * group + i))

    quarter = half // 2
    infos, grads = [], []
    for part, (sums_x, sums_y) in enumerate(halves):
        logits, listed, stats = row_stats(part, own, sums_x, sums_y, after(ids, *infos), width)
        stats = lax.all_gather(stats, "vocab", axis=0)
        grad, info = logit_grads(part, logits, listed, stats, loss_scale[:, None], width)
        infos.append(info)
        grads.append(grad)
    log_refusal = jnp.concatenate([info[:, 0] for info in infos])

    def neighbours(grad, *waits):
        sent = after(grad, *waits)
        return grad, send(sent, to_x), send(sent, to_y)

    def diagonal(grad_x, grad_y, *waits):
        passed_x, passed_y = after(grad_y, *waits)[:quarter], after(grad_x, *waits)[quarter:]
        return (passed_x, passed_y), [send(passed_x, to_x), send(passed_y, to_y)]

    def gradient(rows, waits_other=(), waits_mine=()):
        rows = jnp.concatenate(rows)
        others = back(rows, head, after(place_other, *waits_other), width, group, False)
        received = [lax.ppermute(c, "vocab", to) for c, to in zip(others, to_member[spread - 1 :])]
        keep, *codes = back(rows, head, after(place_mine, *others, *waits_mine), width, group, True)
        received += [lax.ppermute(c, "vocab", to) for c, to in zip(codes, to_member)]
        return keep, received

    def blocks(keep, received, *waits):
        keep, *codes = group_sum(after(place_block, *waits), keep, received)
        return keep, [lax.ppermute(c, "vocab", to) for c, to in zip(codes, to_block)]

    rows_a = neighbours(grads[0])
    _, far_a = diagonal(*rows_a[1:], infos[1])
    rows_b = neighbours(grads[1], *far_a)
    keep_a, received_a = gradient((*rows_a, *far_a))
    passed, far_b = diagonal(*rows_b[1:], keep_a)
    keep_a, received_a = blocks(keep_a, received_a, *passed)
    sum_a = last_sum(keep_a, received_a)
    keep_b, received_b = gradient((*rows_b, *far_b), received_a, [sum_a])
    sum_b = last_sum(*blocks(keep_b, received_b))
    grad_cols = [lax.ppermute(total, ("prompt", "vocab"), moves) for total in (sum_a, sum_b)]

    slice_width = model_width // vocab_size
    col_start = shard * slice_width
    codes = jnp.concatenate(grad_cols)
    power = codes[:, slice_width : slice_width + 1].astype(jnp.float32)
    grad_cols = codes[:, :slice_width].astype(jnp.float32) * jnp.exp(power * per_step)
    term = codes[:, slice_width + 1 : slice_width + 3].astype(jnp.float32)
    row_term = term[:, 0] * jnp.exp(term[:, 1] * per_step)
    hidden_cols = lax.dynamic_slice_in_dim(hidden, col_start, slice_width, 1).astype(jnp.float32)
    gain_cols = lax.dynamic_slice_in_dim(gain, col_start, slice_width, 0)
    grad_hidden = (
        inverse_rms * gain_cols * grad_cols
        - hidden_cols * (inverse_rms * inverse_rms / model_width) * row_term[:, None]
    )
    return (grad_hidden, log_refusal)


def solution(mesh):
    return jax.shard_map(
        shards,
        mesh=mesh,
        in_specs=(
            P("prompt", None),
            P("prompt", "vocab"),
            P(),
            P("prompt", None),
            P("prompt"),
            P("prompt"),
        ),
        out_specs=(P("prompt", "vocab"), P("prompt")),
        check_vma=False,
    )
```
